32 devices in a mesh: sec: 2 (over x), gx: 8 (over z, y), gy: 2 (over core).
Axes of the slice: x: 2, y: 2, z: 4, core: 2. Of those that a mesh axis runs over, the one named last changes fastest.
Arguments:
- sections: float32 [2, 8, 128, 64, 128], P('sec', None, 'gx', 'gy'), may hold values from -4 to 8, as said below
- fiber_angles: float32 [8, 2], replicated, may hold values from -3.140625 to 3.140625
- fiber_class: int32 [128, 64, 8], P('gx', 'gy'), may hold values from 0 to 7
- row_map: int32 [8, 2, 512], P('gx', 'gy'), may hold values from 0 to 511, each once within a row
- interface_rows: int32 [2, 8, 2, 32], P(None, 'gx', 'gy'), may hold values from 0 to 31, each once within a row
Outputs:
- updated: float32 [2, 4, 128, 64, 128], P('sec', None, 'gx', 'gy')
The draws below stay inside these ranges and needn't reach their ends.
Inputs may be any that keep to these rules, and one draw needn't show every extreme that they name: sections[0] holds calcium of 0.05 to 1, gates of 0 to 1, a bound buffer of 0 to 0.8 and tension of 0 to 1; sections[1] holds a stiffness of 0.5 to 2 and an activation coefficient of 2 to 8. `fiber_class`: the class of each column's block of 16 cells through the thickness. `row_map`: each block's list is a permutation of its 512 column places. `interface_rows`: for each side and block, a permutation of the 32 rows.
All inputs are finite; a program needn't handle non-finite values.
Results may differ from the reference program's by a relative error of at most 0.00002.
Values sent between devices are 32-bit elements; how exact they have to be, the bound alone decides.
No kernel may reach another device: no remote copies, remote signals or barrier semaphores. Data moves between devices by JAX's collectives and lax.ppermute only.
A program may use at most 64 MiB of HBM per device.

```python
import math
import jax
import jax.numpy as jnp

CX = 16
CY = 32
NZ = 128
CLASSES = 8
STEPS = 2
SWEEPS = 2
NX = 128
NY = 64
NZB = 8
COLS = 512
N_GX = 8
N_GY = 2


def draw_sections(key, part):
    grid_shape = (NX, NY, NZ)
    subkeys = jax.random.split(key, 16)
    voltage = jnp.clip(0.8 * jax.random.normal(subkeys[0], grid_shape, jnp.float32), -3.0, 3.0)
    motion = [jnp.clip(0.5 * jax.random.normal(subkeys[8 + channel], grid_shape, jnp.float32), -2.5, 2.5) for channel in range(3)]
    load_list = [jnp.clip(jax.random.normal(subkeys[11 + channel], grid_shape, jnp.float32), -4.0, 4.0) for channel in range(3)]
    calcium = jax.random.uniform(subkeys[1], grid_shape, jnp.float32, 0.05, 1.0)
    gate_list = [jax.random.uniform(subkeys[2 + channel], grid_shape, jnp.float32, 0.0, 1.0) for channel in range(4)]
    buffered = jax.random.uniform(subkeys[6], grid_shape, jnp.float32, 0.0, 0.8)
    tension = jax.random.uniform(subkeys[7], grid_shape, jnp.float32, 0.0, 1.0)
    stiffness = jnp.exp(jax.random.uniform(subkeys[14], grid_shape, jnp.float32, math.log(0.5), math.log(2.0)))
    coupling = jnp.exp(jax.random.uniform(subkeys[15], grid_shape, jnp.float32, math.log(2.0), math.log(8.0)))
    electric = jnp.stack([voltage, calcium] + gate_list + [buffered, tension])
    mechanic = jnp.stack(motion + load_list + [stiffness, coupling])
    return jnp.stack([electric, mechanic]).astype(jnp.float32)


def with_ends(values, own_key, smallest, largest):
    spot = [jax.random.randint(jax.random.fold_in(own_key, axis), (), 0, length) for axis, length in enumerate(values.shape)]
    longest = values.shape.index(max(values.shape))
    next_to = spot[:longest] + [(spot[longest] + 1) % values.shape[longest]] + spot[longest + 1:]
    return values.at[tuple(spot)].set(smallest).at[tuple(next_to)].set(largest)


def setup_inputs(seed: int = 0) -> dict:
    key_of = jax.random.split(jax.random.key(seed), 6)
    sections = draw_sections(jax.random.fold_in(key_of[5], 71), 0)
    fiber_angles = jnp.clip(jax.random.uniform(key_of[1], (CLASSES, 2), jnp.float32, -3.140625, 3.140625), -3.140625, 3.140625)
    fiber_class = with_ends(jax.random.randint(key_of[2], (NX, NY, NZB), 0, CLASSES), jax.random.fold_in(key_of[2], 1), 0, CLASSES - 1).astype(jnp.int32)
    row_map = jax.vmap(lambda own: jax.random.permutation(own, COLS))(jax.random.split(key_of[3], N_GX * N_GY)).reshape((N_GX, N_GY, COLS)).astype(jnp.int32)
    interface_rows = jax.vmap(lambda own: jax.random.permutation(own, CY))(jax.random.split(key_of[4], 2 * N_GX * N_GY)).reshape((2, N_GX, N_GY, CY)).astype(jnp.int32)
    return {"sections": sections, "fiber_angles": fiber_angles, "fiber_class": fiber_class, "row_map": row_map, "interface_rows": interface_rows}


sigma_long = 1.0
sigma_cross = 0.25
time_step = 0.1
shear_modulus = 1.0
lame_first = 1.0
relax_weight = 0.6
tie_stiffness = 2.0
diagonal_coef = 10.0


def fiber_table(fiber_angles):
    azimuth = fiber_angles[:, 0]
    elevation = fiber_angles[:, 1]
    fiber_dir = [jnp.cos(azimuth) * jnp.cos(elevation), jnp.sin(azimuth) * jnp.cos(elevation), jnp.sin(elevation)]
    spread_gap = sigma_long - sigma_cross
    return jnp.stack(fiber_dir + [
        sigma_cross + spread_gap * fiber_dir[0] * fiber_dir[0],
        sigma_cross + spread_gap * fiber_dir[1] * fiber_dir[1],
        sigma_cross + spread_gap * fiber_dir[2] * fiber_dir[2],
        spread_gap * fiber_dir[0] * fiber_dir[1],
        spread_gap * fiber_dir[0] * fiber_dir[2],
        spread_gap * fiber_dir[1] * fiber_dir[2]])


def shifted(values, offset):
    rolled = jnp.roll(values, -offset[0], axis=-3)
    rolled = jnp.roll(rolled, -offset[1], axis=-2)
    widths = [(0, 0)] * (values.ndim - 1) + [(1, 1)]
    padded = jnp.pad(rolled, widths)
    size_z = values.shape[-1]
    return padded[..., 1 + offset[2]:1 + offset[2] + size_z]


def unit_vec(axis_a, factor):
    return tuple(factor if place_a == axis_a else 0 for place_a in range(3))


def add_offsets(first_off, second_off):
    return tuple(first_off[place_a] + second_off[place_a] for place_a in range(3))


def second_diff(pick_cells, values, axis_a, centre):
    return pick_cells(values, unit_vec(axis_a, 1)) - 2.0 * centre + pick_cells(values, unit_vec(axis_a, -1))


def cross_diff(pick_cells, values, axis_a, axis_b):
    plus_a, minus_a = unit_vec(axis_a, 1), unit_vec(axis_a, -1)
    plus_b, minus_b = unit_vec(axis_b, 1), unit_vec(axis_b, -1)
    return 0.25 * (pick_cells(values, add_offsets(plus_a, plus_b)) - pick_cells(values, add_offsets(plus_a, minus_b))
                   - pick_cells(values, add_offsets(minus_a, plus_b)) + pick_cells(values, add_offsets(minus_a, minus_b)))


def diffuse(pick_cells, values, cell_fiber):
    centre = pick_cells(values, (0, 0, 0))
    result = jnp.zeros_like(centre)
    for axis_a in range(3):
        result = result + cell_fiber[3 + axis_a] * second_diff(pick_cells, values, axis_a, centre)
    for pair_axes, slot_index in (((0, 1), 6), ((0, 2), 7), ((1, 2), 8)):
        result = result + 2.0 * cell_fiber[slot_index] * cross_diff(pick_cells, values, pair_axes[0], pair_axes[1])
    return result


def ionic_step(cell_state, diffusion):
    voltage, calcium, activation, inactivation, potassium, slow_gate, buffered, tension = cell_state
    bound_share = calcium * calcium / (calcium * calcium + 0.25)
    calcium_flow = 1.2 * activation * inactivation * (voltage - 2.0)
    current_sum = calcium_flow + 0.8 * potassium * (voltage + 1.0) + 0.6 * bound_share * slow_gate * (voltage + 1.0) + 0.1 * voltage
    binding = 2.0 * calcium * (1.0 - buffered) - 0.4 * buffered
    return [voltage + time_step * (diffusion - current_sum),
            calcium + time_step * (-0.3 * calcium_flow - 0.5 * calcium - binding),
            activation + time_step * (jax.nn.sigmoid(2.0 * voltage + 1.0) - activation) / 0.5,
            inactivation + time_step * (jax.nn.sigmoid(-2.0 * voltage) - inactivation) / 3.0,
            potassium + time_step * (jax.nn.sigmoid(2.0 * voltage) - potassium),
            slow_gate + time_step * (jax.nn.sigmoid(voltage - 0.5) - slow_gate) / 5.0,
            buffered + time_step * binding,
            tension + time_step * (bound_share - tension) / 2.0]


def navier(pick_cells, motion, stiffness):
    centre = pick_cells(motion, (0, 0, 0))
    laplace = jnp.zeros_like(centre)
    for axis_a in range(3):
        laplace = laplace + second_diff(pick_cells, motion, axis_a, centre)
    pieces = []
    for component in range(3):
        component_term = second_diff(pick_cells, motion[component], component, centre[component])
        for other_axis in range(3):
            if other_axis != component:
                component_term = component_term + cross_diff(pick_cells, motion[other_axis], component, other_axis)
        pieces.append(component_term)
    graddiv = jnp.stack(pieces)
    return centre, -stiffness * (shear_modulus * laplace + (lame_first + shear_modulus) * graddiv)


def reference(sections, fiber_angles, fiber_class, row_map, interface_rows):
    fiber_rows = fiber_table(fiber_angles)
    block_depth = NZ // fiber_class.shape[-1]
    cell_fiber = jnp.repeat(jnp.moveaxis(fiber_rows.T[fiber_class], -1, 0), block_depth, axis=-1)
    cell_state = [sections[0, channel] for channel in range(8)]
    for repeat in range(STEPS):
        diffusion = diffuse(shifted, cell_state[0], cell_fiber)
        cell_state = ionic_step(cell_state, diffusion)
    tension_out = cell_state[7]
    blocks = tension_out.reshape(N_GX, CX, N_GY, CY, NZ).transpose(0, 2, 1, 3, 4).reshape(N_GX, N_GY, CX * CY, NZ)
    index_map = jnp.broadcast_to(row_map.astype(jnp.int32)[..., None], blocks.shape)
    remapped = jnp.take_along_axis(blocks, index_map, axis=2)
    remapped = remapped.reshape(N_GX, N_GY, CX, CY, NZ).transpose(0, 2, 1, 3, 4).reshape(NX, NY, NZ)
    activity = sections[1, 7] * remapped
    motion = sections[1, 0:3]
    stiffness = sections[1, 6]
    drive = sections[1, 3:6] + activity * cell_fiber[0:3]
    for repeat in range(SWEEPS):
        partial_value = (tie_stiffness * stiffness) * motion
        grid6 = partial_value.reshape(3, N_GX, CX, N_GY, CY, NZ)
        first_plane = grid6[:, :, 0]
        last_plane = grid6[:, :, -1]
        from_left = jnp.roll(last_plane, 1, axis=1)
        from_right = jnp.roll(first_plane, -1, axis=1)
        rows_first = jnp.broadcast_to(interface_rows[0].astype(jnp.int32)[None, :, :, :, None], first_plane.shape)
        rows_last = jnp.broadcast_to(interface_rows[1].astype(jnp.int32)[None, :, :, :, None], first_plane.shape)
        left_term = jnp.take_along_axis(from_left, rows_first, axis=3) - first_plane
        right_term = jnp.take_along_axis(from_right, rows_last, axis=3) - last_plane
        tie_force = jnp.zeros_like(grid6).at[:, :, 0].add(left_term).at[:, :, -1].add(right_term)
        tie_force = tie_force.reshape(3, NX, NY, NZ)
        centre, applied = navier(shifted, motion, stiffness)
        motion = centre + relax_weight * (drive + tie_force - applied) / (diagonal_coef * stiffness)
    electric_out = jnp.stack([cell_state[0], cell_state[1], cell_state[4], cell_state[7]])
    mechanic_out = jnp.concatenate([motion, activity[None]], axis=0)
    return jnp.stack([electric_out, mechanic_out])
```

```python
import jax
import jax.numpy as jnp
from jax import lax
from jax.experimental import pallas as pl
from jax.experimental.pallas import tpu as pltpu
from jax.sharding import PartitionSpec as P

DT = 0.1
OMEGA = 0.06
F32 = jnp.float32
HIGHEST = lax.Precision.HIGHEST
VMEM_LIMIT = 24 * 1024 * 1024

ROW_NOW, ROW_NEXT, ROW_STIFF, ROW_COEF, ROW_SIDE, ROW_CLASS, ROW_LIST = 0, 96, 192, 224, 256, 280, 288
MESSAGE_ROWS = 296


def swap_pairs(pairs):
    return pairs + [(b, a) for a, b in pairs]


def sigmoid(v):
    return 1.0 / (1.0 + jnp.exp(-v))


def shift_y(w):
    rows = w.shape[0]
    return pltpu.roll(w, rows - 1, 0), pltpu.roll(w, 1, 0)


def shift_z(w):
    depth = w.shape[1]
    lane = lax.broadcasted_iota(jnp.int32, w.shape, 1)
    up = jnp.where(lane == depth - 1, 0.0, pltpu.roll(w, depth - 1, 1))
    down = jnp.where(lane == 0, 0.0, pltpu.roll(w, 1, 1))
    return up, down


def motion_parts(u, rows):
    sum_y, dif_y, sum_z, dif_z = [], [], [], []
    for w in u:
        yp, ym = shift_y(w)
        zp, zm = shift_z(w)
        sum_y.append(yp + ym)
        dif_y.append(yp - ym)
        sum_z.append(zp + zm)
        dif_z.append(zp - zm)
    cross = []
    for b in (1, 2):
        yp, ym = shift_y(dif_z[b])
        cross.append(0.5 * (yp - ym))
    inner = (
        sum_y[0] + sum_z[0],
        3.0 * sum_y[1] + sum_z[1] + cross[1],
        sum_y[2] + 3.0 * sum_z[2] + cross[0],
    )
    odd = (0.5 * (dif_y[1] + dif_z[2]), 0.5 * dif_y[0], 0.5 * dif_z[0])
    even = (3.0 * u[0], u[1], u[2])
    cut = lambda ws: [w[:rows] for w in ws]
    return cut(inner), cut(even), cut(odd)


def voltage_parts(v, rows):
    yp, ym = shift_y(v)
    zp, zm = shift_z(v)
    dif_z = zp - zm
    zyp, zym = shift_y(dif_z)
    return [w[:rows] for w in (yp + ym, zp + zm, yp - ym, dif_z, zyp - zym)]


def spread(classes, block_depth):
    blocks, _ = classes.shape
    cell = lax.broadcasted_iota(jnp.int32, (blocks, blocks * block_depth), 1) // block_depth
    block = lax.broadcasted_iota(jnp.int32, (blocks, blocks * block_depth), 0)
    pick = (cell == block).astype(F32)
    return lax.dot_general(
        classes.astype(F32), pick, (((0,), (0,)), ((), ())), preferred_element_type=F32
    )


def fiber_of(tab_ref, cls):
    out = [jnp.full(cls.shape, tab_ref[a, 0], F32) for a in range(3)]
    for k in range(1, tab_ref.shape[1]):
        hit = cls == float(k)
        out = [jnp.where(hit, tab_ref[a, k], out[a]) for a in range(3)]
    return out


def conduct(fib):
    d = {}
    for a in range(3):
        d[a, a] = 0.25 + 0.75 * fib[a] * fib[a]
    for a, b in ((0, 1), (0, 2), (1, 2)):
        d[a, b] = 0.75 * fib[a] * fib[b]
    return d


def plane_sum(d, v, parts):
    sum_y, sum_z, _, _, cross = parts
    return (
        d[1, 1] * sum_y + d[2, 2] * sum_z + 0.5 * d[1, 2] * cross - 2.0 * (d[0, 0] + d[1, 1] + d[2, 2]) * v
    )


def from_plane(d, v, dif_y, dif_z, sign):
    return d[0, 0] * v + (0.5 * sign) * (d[0, 1] * dif_y + d[0, 2] * dif_z)


def currents(v, c, d, f, n, r):
    q = c * c / (c * c + 0.25)
    calcium_flow = 1.2 * d * f * (v - 2.0)
    total = calcium_flow + 0.8 * n * (v + 1.0) + 0.6 * q * r * (v + 1.0) + 0.1 * v
    return q, calcium_flow, total


def permute_rows(listed, values):
    rows = values.shape[0]
    pick = (lax.broadcasted_iota(jnp.int32, (rows, rows), 0).astype(F32) == listed).astype(F32)
    return lax.dot_general(
        pick, values, (((0,), (0,)), ((), ())), precision=HIGHEST, preferred_element_type=F32
    )


def tie_rows(listed, stiff, u):
    joined = jnp.concatenate([2.0 * stiff * w for w in u], axis=1)
    moved = permute_rows(listed, joined)
    depth = u[0].shape[1]
    return [moved[:, a * depth : (a + 1) * depth] for a in range(3)]


def whole(main, side):
    return jnp.concatenate([main, side], axis=0)


def tension_kernel(pos_ref, map_ref, sec_ref, all_ref, a_ref, b_ref, plain):
    size_x, size_y = sec_ref.shape[1], sec_ref.shape[2]

    @pl.when(pos_ref[0] == 0)
    def _():
        def plane(x, carry):
            v, c, d, f, bound, s = [sec_ref[k, x] for k in (0, 1, 2, 3, 6, 7)]
            calcium_flow = 1.2 * d * f * (v - 2.0)
            q = c * c / (c * c + 0.25)
            flow = 2.0 * c * (1.0 - bound) - 0.4 * bound
            c1 = c + DT * (-0.3 * calcium_flow - 0.5 * c - flow)
            s1 = s + DT * (q - s) / 2.0
            q1 = c1 * c1 / (c1 * c1 + 0.25)
            plain[pl.ds(pl.multiple_of(x * size_y, size_y), size_y), :] = s1 + DT * (q1 - s1) / 2.0
            return carry

        lax.fori_loop(0, size_x, plane, 0)

        def rows(i, carry):
            for k in range(16):
                p = i * 16 + k
                all_ref[pl.ds(p, 1), :] = plain[pl.ds(map_ref[p], 1), :]
            return carry

        lax.fori_loop(0, size_x * size_y // 16, rows, 0)
        last = (size_x - 1) * size_y
        even = pos_ref[1] == 0
        a_ref[...] = all_ref[pl.ds(pl.multiple_of(jnp.where(even, last, 0), size_y), size_y), :]
        b_ref[...] = all_ref[pl.ds(pl.multiple_of(jnp.where(even, 0, last), size_y), size_y), :]


def message_kernel(pos_ref, tab_ref, sec_ref, side_ref, cls_ref, list_ref, a_ref, b_ref):
    size_x, size_y = sec_ref.shape[1], sec_ref.shape[2]
    block_depth = sec_ref.shape[3] // cls_ref.shape[1]
    for slot, out in enumerate((a_ref, b_ref)):
        right = (pos_ref[1] + slot) % 2 == 0
        edge = jnp.where(right, size_x - 1, 0)
        inner = jnp.where(right, size_x - 2, 1)
        sign = jnp.where(right, 1.0, -1.0).astype(F32)
        out[ROW_CLASS : ROW_CLASS + cls_ref.shape[1], 0:size_y] = cls_ref[edge].astype(F32)
        out[ROW_LIST : ROW_LIST + 8, 0:size_y] = jnp.broadcast_to(
            list_ref[jnp.where(right, 1, 0)].astype(F32), (8, size_y)
        )
        for a in range(3):
            out[ROW_NOW + a * size_y : ROW_NOW + (a + 1) * size_y, :] = sec_ref[a, edge]
            out[ROW_SIDE + a * 8 : ROW_SIDE + (a + 1) * 8, :] = side_ref[a, edge]

        @pl.when(pos_ref[0] == 0)
        def _():
            v, c, d, f, n, r = [sec_ref[k, edge] for k in range(6)]
            con = conduct(fiber_of(tab_ref, spread(cls_ref[edge], block_depth)))
            own = voltage_parts(whole(v, side_ref[0, edge]), size_y)
            near_v = sec_ref[0, inner]
            near = voltage_parts(whole(near_v, side_ref[0, inner]), size_y)
            _, _, total = currents(v, c, d, f, n, r)
            lap = plane_sum(con, v, own) + from_plane(con, near_v, near[2], near[3], -sign)
            out[ROW_NEXT : ROW_NEXT + size_y, :] = v + DT * (lap - total)

        @pl.when(pos_ref[0] != 0)
        def _():
            u = [sec_ref[a, edge] for a in range(3)]
            within, _, _ = motion_parts([whole(u[a], side_ref[a, edge]) for a in range(3)], size_y)
            _, even, odd = motion_parts(
                [whole(sec_ref[a, inner], side_ref[a, inner]) for a in range(3)], size_y
            )
            stiff = sec_ref[6, edge]
            beta = OMEGA / stiff
            out[ROW_STIFF : ROW_STIFF + size_y, :] = stiff
            out[ROW_COEF : ROW_COEF + size_y, :] = beta * sec_ref[7, edge]
            for a in range(3):
                out[ROW_NEXT + a * size_y : ROW_NEXT + (a + 1) * size_y, :] = (
                    0.28 * u[a]
                    + beta * sec_ref[3 + a, edge]
                    + OMEGA * (within[a] + even[a] - sign * odd[a])
                )


def first_kernel(
    pos_ref, tab_ref, sec_ref, side_ref, cls_ref, list_ref, got_a, got_b, ten_ref, ten_a, ten_b,
    next_ref, share_ref, rest_ref, wide, odds, evens
):
    size_x, size_y = sec_ref.shape[1], sec_ref.shape[2]
    block_depth = sec_ref.shape[3] // cls_ref.shape[1]
    slots = []
    for slot, got in enumerate((got_a, got_b)):
        right = (pos_ref[1] + slot) % 2 == 0
        slots.append(
            (
                got,
                (ten_a, ten_b)[slot],
                jnp.where(right, size_x + 1, 0),
                jnp.where(right, size_x - 1, 0),
                jnp.where(right, 1, 0),
                jnp.where(right, 1.0, -1.0).astype(F32),
            )
        )
    pick_last = lax.broadcasted_iota(jnp.int32, (8, sec_ref.shape[3]), 0) == 7

    def put(a, x, value):
        next_ref[a, x] = value
        share_ref[a, x] = jnp.where(pick_last, value[size_y - 8 :], value[:8])

    def got_plane(got, a):
        return whole(
            got[ROW_NOW + a * size_y : ROW_NOW + (a + 1) * size_y, :],
            got[ROW_SIDE + a * 8 : ROW_SIDE + (a + 1) * 8, :],
        )

    @pl.when(pos_ref[0] == 0)
    def _():
        for got, _, at, _, _, _ in slots:
            w = got_plane(got, 0)
            parts = voltage_parts(w, size_y)
            wide[0, at] = w[:size_y]
            odds[0, at] = parts[2]
            odds[1, at] = parts[3]

        def prepare(x, carry):
            v = sec_ref[0, x]
            parts = voltage_parts(whole(v, side_ref[0, x]), size_y)
            con = conduct(fiber_of(tab_ref, spread(cls_ref[x], block_depth)))
            wide[0, x + 1] = v
            odds[0, x + 1] = parts[2]
            odds[1, x + 1] = parts[3]
            evens[0, x + 1] = plane_sum(con, v, parts)
            return carry

        lax.fori_loop(0, size_x, prepare, 0)

        def step(x, carry):
            v, c, d, f, n, r, bound, s = [sec_ref[k, x] for k in range(8)]
            con = conduct(fiber_of(tab_ref, spread(cls_ref[x], block_depth)))
            lap = (
                evens[0, x + 1]
                + con[0, 0] * (wide[0, x + 2] + wide[0, x])
                + 0.5 * con[0, 1] * (odds[0, x + 2] - odds[0, x])
                + 0.5 * con[0, 2] * (odds[1, x + 2] - odds[1, x])
            )
            q, calcium_flow, total = currents(v, c, d, f, n, r)
            flow = 2.0 * c * (1.0 - bound) - 0.4 * bound
            put(0, x + 1, v + DT * (lap - total))
            rest_ref[0, x] = c + DT * (-0.3 * calcium_flow - 0.5 * c - flow)
            rest_ref[1, x] = d + DT * (sigmoid(2.0 * v + 1.0) - d) / 0.5
            rest_ref[2, x] = f + DT * (sigmoid(-2.0 * v) - f) / 3.0
            rest_ref[3, x] = n + DT * (sigmoid(2.0 * v) - n)
            rest_ref[4, x] = r + DT * (sigmoid(v - 0.5) - r) / 5.0
            rest_ref[5, x] = bound + DT * flow
            rest_ref[6, x] = s + DT * (q - s) / 2.0
            return carry

        lax.fori_loop(0, size_x, step, 0)
        for got, _, at, edge, _, sign in slots:
            con = conduct(
                fiber_of(tab_ref, spread(got[ROW_CLASS : ROW_CLASS + cls_ref.shape[1], 0:size_y], block_depth))
            )
            put(
                0,
                at,
                got[ROW_NEXT : ROW_NEXT + size_y, :]
                + DT * from_plane(con, wide[0, edge + 1], odds[0, edge + 1], odds[1, edge + 1], -sign),
            )

    @pl.when(pos_ref[0] != 0)
    def _():
        for got, _, at, _, _, _ in slots:
            _, even, odd = motion_parts([got_plane(got, a) for a in range(3)], size_y)
            for a in range(3):
                odds[a, at] = odd[a]
                evens[a, at] = even[a]

        def prepare(x, carry):
            u = [sec_ref[a, x] for a in range(3)]
            within, even, odd = motion_parts([whole(u[a], side_ref[a, x]) for a in range(3)], size_y)
            stiff = sec_ref[6, x]
            beta = OMEGA / stiff
            fib = fiber_of(tab_ref, spread(cls_ref[x], block_depth))
            act = sec_ref[7, x] * ten_ref[pl.ds(pl.multiple_of(x * size_y, size_y), size_y), :]
            rest_ref[6, x] = act
            for a in range(3):
                drive = beta * (sec_ref[3 + a, x] + act * fib[a])
                rest_ref[a, x] = drive
                wide[a, x + 1] = 0.4 * u[a] + drive + OMEGA * within[a]
                odds[a, x + 1] = odd[a]
                evens[a, x + 1] = even[a]
            return carry

        lax.fori_loop(0, size_x, prepare, 0)
        for got, _, _, edge, which, _ in slots:
            beta = OMEGA / sec_ref[6, edge]
            stiff = got[ROW_STIFF : ROW_STIFF + size_y, :]
            ties = tie_rows(
                list_ref[which].astype(F32),
                stiff,
                [got[ROW_NOW + a * size_y : ROW_NOW + (a + 1) * size_y, :] for a in range(3)],
            )
            for a in range(3):
                wide[a, edge + 1] = wide[a, edge + 1] + beta * ties[a] - 0.12 * sec_ref[a, edge]

        def sweep(x, carry):
            for a in range(3):
                put(
                    a,
                    x + 1,
                    wide[a, x + 1]
                    + OMEGA * (evens[a, x + 2] + evens[a, x] + odds[a, x + 2] - odds[a, x]),
                )
            return carry

        lax.fori_loop(0, size_x, sweep, 0)
        for got, ten, at, edge, _, sign in slots:
            fib = fiber_of(
                tab_ref, spread(got[ROW_CLASS : ROW_CLASS + cls_ref.shape[1], 0:size_y], block_depth)
            )
            beta = OMEGA / got[ROW_STIFF : ROW_STIFF + size_y, :]
            drive = got[ROW_COEF : ROW_COEF + size_y, :] * ten[...]
            ties = tie_rows(
                got[ROW_LIST : ROW_LIST + 1, 0:size_y], sec_ref[6, edge], [sec_ref[a, edge] for a in range(3)]
            )
            for a in range(3):
                put(
                    a,
                    at,
                    got[ROW_NEXT + a * size_y : ROW_NEXT + (a + 1) * size_y, :]
                    + OMEGA * (evens[a, edge + 1] - sign * odds[a, edge + 1])
                    + beta * ties[a]
                    + drive * fib[a],
                )


def second_kernel(
    pos_ref, tab_ref, sec_ref, cls_ref, list_ref, got_a, got_b, next_ref, share_ref, rest_ref,
    out_ref, wide, odds, evens
):
    size_x, size_y = sec_ref.shape[1], sec_ref.shape[2]
    block_depth = sec_ref.shape[3] // cls_ref.shape[1]

    @pl.when(pos_ref[0] == 0)
    def _():
        def prepare(x, carry):
            parts = voltage_parts(whole(next_ref[0, x], share_ref[0, x]), size_y)
            for k in range(5):
                (wide, wide, odds, odds, wide)[k][(0, 1, 0, 1, 2)[k], x] = parts[k]
            return carry

        lax.fori_loop(0, size_x + 2, prepare, 0)

        def step(x, carry):
            v = next_ref[0, x + 1]
            c, d, f, n, r, bound, s = [rest_ref[k, x] for k in range(7)]
            con = conduct(fiber_of(tab_ref, spread(cls_ref[x], block_depth)))
            lap = (
                plane_sum(con, v, (wide[0, x + 1], wide[1, x + 1], None, None, wide[2, x + 1]))
                + con[0, 0] * (next_ref[0, x + 2] + next_ref[0, x])
                + 0.5 * con[0, 1] * (odds[0, x + 2] - odds[0, x])
                + 0.5 * con[0, 2] * (odds[1, x + 2] - odds[1, x])
            )
            q, calcium_flow, total = currents(v, c, d, f, n, r)
            flow = 2.0 * c * (1.0 - bound) - 0.4 * bound
            out_ref[0, 0, x] = v + DT * (lap - total)
            out_ref[0, 1, x] = c + DT * (-0.3 * calcium_flow - 0.5 * c - flow)
            out_ref[0, 2, x] = n + DT * (sigmoid(2.0 * v) - n)
            out_ref[0, 3, x] = s + DT * (q - s) / 2.0
            return carry

        lax.fori_loop(0, size_x, step, 0)

    @pl.when(pos_ref[0] != 0)
    def _():
        def prepare(x, carry):
            u = [next_ref[a, x] for a in range(3)]
            within, even, odd = motion_parts([whole(u[a], share_ref[a, x]) for a in range(3)], size_y)
            own = jnp.clip(x - 1, 0, size_x - 1)
            for a in range(3):
                wide[a, x] = 0.4 * u[a] + rest_ref[a, own] + OMEGA * within[a]
                odds[a, x] = odd[a]
                evens[a, x] = even[a]
            return carry

        lax.fori_loop(0, size_x + 2, prepare, 0)
        for slot, got in enumerate((got_a, got_b)):
            right = (pos_ref[1] + slot) % 2 == 0
            at = jnp.where(right, size_x + 1, 0)
            edge = jnp.where(right, size_x - 1, 0)
            beta = OMEGA / sec_ref[6, edge]
            ties = tie_rows(
                list_ref[jnp.where(right, 1, 0)].astype(F32),
                got[ROW_STIFF : ROW_STIFF + size_y, :],
                [next_ref[a, at] for a in range(3)],
            )
            for a in range(3):
                wide[a, edge + 1] = wide[a, edge + 1] + beta * ties[a] - 0.12 * next_ref[a, edge + 1]

        def sweep(x, carry):
            for a in range(3):
                out_ref[0, a, x] = wide[a, x + 1] + OMEGA * (
                    evens[a, x + 2] + evens[a, x] + odds[a, x + 2] - odds[a, x]
                )
            out_ref[0, 3, x] = rest_ref[6, x]
            return carry

        lax.fori_loop(0, size_x, sweep, 0)


def fiber_table(fiber_angles):
    azimuth = fiber_angles[:, 0]
    elevation = fiber_angles[:, 1]
    return jnp.stack(
        [
            jnp.cos(azimuth) * jnp.cos(elevation),
            jnp.sin(azimuth) * jnp.cos(elevation),
            jnp.sin(elevation),
        ]
    )


def call(kernel, name, out_shape, operands, spaces, scratch=()):
    return pl.pallas_call(
        kernel,
        name=name,
        out_shape=out_shape,
        in_specs=[pl.BlockSpec(memory_space=space) for space in spaces],
        out_specs=jax.tree.map(lambda _: pl.BlockSpec(memory_space=pltpu.VMEM), out_shape),
        scratch_shapes=scratch,
        compiler_params=pltpu.CompilerParams(vmem_limit_bytes=VMEM_LIMIT),
    )(*operands)


def local(sections, fiber_angles, fiber_class, row_map, interface_rows):
    own = sections[0]
    _, size_x, size_y, depth = own.shape
    n_gx = lax.axis_size("gx")
    n_gy = lax.axis_size("gy")
    assert n_gx % 2 == 0 and n_gy == 2
    swap_a = swap_pairs([(i, i + 1) for i in range(0, n_gx, 2)])
    swap_b = swap_pairs([(i, (i + 1) % n_gx) for i in range(1, n_gx, 2)])
    cross_a = [(s * n_gx + i, (1 - s) * n_gx + j) for s in range(2) for i, j in swap_a]
    cross_b = [(s * n_gx + i, (1 - s) * n_gx + j) for s in range(2) for i, j in swap_b]
    both = swap_pairs([(0, 1)])
    S, V = pltpu.SMEM, pltpu.VMEM
    f32 = lambda *shape: jax.ShapeDtypeStruct(shape, F32)

    pos = jnp.stack([lax.axis_index("sec"), lax.axis_index("gx") % 2]).astype(jnp.int32)
    table = fiber_table(fiber_angles)
    classes = fiber_class.transpose(0, 2, 1)
    lists = interface_rows.reshape(2, 1, size_y)

    pick_last = jnp.arange(8)[:, None] == 7
    share = jnp.where(pick_last, own[:3, :, size_y - 8 :], own[:3, :, :8])
    side = lax.ppermute(share, "gy", both)
    tension, ten_a, ten_b = call(
        tension_kernel,
        "tension",
        (f32(size_x * size_y, depth), f32(size_y, depth), f32(size_y, depth)),
        (pos, row_map.reshape(-1), own),
        (S, S, V),
        [pltpu.VMEM((size_x * size_y, depth), F32)],
    )
    message_a, message_b = call(
        message_kernel,
        "message",
        (f32(MESSAGE_ROWS, depth), f32(MESSAGE_ROWS, depth)),
        (pos, table, own, side, classes, lists),
        (S, S, V, V, V, V),
    )
    got_b = lax.ppermute(message_b, "gx", swap_b)
    got_a = lax.ppermute(message_a, "gx", swap_a)
    ten_b = lax.ppermute(ten_b, ("sec", "gx"), cross_b)
    ten_a = lax.ppermute(ten_a, ("sec", "gx"), cross_a)
    tension = lax.ppermute(tension, "sec", both)
    fields = lambda n: pltpu.VMEM((n, size_x + 2, size_y, depth), F32)
    moved, share, rest = call(
        first_kernel,
        "first",
        (f32(3, size_x + 2, size_y, depth), f32(3, size_x + 2, 8, depth), f32(7, size_x, size_y, depth)),
        (pos, table, own, side, classes, lists, got_a, got_b, tension, ten_a, ten_b),
        (S, S, V, V, V, V, V, V, V, V, V),
        [fields(3), fields(3), fields(3)],
    )
    side = lax.ppermute(share, "gy", both)
    return call(
        second_kernel,
        "second",
        f32(1, 4, size_x, size_y, depth),
        (pos, table, own, classes, lists, got_a, got_b, moved, side, rest),
        (S, S, V, V, V, V, V, V, V, V),
        [fields(3), fields(3), fields(3)],
    )


def solution(mesh):
    in_specs = (
        P("sec", None, "gx", "gy", None),
        P(),
        P("gx", "gy", None),
        P("gx", "gy", None),
        P(None, "gx", "gy", None),
    )
    out_specs = P("sec", None, "gx", "gy", None)
    return jax.shard_map(local, mesh=mesh, in_specs=in_specs, out_specs=out_specs, check_vma=False)
```

```python
import jax
import jax.numpy as jnp
from jax import lax
from jax.experimental import pallas as pl
from jax.experimental.pallas import tpu as pltpu
from jax.sharding import PartitionSpec as P

DT = 0.1
OMEGA = 0.06
F32 = jnp.float32
HIGHEST = lax.Precision.HIGHEST
VMEM_LIMIT = 32 * 1024 * 1024

PAD = 8

ROW_NOW, ROW_NEXT, ROW_STIFF, ROW_COEF, ROW_SIDE, ROW_CLASS, ROW_LIST = 0, 96, 192, 224, 256, 280, 288
MESSAGE_ROWS = 296


def swap_pairs(pairs):
    return pairs + [(b, a) for a, b in pairs]


def inverse(v):
    r = pl.reciprocal(v, approx=True)
    return r * (2.0 - v * r)


def rise(c):
    c2 = c * c
    return c2 * inverse(c2 + 0.25)


def ends(like):
    lane = lax.broadcasted_iota(jnp.int32, like, 1)
    return lane == like[1] - 1, lane == 0


def up_z(w, last):
    return jnp.where(last, 0.0, pltpu.roll(w, w.shape[1] - 1, 1))


def down_z(w, first):
    return jnp.where(first, 0.0, pltpu.roll(w, 1, 1))


def rows_of(pad, a, x, size_y, shift=0):
    return pad[a, x, PAD + shift : PAD + shift + size_y, :]


def motion_rate(pad, x, size_y):
    at = lambda a, dx=0, dy=0: rows_of(pad, a, x + dx, size_y, dy)
    u0, u1, u2 = at(0), at(1), at(2)
    last, first = ends(u0.shape)
    w0p, w0m, w1p, w1m = at(0, 1), at(0, -1), at(1, 1), at(1, -1)
    w2p, w2m = at(2, 1), at(2, -1)
    e0, e2 = 0.5 * (w0p - w0m), 0.5 * (w2p - w2m)
    e0y = (at(0, 1, 1) - at(0, -1, 1)) - (at(0, 1, -1) - at(0, -1, -1))
    e1y = (at(1, 1, 1) - at(1, -1, 1)) - (at(1, 1, -1) - at(1, -1, -1))
    v1p, v1m, v2p, v2m = at(1, 0, 1), at(1, 0, -1), at(2, 0, 1), at(2, 0, -1)
    d2 = 0.5 * (v2p - v2m)
    d1 = 0.5 * (v1p - v1m) + e0
    r0 = (
        up_z(u0 + e2, last) + down_z(u0 - e2, first)
        + (at(0, 0, 1) + at(0, 0, -1)) + 0.5 * e1y + 3.0 * (w0p + w0m)
    )
    r1 = (
        up_z(u1 + d2, last) + down_z(u1 - d2, first)
        + 3.0 * (v1p + v1m) + 0.5 * e0y + (w1p + w1m)
    )
    t2 = 3.0 * u2
    r2 = up_z(t2 + d1, last) + down_z(t2 - d1, first) + (v2p + v2m) + (w2p + w2m)
    return r0, r1, r2


def motion_from(pad, x, sign, size_y):
    u0, u1, u2 = [rows_of(pad, a, x, size_y) for a in range(3)]
    last, first = ends(u0.shape)
    half = 0.5 * sign
    dy0 = rows_of(pad, 0, x, size_y, 1) - rows_of(pad, 0, x, size_y, -1)
    dy1 = rows_of(pad, 1, x, size_y, 1) - rows_of(pad, 1, x, size_y, -1)
    dz0 = up_z(u0, last) - down_z(u0, first)
    dz2 = up_z(u2, last) - down_z(u2, first)
    return 3.0 * u0 + half * (dy1 + dz2), u1 + half * dy0, u2 + half * dz0


def volt_rate(pad, x, fib, size_y):
    at = lambda dx=0, dy=0: rows_of(pad, 0, x + dx, size_y, dy)
    v, wp, wm, yp, ym = at(), at(1), at(-1), at(0, 1), at(0, -1)
    last, first = ends(v.shape)
    e = wp - wm
    ey = (at(1, 1) - at(-1, 1)) - (at(1, -1) - at(-1, -1))
    dy = yp - ym
    sum_z = up_z(v, last) + down_z(v, first)
    ez = up_z(e, last) - down_z(e, first)
    dyz = up_z(dy, last) - down_z(dy, first)
    g = [0.75 * w for w in fib]
    d00, d11, d22 = [0.25 + a * b for a, b in zip(g, fib)]
    return (
        d00 * (wp + wm) + d11 * (yp + ym) + d22 * sum_z - 2.0 * (d00 + d11 + d22) * v
        + 0.5 * (fib[0] * (g[1] * ey + g[2] * ez) + g[1] * fib[2] * dyz)
    )


def volt_from(pad, x, fib, sign, size_y):
    v = rows_of(pad, 0, x, size_y)
    last, first = ends(v.shape)
    dy = rows_of(pad, 0, x, size_y, 1) - rows_of(pad, 0, x, size_y, -1)
    dz = up_z(v, last) - down_z(v, first)
    g = 0.75 * fib[0]
    return (0.25 + g * fib[0]) * v + (0.5 * sign) * g * (fib[1] * dy + fib[2] * dz)


def currents(v, c, d, f, n, r):
    q = rise(c)
    calcium_flow = 1.2 * d * f * (v - 2.0)
    return q, calcium_flow, calcium_flow + (0.8 * n + 0.6 * q * r) * (v + 1.0) + 0.1 * v


def spread(classes, block_depth):
    blocks, _ = classes.shape
    cell = lax.broadcasted_iota(jnp.int32, (blocks, blocks * block_depth), 1) // block_depth
    block = lax.broadcasted_iota(jnp.int32, (blocks, blocks * block_depth), 0)
    pick = (cell == block).astype(F32)
    return lax.dot_general(
        classes.astype(F32), pick, (((0,), (0,)), ((), ())), preferred_element_type=F32
    )


def fiber_of(tab_ref, cls):
    out = [jnp.full(cls.shape, tab_ref[a, 0], F32) for a in range(3)]
    for k in range(1, tab_ref.shape[1]):
        hit = cls == float(k)
        out = [jnp.where(hit, tab_ref[a, k], out[a]) for a in range(3)]
    return out


def permute_rows(listed, values):
    rows = values.shape[0]
    pick = (lax.broadcasted_iota(jnp.int32, (rows, rows), 0).astype(F32) == listed).astype(F32)
    return lax.dot_general(
        pick, values, (((0,), (0,)), ((), ())), precision=HIGHEST, preferred_element_type=F32
    )


def tie_rows(listed, stiff, u):
    joined = jnp.concatenate([2.0 * stiff * w for w in u], axis=1)
    moved = permute_rows(listed, joined)
    depth = u[0].shape[1]
    return [moved[:, a * depth : (a + 1) * depth] for a in range(3)]


def edges_tile(value):
    rows = value.shape[0]
    last = lax.broadcasted_iota(jnp.int32, (8, value.shape[1]), 0) == 7
    return jnp.where(last, value[rows - 8 :], value[:8])


def fill_sides(pad, a, x, tile, size_y):
    pad[a, x, 0:PAD, :] = tile
    pad[a, x, PAD + size_y :, :] = tile


def sides(pos_ref, size_x):
    out = []
    for slot in range(2):
        right = (pos_ref[1] + slot) % 2 == 0
        out.append(
            (
                jnp.where(right, size_x + 1, 0),
                jnp.where(right, size_x - 1, 0),
                jnp.where(right, 1, 0),
                jnp.where(right, 1.0, -1.0).astype(F32),
            )
        )
    return out


def load_kernel(sec_hbm, pad, rest, share, sems):
    size_x, size_y = sec_hbm.shape[1], sec_hbm.shape[2]
    inside = pl.ds(PAD, size_y)
    main = pltpu.make_async_copy(sec_hbm.at[0:3], pad.at[:, 1 : size_x + 1, inside, :], sems.at[0])
    other = pltpu.make_async_copy(sec_hbm.at[3:8], rest, sems.at[1])
    main.start()
    other.start()
    zeros = jnp.zeros(pad.shape[2:], F32)
    for a in range(3):
        pad[a, 0] = zeros
        pad[a, size_x + 1] = zeros
    main.wait()

    def plane(x, carry):
        for a in range(3):
            share[a, x] = edges_tile(rows_of(pad, a, x + 1, size_y))
        return carry

    lax.fori_loop(0, size_x, plane, 0, unroll=4)
    other.wait()


def local_kernel(pos_ref, map_ref, tab_ref, pad, rest, cls_ref, plain, all_ref, a_ref, b_ref, fib_ref, flat):
    size_x, size_y = rest.shape[1], rest.shape[2]
    blocks, classes = cls_ref.shape[1], tab_ref.shape[1]
    depth = rest.shape[3]

    @pl.when(pos_ref[0] == 0)
    def _():
        def plane(x, carry):
            v, c, d = [rows_of(pad, a, x + 1, size_y) for a in range(3)]
            f, bound, s = rest[0, x], rest[3, x], rest[4, x]
            calcium_flow = 1.2 * d * f * (v - 2.0)
            flow = 2.0 * c * (1.0 - bound) - 0.4 * bound
            c1 = c + DT * (-0.3 * calcium_flow - 0.5 * c - flow)
            s1 = s + (0.5 * DT) * (rise(c) - s)
            plain[pl.ds(pl.multiple_of(x * size_y, size_y), size_y), :] = s1 + (0.5 * DT) * (rise(c1) - s1)
            return carry

        lax.fori_loop(0, size_x, plane, 0, unroll=2)

        def rows(i, carry):
            for k in range(16):
                p = i * 16 + k
                all_ref[pl.ds(p, 1), :] = plain[pl.ds(map_ref[p], 1), :]
            return carry

        lax.fori_loop(0, size_x * size_y // 16, rows, 0)
        last = (size_x - 1) * size_y
        even = pos_ref[1] == 0
        a_ref[...] = all_ref[pl.ds(pl.multiple_of(jnp.where(even, last, 0), size_y), size_y), :]
        b_ref[...] = all_ref[pl.ds(pl.multiple_of(jnp.where(even, 0, last), size_y), size_y), :]

    for x in range(size_x):
        flat[:, x * size_y : (x + 1) * size_y] = cls_ref[x]
    cls = flat[...]
    hits = jnp.concatenate([(cls == k).astype(F32) for k in range(classes)], axis=0)
    own = lax.broadcasted_iota(jnp.int32, (blocks, depth), 1) // (depth // blocks)
    own = own == lax.broadcasted_iota(jnp.int32, (blocks, depth), 0)
    table = jnp.concatenate(
        [
            jnp.concatenate([jnp.where(own, tab_ref[a, k], 0.0) for a in range(3)], axis=1)
            for k in range(classes)
        ],
        axis=0,
    )
    fib = lax.dot_general(
        hits, table, (((0,), (0,)), ((), ())), precision=HIGHEST, preferred_element_type=F32
    )
    for a in range(3):
        fib_ref[a] = fib[:, a * depth : (a + 1) * depth]


def message_kernel(pos_ref, pad_in, rest, side_ref, fib_ref, cls_ref, list_ref, a_ref, b_ref, pad):
    size_x, size_y = rest.shape[1], rest.shape[2]

    def fill(x, carry):
        for a in range(3):
            fill_sides(pad, a, x + 1, side_ref[a, x], size_y)
        return carry

    lax.fori_loop(0, size_x, fill, 0, unroll=4)
    for (_, edge, which, _), out in zip(sides(pos_ref, size_x), (a_ref, b_ref)):
        out[ROW_CLASS : ROW_CLASS + cls_ref.shape[1], 0:size_y] = cls_ref[edge].astype(F32)
        out[ROW_LIST : ROW_LIST + 8, 0:size_y] = jnp.broadcast_to(list_ref[which].astype(F32), (8, size_y))
        for a in range(3):
            out[ROW_NOW + a * size_y : ROW_NOW + (a + 1) * size_y, :] = rows_of(pad, a, edge + 1, size_y)
            out[ROW_SIDE + a * 8 : ROW_SIDE + (a + 1) * 8, :] = side_ref[a, edge]

        @pl.when(pos_ref[0] == 0)
        def _():
            v, c, d = [rows_of(pad, a, edge + 1, size_y) for a in range(3)]
            f, n, r = [rest[k, edge] for k in range(3)]
            place = pl.ds(pl.multiple_of(edge * size_y, size_y), size_y)
            rate = volt_rate(pad, edge + 1, [fib_ref[a, place, :] for a in range(3)], size_y)
            _, _, total = currents(v, c, d, f, n, r)
            out[ROW_NEXT : ROW_NEXT + size_y, :] = v + DT * (rate - total)

        @pl.when(pos_ref[0] != 0)
        def _():
            rate = motion_rate(pad, edge + 1, size_y)
            stiff = rest[3, edge]
            beta = OMEGA * inverse(stiff)
            out[ROW_STIFF : ROW_STIFF + size_y, :] = stiff
            out[ROW_COEF : ROW_COEF + size_y, :] = beta * rest[4, edge]
            for a in range(3):
                out[ROW_NEXT + a * size_y : ROW_NEXT + (a + 1) * size_y, :] = (
                    0.28 * rows_of(pad, a, edge + 1, size_y) + beta * rest[a, edge] + OMEGA * rate[a]
                )


def inner_kernel(pos_ref, pad, rest, fib_ref, ten_ref, next_pad, share, keep):
    size_x, size_y = rest.shape[1], rest.shape[2]

    def put(a, x, value):
        next_pad[a, x, PAD : PAD + size_y, :] = value
        share[a, x] = edges_tile(value)

    @pl.when(pos_ref[0] == 0)
    def _():
        def plane(x, carry):
            place = pl.ds(pl.multiple_of(x * size_y, size_y), size_y)
            v, c, d = [rows_of(pad, a, x + 1, size_y) for a in range(3)]
            f, n, r, bound, _ = [rest[k, x] for k in range(5)]
            rate = volt_rate(pad, x + 1, [fib_ref[a, place, :] for a in range(3)], size_y)
            q, calcium_flow, total = currents(v, c, d, f, n, r)
            flow = 2.0 * c * (1.0 - bound) - 0.4 * bound
            put(0, x + 1, v + DT * (rate - total))
            c1 = c + DT * (-0.3 * calcium_flow - 0.5 * c - flow)
            tv = jnp.tanh(v)
            d1 = (1.0 - 2.0 * DT) * d + DT * (1.0 + jnp.tanh(v + 0.5))
            f1 = (1.0 - DT / 3.0) * f + (DT / 6.0) * (1.0 - tv)
            n1 = (1.0 - DT) * n + (0.5 * DT) * (1.0 + tv)
            r1 = (1.0 - DT / 5.0) * r + (DT / 10.0) * (1.0 + jnp.tanh(0.5 * v - 0.25))
            bound1 = bound + DT * flow
            flow1 = 2.0 * c1 * (1.0 - bound1) - 0.4 * bound1
            gate = 1.2 * d1 * f1
            leak = 0.8 * n1 + 0.6 * rise(c1) * r1
            keep[0, x] = n1
            keep[1, x] = gate
            keep[2, x] = leak
            keep[3, x] = c1 - DT * (0.5 * c1 + flow1)
            return carry

        lax.fori_loop(0, size_x, plane, 0, unroll=2)

    @pl.when(pos_ref[0] != 0)
    def _():
        def plane(x, carry):
            place = pl.ds(pl.multiple_of(x * size_y, size_y), size_y)
            rate = motion_rate(pad, x + 1, size_y)
            beta = OMEGA * inverse(rest[3, x])
            act = rest[4, x] * ten_ref[place, :]
            keep[3, x] = act
            for a in range(3):
                drive = beta * (rest[a, x] + act * fib_ref[a, place, :])
                keep[a, x] = drive
                put(a, x + 1, 0.4 * rows_of(pad, a, x + 1, size_y) + drive + OMEGA * rate[a])
            return carry

        lax.fori_loop(0, size_x, plane, 0, unroll=2)


def outer_kernel(
    pos_ref, tab_ref, pad_in, rest, fib_ref, cls_ref, list_ref, got_a, got_b, ten_a, ten_b, next_in, share_in,
    next_pad, share, wide
):
    size_x, size_y = rest.shape[1], rest.shape[2]
    block_depth = rest.shape[3] // cls_ref.shape[1]

    def put(a, x, value):
        next_pad[a, x, PAD : PAD + size_y, :] = value
        share[a, x] = edges_tile(value)

    work = list(zip(sides(pos_ref, size_x), (got_a, got_b), (ten_a, ten_b)))
    for slot, (_, got, _) in enumerate(work):
        for a in range(3):
            wide[a, slot, PAD : PAD + size_y, :] = got[ROW_NOW + a * size_y : ROW_NOW + (a + 1) * size_y, :]
            fill_sides(wide, a, slot, got[ROW_SIDE + a * 8 : ROW_SIDE + (a + 1) * 8, :], size_y)

    @pl.when(pos_ref[0] == 0)
    def _():
        for slot, ((halo, edge, _, sign), got, _) in enumerate(work):
            place = pl.ds(pl.multiple_of(edge * size_y, size_y), size_y)
            fib = [fib_ref[a, place, :] for a in range(3)]
            put(
                0,
                edge + 1,
                rows_of(next_pad, 0, edge + 1, size_y) + DT * volt_from(wide, slot, fib, sign, size_y),
            )
            fib = fiber_of(
                tab_ref, spread(got[ROW_CLASS : ROW_CLASS + cls_ref.shape[1], 0:size_y], block_depth)
            )
            put(
                0,
                halo,
                got[ROW_NEXT : ROW_NEXT + size_y, :] + DT * volt_from(pad_in, edge + 1, fib, -sign, size_y),
            )

    @pl.when(pos_ref[0] != 0)
    def _():
        for slot, ((halo, edge, which, sign), got, ten) in enumerate(work):
            stiff = got[ROW_STIFF : ROW_STIFF + size_y, :]
            own = rest[3, edge]
            now = [rows_of(pad_in, a, edge + 1, size_y) for a in range(3)]
            theirs = [rows_of(wide, a, slot, size_y) for a in range(3)]
            ties = tie_rows(list_ref[which].astype(F32), stiff, theirs)
            rate = motion_from(wide, slot, sign, size_y)
            beta = OMEGA * inverse(own)
            for a in range(3):
                put(
                    a,
                    edge + 1,
                    rows_of(next_pad, a, edge + 1, size_y) + OMEGA * rate[a] + beta * ties[a] - 0.12 * now[a],
                )
            fib = fiber_of(
                tab_ref, spread(got[ROW_CLASS : ROW_CLASS + cls_ref.shape[1], 0:size_y], block_depth)
            )
            ties = tie_rows(got[ROW_LIST : ROW_LIST + 1, 0:size_y], own, now)
            rate = motion_from(pad_in, edge + 1, -sign, size_y)
            beta = OMEGA * inverse(stiff)
            drive = got[ROW_COEF : ROW_COEF + size_y, :] * ten[...]
            for a in range(3):
                put(
                    a,
                    halo,
                    got[ROW_NEXT + a * size_y : ROW_NEXT + (a + 1) * size_y, :]
                    + OMEGA * rate[a] + beta * ties[a] + drive * fib[a],
                )


def last_kernel(
    pos_ref, rest, fib_ref, list_ref, plain, got_a, got_b, next_in, side_ref, keep, out_hbm, next_pad, out, sems
):
    size_x, size_y = rest.shape[1], rest.shape[2]
    chunk = size_x // sems.shape[0]

    def copy_out(i):
        return pltpu.make_async_copy(
            out.at[:, pl.ds(i * chunk, chunk)], out_hbm.at[0, :, pl.ds(i * chunk, chunk)], sems.at[i]
        )

    def fill(x, carry):
        for a in range(3):
            fill_sides(next_pad, a, x, side_ref[a, x], size_y)
        return carry

    @pl.when(pos_ref[0] == 0)
    def _():
        def fill_one(x, carry):
            fill_sides(next_pad, 0, x, side_ref[0, x], size_y)
            return carry

        lax.fori_loop(0, size_x + 2, fill_one, 0, unroll=3)

        def step(i, carry):
            for k in range(chunk):
                x = i * chunk + k
                place = pl.ds(pl.multiple_of(x * size_y, size_y), size_y)
                v = rows_of(next_pad, 0, x + 1, size_y)
                n, gate, leak, rest_c = [keep[k, x] for k in range(4)]
                rate = volt_rate(next_pad, x + 1, [fib_ref[a, place, :] for a in range(3)], size_y)
                flow = gate * (v - 2.0)
                out[0, x] = v + DT * (rate - flow - leak * (v + 1.0) - 0.1 * v)
                out[1, x] = rest_c - (0.3 * DT) * flow
                out[2, x] = (1.0 - DT) * n + (0.5 * DT) * (1.0 + jnp.tanh(v))
                out[3, x] = plain[place, :]
            copy_out(i).start()
            return carry

        lax.fori_loop(0, size_x // chunk, step, 0)

    @pl.when(pos_ref[0] != 0)
    def _():
        lax.fori_loop(0, size_x + 2, fill, 0, unroll=3)
        for (halo, edge, which, _), got in zip(sides(pos_ref, size_x), (got_a, got_b)):
            beta = OMEGA * inverse(rest[3, edge])
            tie = tie_rows(
                list_ref[which].astype(F32),
                got[ROW_STIFF : ROW_STIFF + size_y, :],
                [rows_of(next_pad, a, halo, size_y) for a in range(3)],
            )
            for a in range(3):
                out[a, edge] = beta * tie[a] - 0.12 * rows_of(next_pad, a, edge + 1, size_y)

        def sweep(i, carry):
            for k in range(chunk):
                x = i * chunk + k
                rate = motion_rate(next_pad, x + 1, size_y)
                tied = jnp.logical_or(x == 0, x == size_x - 1)
                for a in range(3):
                    value = 0.4 * rows_of(next_pad, a, x + 1, size_y) + keep[a, x] + OMEGA * rate[a]
                    out[a, x] = value + jnp.where(tied, out[a, x], 0.0)
                out[3, x] = keep[3, x]
            copy_out(i).start()
            return carry

        lax.fori_loop(0, size_x // chunk, sweep, 0)

    for i in range(size_x // chunk):
        copy_out(i).wait()


def fiber_table(fiber_angles):
    azimuth = fiber_angles[:, 0]
    elevation = fiber_angles[:, 1]
    return jnp.stack(
        [
            jnp.cos(azimuth) * jnp.cos(elevation),
            jnp.sin(azimuth) * jnp.cos(elevation),
            jnp.sin(elevation),
        ]
    )


def call(kernel, name, out_shape, operands, spaces, scratch=(), out_spaces=None, aliases=()):
    if out_spaces is None:
        out_spaces = [pltpu.VMEM] * len(out_shape)
    return pl.pallas_call(
        kernel,
        name=name,
        out_shape=tuple(out_shape),
        in_specs=[pl.BlockSpec(memory_space=space) for space in spaces],
        out_specs=tuple(pl.BlockSpec(memory_space=space) for space in out_spaces),
        scratch_shapes=scratch,
        input_output_aliases=dict(aliases),
        compiler_params=pltpu.CompilerParams(vmem_limit_bytes=VMEM_LIMIT),
    )(*operands)


def local(sections, fiber_angles, fiber_class, row_map, interface_rows):
    own = sections[0]
    channels, size_x, size_y, depth = own.shape
    n_gx = lax.axis_size("gx")
    n_gy = lax.axis_size("gy")
    assert n_gx % 2 == 0 and n_gy == 2
    swap_a = swap_pairs([(i, i + 1) for i in range(0, n_gx, 2)])
    swap_b = swap_pairs([(i, (i + 1) % n_gx) for i in range(1, n_gx, 2)])
    cross_a = [(s * n_gx + i, (1 - s) * n_gx + j) for s in range(2) for i, j in swap_a]
    cross_b = [(s * n_gx + i, (1 - s) * n_gx + j) for s in range(2) for i, j in swap_b]
    both = swap_pairs([(0, 1)])
    S, V, H = pltpu.SMEM, pltpu.VMEM, pltpu.HBM
    f32 = lambda *shape: jax.ShapeDtypeStruct(shape, F32)
    columns = size_x * size_y
    padded = f32(3, size_x + 2, size_y + 2 * PAD, depth)
    tiles = f32(3, size_x + 2, 8, depth)
    plane = f32(size_y, depth)

    pos = jnp.stack([lax.axis_index("sec"), lax.axis_index("gx") % 2]).astype(jnp.int32)
    table = fiber_table(fiber_angles)
    classes = fiber_class.transpose(0, 2, 1)
    lists = interface_rows.reshape(2, 1, size_y)

    pad, rest, share = call(
        load_kernel,
        "load",
        (padded, f32(channels - 3, size_x, size_y, depth), f32(3, size_x, 8, depth)),
        (pltpu.with_memory_space_constraint(own, H),),
        (H,),
        [pltpu.SemaphoreType.DMA((2,))],
    )
    side = lax.ppermute(share, "gy", both)
    plain, tension, ten_a, ten_b, fib = call(
        local_kernel,
        "local",
        (f32(columns, depth), f32(columns, depth), plane, plane, f32(3, columns, depth)),
        (pos, row_map.reshape(-1), table, pad, rest, classes),
        (S, S, S, V, V, V),
        [pltpu.VMEM((classes.shape[1], columns), jnp.int32)],
    )
    message = f32(MESSAGE_ROWS, depth)
    message_a, message_b, pad = call(
        message_kernel,
        "message",
        (message, message, padded),
        (pos, pad, rest, side, fib, classes, lists),
        (S, V, V, V, V, V, V),
        aliases={1: 2},
    )
    got_b = lax.ppermute(message_b, "gx", swap_b)
    got_a = lax.ppermute(message_a, "gx", swap_a)
    ten_b = lax.ppermute(ten_b, ("sec", "gx"), cross_b)
    ten_a = lax.ppermute(ten_a, ("sec", "gx"), cross_a)
    tension = lax.ppermute(tension, "sec", both)
    moved, share, keep = call(
        inner_kernel,
        "inner",
        (padded, tiles, f32(4, size_x, size_y, depth)),
        (pos, pad, rest, fib, tension),
        (S, V, V, V, V),
    )
    moved, share = call(
        outer_kernel,
        "outer",
        (padded, tiles),
        (pos, table, pad, rest, fib, classes, lists, got_a, got_b, ten_a, ten_b, moved, share),
        (S, S, V, V, V, V, V, V, V, V, V, V, V),
        [pltpu.VMEM((3, 2) + padded.shape[2:], F32)],
        aliases={11: 0, 12: 1},
    )
    side = lax.ppermute(share, "gy", both)
    return call(
        last_kernel,
        "last",
        (f32(1, 4, size_x, size_y, depth), padded),
        (pos, rest, fib, lists, plain, got_a, got_b, moved, side, keep),
        (S, V, V, V, V, V, V, V, V, V),
        [
            pltpu.VMEM((4, size_x, size_y, depth), F32),
            pltpu.SemaphoreType.DMA((4,)),
        ],
        out_spaces=(H, V),
        aliases={7: 1},
    )[0]


def solution(mesh):
    in_specs = (
        P("sec", None, "gx", "gy", None),
        P(),
        P("gx", "gy", None),
        P("gx", "gy", None),
        P(None, "gx", "gy", None),
    )
    out_specs = P("sec", None, "gx", "gy", None)
    return jax.shard_map(local, mesh=mesh, in_specs=in_specs, out_specs=out_specs, check_vma=False)
```

```python
import jax
import jax.numpy as jnp
from jax import lax
from jax.experimental import pallas as pl
from jax.experimental.pallas import tpu as pltpu
from jax.sharding import PartitionSpec as P

DT = 0.1
OMEGA = 0.06
F32 = jnp.float32
HIGHEST = lax.Precision.HIGHEST
VMEM_LIMIT = 32 * 1024 * 1024

PAD = 8

ROW_NOW, ROW_NEXT, ROW_STIFF, ROW_SIDE, ROW_LIST = 0, 96, 192, 224, 248
MESSAGE_ROWS = 256


def swap_pairs(pairs):
    return pairs + [(b, a) for a, b in pairs]


def inverse(v):
    r = pl.reciprocal(v, approx=True)
    return r * (2.0 - v * r)


def rise(c):
    c2 = c * c
    return c2 * inverse(c2 + 0.25)


def ends(like):
    lane = lax.broadcasted_iota(jnp.int32, like, 1)
    return lane == like[1] - 1, lane == 0


def up_z(w, last):
    return jnp.where(last, 0.0, pltpu.roll(w, w.shape[1] - 1, 1))


def down_z(w, first):
    return jnp.where(first, 0.0, pltpu.roll(w, 1, 1))


def rows_of(pad, a, x, size_y, shift=0):
    return pad[a, x, PAD + shift : PAD + shift + size_y, :]


def motion_rate(pad, x, size_y):
    at = lambda a, dx=0, dy=0: rows_of(pad, a, x + dx, size_y, dy)
    u0, u1, u2 = at(0), at(1), at(2)
    last, first = ends(u0.shape)
    w0p, w0m, w1p, w1m = at(0, 1), at(0, -1), at(1, 1), at(1, -1)
    w2p, w2m = at(2, 1), at(2, -1)
    e0, e2 = 0.5 * (w0p - w0m), 0.5 * (w2p - w2m)
    e0y = (at(0, 1, 1) - at(0, -1, 1)) - (at(0, 1, -1) - at(0, -1, -1))
    e1y = (at(1, 1, 1) - at(1, -1, 1)) - (at(1, 1, -1) - at(1, -1, -1))
    v1p, v1m, v2p, v2m = at(1, 0, 1), at(1, 0, -1), at(2, 0, 1), at(2, 0, -1)
    d2 = 0.5 * (v2p - v2m)
    d1 = 0.5 * (v1p - v1m) + e0
    r0 = (
        up_z(u0 + e2, last) + down_z(u0 - e2, first)
        + (at(0, 0, 1) + at(0, 0, -1)) + 0.5 * e1y + 3.0 * (w0p + w0m)
    )
    r1 = (
        up_z(u1 + d2, last) + down_z(u1 - d2, first)
        + 3.0 * (v1p + v1m) + 0.5 * e0y + (w1p + w1m)
    )
    t2 = 3.0 * u2
    r2 = up_z(t2 + d1, last) + down_z(t2 - d1, first) + (v2p + v2m) + (w2p + w2m)
    return r0, r1, r2


def motion_from(pad, x, sign, size_y):
    u0, u1, u2 = [rows_of(pad, a, x, size_y) for a in range(3)]
    last, first = ends(u0.shape)
    half = 0.5 * sign
    dy0 = rows_of(pad, 0, x, size_y, 1) - rows_of(pad, 0, x, size_y, -1)
    dy1 = rows_of(pad, 1, x, size_y, 1) - rows_of(pad, 1, x, size_y, -1)
    dz0 = up_z(u0, last) - down_z(u0, first)
    dz2 = up_z(u2, last) - down_z(u2, first)
    return 3.0 * u0 + half * (dy1 + dz2), u1 + half * dy0, u2 + half * dz0


def volt_rate(pad, x, fib, size_y):
    at = lambda dx=0, dy=0: rows_of(pad, 0, x + dx, size_y, dy)
    v, wp, wm, yp, ym = at(), at(1), at(-1), at(0, 1), at(0, -1)
    last, first = ends(v.shape)
    e = wp - wm
    ey = (at(1, 1) - at(-1, 1)) - (at(1, -1) - at(-1, -1))
    dy = yp - ym
    sum_z = up_z(v, last) + down_z(v, first)
    ez = up_z(e, last) - down_z(e, first)
    dyz = up_z(dy, last) - down_z(dy, first)
    g = [0.75 * w for w in fib]
    d00, d11, d22 = [0.25 + a * b for a, b in zip(g, fib)]
    return (
        d00 * (wp + wm) + d11 * (yp + ym) + d22 * sum_z - 2.0 * (d00 + d11 + d22) * v
        + 0.5 * (fib[0] * (g[1] * ey + g[2] * ez) + g[1] * fib[2] * dyz)
    )


def couplings(fib):
    g = 0.75 * fib[0]
    return 0.25 + g * fib[0], 0.5 * g * fib[1], 0.5 * g * fib[2]


def volt_from(pad, x, coupled, sign, size_y):
    v = rows_of(pad, 0, x, size_y)
    last, first = ends(v.shape)
    dy = rows_of(pad, 0, x, size_y, 1) - rows_of(pad, 0, x, size_y, -1)
    dz = up_z(v, last) - down_z(v, first)
    return coupled[0] * v + sign * (coupled[1] * dy + coupled[2] * dz)


def currents(v, c, d, f, n, r):
    q = rise(c)
    calcium_flow = 1.2 * d * f * (v - 2.0)
    return q, calcium_flow, calcium_flow + (0.8 * n + 0.6 * q * r) * (v + 1.0) + 0.1 * v


def permute_rows(listed, values):
    rows = values.shape[0]
    pick = (lax.broadcasted_iota(jnp.int32, (rows, rows), 0).astype(F32) == listed).astype(F32)
    return lax.dot_general(
        pick, values, (((0,), (0,)), ((), ())), precision=HIGHEST, preferred_element_type=F32
    )


def tie_rows(listed, stiff, u):
    joined = jnp.concatenate([2.0 * stiff * w for w in u], axis=1)
    moved = permute_rows(listed, joined)
    depth = u[0].shape[1]
    return [moved[:, a * depth : (a + 1) * depth] for a in range(3)]


def edges_tile(value):
    rows = value.shape[0]
    last = lax.broadcasted_iota(jnp.int32, (8, value.shape[1]), 0) == 7
    return jnp.where(last, value[rows - 8 :], value[:8])


def fill_sides(pad, a, x, tile, size_y):
    pad[a, x, 0:PAD, :] = tile
    pad[a, x, PAD + size_y :, :] = tile


def sides(size_x):
    out = []
    for slot in range(2):
        right = (lax.axis_index("gx") + slot) % 2 == 0
        out.append(
            (
                jnp.where(right, size_x + 1, 0),
                jnp.where(right, size_x - 1, 0),
                jnp.where(right, 1, 0),
                jnp.where(right, 1.0, -1.0).astype(F32),
            )
        )
    return out


def place_of(x, size_y):
    return pl.ds(pl.multiple_of(x * size_y, size_y), size_y)


def electric():
    return lax.axis_index("sec") == 0


def fiber_fields(angles, cls, flat, fib_ref, size_x, size_y):
    blocks, classes, depth = cls.shape[1], angles.shape[1], fib_ref.shape[2]
    azimuth, elevation = angles[0:1, :], angles[1:2, :]
    flat_part = jnp.cos(elevation)
    fib = [jnp.cos(azimuth) * flat_part, jnp.sin(azimuth) * flat_part, jnp.sin(elevation)]
    for x in range(size_x):
        flat[:, x * size_y : (x + 1) * size_y] = cls[x]
    own = lax.broadcasted_iota(jnp.int32, (blocks, depth), 1) // (depth // blocks)
    own = own == lax.broadcasted_iota(jnp.int32, (blocks, depth), 0)
    hits = jnp.concatenate([(flat[...] == k).astype(F32) for k in range(classes)], axis=0)
    table = jnp.concatenate(
        [
            jnp.concatenate(
                [jnp.where(own, jnp.broadcast_to(w[:, k : k + 1], own.shape), 0.0) for w in fib], axis=1
            )
            for k in range(classes)
        ],
        axis=0,
    )
    high = table.astype(jnp.bfloat16).astype(F32)
    mid = (table - high).astype(jnp.bfloat16).astype(F32)
    parts = jnp.concatenate([high, mid, table - high - mid], axis=0)
    found = lax.dot_general(
        jnp.concatenate([hits] * 3, axis=0), parts, (((0,), (0,)), ((), ())), preferred_element_type=F32
    )
    for a in range(3):
        fib_ref[a] = found[:, a * depth : (a + 1) * depth]


def load_kernel(
    sec_hbm, cls_hbm, ang_hbm, map_hbm, pad, rest, share, plain, edge_ten, fib_ref, cls, ang, map_ref, flat, sems
):
    size_x, size_y = sec_hbm.shape[1], sec_hbm.shape[2]
    small = [
        pltpu.make_async_copy(src, dst, sems.at[i])
        for i, (src, dst) in enumerate(((cls_hbm, cls), (ang_hbm, ang), (map_hbm, map_ref)))
    ]
    pieces = (sems.shape[0] - 3) // 2
    chunk = size_x // pieces
    main = []
    for i in range(pieces):
        here, there = pl.ds(i * chunk, chunk), pl.ds(i * chunk + 1, chunk)
        main.append(
            (
                pltpu.make_async_copy(
                    sec_hbm.at[0:3, here], pad.at[:, there, pl.ds(PAD, size_y), :], sems.at[3 + 2 * i]
                ),
                pltpu.make_async_copy(sec_hbm.at[3:8, here], rest.at[:, here], sems.at[4 + 2 * i]),
            )
        )
    for copy in small:
        copy.start()
    for pair in main:
        for copy in pair:
            copy.start()
    zeros = jnp.zeros(pad.shape[2:], F32)
    for a in range(3):
        pad[a, 0] = zeros
        pad[a, size_x + 1] = zeros
    small[0].wait()
    small[1].wait()
    fiber_fields(ang[...], cls, flat, fib_ref, size_x, size_y)

    def tension(x, carry):
        v, c, d = [rows_of(pad, a, x + 1, size_y) for a in range(3)]
        f, bound, s = rest[0, x], rest[3, x], rest[4, x]
        calcium_flow = 1.2 * d * f * (v - 2.0)
        flow = 2.0 * c * (1.0 - bound) - 0.4 * bound
        c1 = c + DT * (-0.3 * calcium_flow - 0.5 * c - flow)
        s1 = s + (0.5 * DT) * (rise(c) - s)
        plain[place_of(x, size_y), :] = s1 + (0.5 * DT) * (rise(c1) - s1)
        return carry

    def pack(x, carry):
        for a in range(3):
            share[a, x] = edges_tile(rows_of(pad, a, x + 1, size_y))
        return carry

    for i, pair in enumerate(main):
        for copy in pair:
            copy.wait()
        lax.fori_loop(i * chunk, (i + 1) * chunk, pack, 0, unroll=True)

        @pl.when(electric())
        def _():
            lax.fori_loop(i * chunk, (i + 1) * chunk, tension, 0, unroll=2)

    small[2].wait()

    @pl.when(electric())
    def _():
        last = (size_x - 1) * size_y
        for p in range(size_y):
            edge_ten[0, p : p + 1, :] = plain[pl.ds(map_ref[p], 1), :]
            edge_ten[1, p : p + 1, :] = plain[pl.ds(map_ref[last + p], 1), :]


def gather_kernel(map_ref, plain, all_ref):
    @pl.when(electric())
    def _():
        def rows(i, carry):
            for k in range(32):
                p = i * 32 + k
                all_ref[pl.ds(p, 1), :] = plain[pl.ds(map_ref[p], 1), :]
            return carry

        lax.fori_loop(0, all_ref.shape[0] // 32, rows, 0)


def message_kernel(pad_in, rest, side_ref, fib_ref, ten_ref, list_ref, a_ref, b_ref, pad):
    size_x, size_y = rest.shape[1], rest.shape[2]

    def fill(x, carry):
        for a in range(3):
            fill_sides(pad, a, x + 1, side_ref[a, x], size_y)
        return carry

    lax.fori_loop(0, size_x, fill, 0, unroll=4)
    for (_, edge, which, _), out in zip(sides(size_x), (a_ref, b_ref)):
        fib = [fib_ref[a, place_of(edge, size_y), :] for a in range(3)]
        out[ROW_LIST : ROW_LIST + 8, 0:size_y] = jnp.broadcast_to(list_ref[which].astype(F32), (8, size_y))
        for a in range(3):
            out[ROW_SIDE + a * 8 : ROW_SIDE + (a + 1) * 8, :] = side_ref[a, edge]

        @pl.when(electric())
        def _():
            v, c, d = [rows_of(pad, a, edge + 1, size_y) for a in range(3)]
            f, n, r = [rest[k, edge] for k in range(3)]
            rate = volt_rate(pad, edge + 1, fib, size_y)
            _, _, total = currents(v, c, d, f, n, r)
            for at, value in zip(
                (ROW_NOW, ROW_NOW + size_y, ROW_NOW + 2 * size_y, ROW_NEXT, ROW_NEXT + size_y),
                (v,) + couplings(fib)[:2] + (v + DT * (rate - total), couplings(fib)[2]),
            ):
                out[at : at + size_y, :] = value

        @pl.when(jnp.logical_not(electric()))
        def _():
            rate = motion_rate(pad, edge + 1, size_y)
            stiff = rest[3, edge]
            beta = OMEGA * inverse(stiff)
            act = rest[4, edge] * ten_ref[which]
            out[ROW_STIFF : ROW_STIFF + size_y, :] = stiff
            for a in range(3):
                u = rows_of(pad, a, edge + 1, size_y)
                out[ROW_NOW + a * size_y : ROW_NOW + (a + 1) * size_y, :] = u
                out[ROW_NEXT + a * size_y : ROW_NEXT + (a + 1) * size_y, :] = (
                    0.28 * u + beta * (rest[a, edge] + act * fib[a]) + OMEGA * rate[a]
                )


def inner_kernel(pad, rest, fib_ref, ten_ref, next_pad, share, keep):
    size_x, size_y = rest.shape[1], rest.shape[2]

    def put(a, x, value):
        next_pad[a, x, PAD : PAD + size_y, :] = value
        share[a, x] = edges_tile(value)

    @pl.when(electric())
    def _():
        def plane(x, carry):
            place = place_of(x, size_y)
            v, c, d = [rows_of(pad, a, x + 1, size_y) for a in range(3)]
            f, n, r, bound, _ = [rest[k, x] for k in range(5)]
            rate = volt_rate(pad, x + 1, [fib_ref[a, place, :] for a in range(3)], size_y)
            q, calcium_flow, total = currents(v, c, d, f, n, r)
            flow = 2.0 * c * (1.0 - bound) - 0.4 * bound
            put(0, x + 1, v + DT * (rate - total))
            c1 = c + DT * (-0.3 * calcium_flow - 0.5 * c - flow)
            tv = jnp.tanh(v)
            d1 = (1.0 - 2.0 * DT) * d + DT * (1.0 + jnp.tanh(v + 0.5))
            f1 = (1.0 - DT / 3.0) * f + (DT / 6.0) * (1.0 - tv)
            n1 = (1.0 - DT) * n + (0.5 * DT) * (1.0 + tv)
            r1 = (1.0 - DT / 5.0) * r + (DT / 10.0) * (1.0 + jnp.tanh(0.5 * v - 0.25))
            bound1 = bound + DT * flow
            flow1 = 2.0 * c1 * (1.0 - bound1) - 0.4 * bound1
            keep[0, x] = n1
            keep[1, x] = 1.2 * d1 * f1
            keep[2, x] = 0.8 * n1 + 0.6 * rise(c1) * r1
            keep[3, x] = c1 - DT * (0.5 * c1 + flow1)
            return carry

        lax.fori_loop(0, size_x, plane, 0, unroll=2)

    @pl.when(jnp.logical_not(electric()))
    def _():
        def plane(x, carry):
            place = place_of(x, size_y)
            rate = motion_rate(pad, x + 1, size_y)
            beta = OMEGA * inverse(rest[3, x])
            act = rest[4, x] * ten_ref[place, :]
            keep[3, x] = act
            for a in range(3):
                drive = beta * (rest[a, x] + act * fib_ref[a, place, :])
                keep[a, x] = drive
                put(a, x + 1, 0.4 * rows_of(pad, a, x + 1, size_y) + drive + OMEGA * rate[a])
            return carry

        lax.fori_loop(0, size_x, plane, 0, unroll=2)


def outer_kernel(pad, rest, fib_ref, list_ref, got_a, got_b, next_in, next_pad, share, wide):
    size_x, size_y = rest.shape[1], rest.shape[2]
    work = list(zip(sides(size_x), (got_a, got_b)))
    for slot, (_, got) in enumerate(work):
        for a in range(3):
            wide[a, slot, PAD : PAD + size_y, :] = got[ROW_NOW + a * size_y : ROW_NOW + (a + 1) * size_y, :]
            fill_sides(wide, a, slot, got[ROW_SIDE + a * 8 : ROW_SIDE + (a + 1) * 8, :], size_y)

    def put(a, x, slot, value):
        next_pad[a, x, PAD : PAD + size_y, :] = value
        share[a, slot] = edges_tile(value)

    @pl.when(electric())
    def _():
        for slot, ((halo, edge, which, sign), got) in enumerate(work):
            fib = [fib_ref[a, place_of(edge, size_y), :] for a in range(3)]
            put(
                0,
                edge + 1,
                1 + which,
                rows_of(next_pad, 0, edge + 1, size_y) + DT * volt_from(wide, slot, couplings(fib), sign, size_y),
            )
            theirs = [
                got[at : at + size_y, :] for at in (ROW_NOW + size_y, ROW_NOW + 2 * size_y, ROW_NEXT + size_y)
            ]
            put(
                0,
                halo,
                3 * which,
                got[ROW_NEXT : ROW_NEXT + size_y, :] + DT * volt_from(pad, edge + 1, theirs, -sign, size_y),
            )

    @pl.when(jnp.logical_not(electric()))
    def _():
        for slot, ((halo, edge, which, sign), got) in enumerate(work):
            stiff = got[ROW_STIFF : ROW_STIFF + size_y, :]
            own = rest[3, edge]
            now = [rows_of(pad, a, edge + 1, size_y) for a in range(3)]
            theirs = [rows_of(wide, a, slot, size_y) for a in range(3)]
            ties = tie_rows(list_ref[which].astype(F32), stiff, theirs)
            rate = motion_from(wide, slot, sign, size_y)
            beta = OMEGA * inverse(own)
            for a in range(3):
                put(
                    a,
                    edge + 1,
                    1 + which,
                    rows_of(next_pad, a, edge + 1, size_y) + OMEGA * rate[a] + beta * ties[a] - 0.12 * now[a],
                )
            ties = tie_rows(got[ROW_LIST : ROW_LIST + 1, 0:size_y], own, now)
            rate = motion_from(pad, edge + 1, -sign, size_y)
            beta = OMEGA * inverse(stiff)
            for a in range(3):
                put(
                    a,
                    halo,
                    3 * which,
                    got[ROW_NEXT + a * size_y : ROW_NEXT + (a + 1) * size_y, :] + OMEGA * rate[a] + beta * ties[a],
                )


def electric_end(x, next_pad, fib_ref, plain, keep, out):
    size_y = fib_ref.shape[1] // keep.shape[1]
    place = place_of(x, size_y)
    v = rows_of(next_pad, 0, x + 1, size_y)
    n, gate, leak, rest_c = [keep[k, x] for k in range(4)]
    rate = volt_rate(next_pad, x + 1, [fib_ref[a, place, :] for a in range(3)], size_y)
    flow = gate * (v - 2.0)
    out[0, x] = v + DT * (rate - flow - leak * (v + 1.0) - 0.1 * v)
    out[1, x] = rest_c - (0.3 * DT) * flow
    out[2, x] = (1.0 - DT) * n + (0.5 * DT) * (1.0 + jnp.tanh(v))
    out[3, x] = plain[place, :]


def mechanic_end(x, next_pad, keep, out, size_y, ties=None):
    rate = motion_rate(next_pad, x + 1, size_y)
    for a in range(3):
        u = rows_of(next_pad, a, x + 1, size_y)
        value = 0.4 * u + keep[a, x] + OMEGA * rate[a]
        out[a, x] = value if ties is None else value + ties[a] - 0.12 * u
    out[3, x] = keep[3, x]


def middle_kernel(fib_ref, plain, next_in, side_ref, keep, out_hbm, next_pad, out, sems):
    size_x = keep.shape[1]
    size_y = fib_ref.shape[1] // size_x
    pieces = sems.shape[0]
    chunk = (size_x - 4) // pieces

    def copy_out(i):
        here = pl.ds(2 + i * chunk, chunk)
        return pltpu.make_async_copy(out.at[:, here], out_hbm.at[0, :, here], sems.at[i])

    def fill(count):
        def one(x, carry):
            for a in range(count):
                fill_sides(next_pad, a, x, side_ref[a, x], size_y)
            return carry

        lax.fori_loop(2, size_x, one, 0, unroll=2)

    @pl.when(electric())
    def _():
        fill(1)

        def step(i, carry):
            for k in range(chunk):
                electric_end(2 + i * chunk + k, next_pad, fib_ref, plain, keep, out)
            copy_out(i).start()
            return carry

        lax.fori_loop(0, pieces, step, 0)

    @pl.when(jnp.logical_not(electric()))
    def _():
        fill(3)

        def sweep(i, carry):
            for k in range(chunk):
                mechanic_end(2 + i * chunk + k, next_pad, keep, out, size_y)
            copy_out(i).start()
            return carry

        lax.fori_loop(0, pieces, sweep, 0)

    for i in range(pieces):
        copy_out(i).wait()


def last_kernel(
    rest, fib_ref, list_ref, plain, got_a, got_b, next_in, side_ref, keep, out_in, out_hbm, next_pad, out, sems
):
    size_x, size_y = rest.shape[1], rest.shape[2]

    def copy_out(slot, first):
        here = pl.ds(first, 2)
        return pltpu.make_async_copy(out.at[:, here], out_hbm.at[0, :, here], sems.at[slot])

    work = []
    for slot, ((halo, edge, which, _), got) in enumerate(zip(sides(size_x), (got_a, got_b))):
        near = jnp.where(which == 1, size_x - 2, 1)
        work.append((halo, edge, near, which, got, copy_out(slot, jnp.minimum(edge, near))))

    @pl.when(electric())
    def _():
        for halo, edge, near, which, _, copy in work:
            fill_sides(next_pad, 0, halo, side_ref[0, 3 * which], size_y)
            fill_sides(next_pad, 0, edge + 1, side_ref[0, 1 + which], size_y)
            for x in (near, edge):
                electric_end(x, next_pad, fib_ref, plain, keep, out)
            copy.start()

    @pl.when(jnp.logical_not(electric()))
    def _():
        for halo, edge, near, which, got, copy in work:
            for a in range(3):
                fill_sides(next_pad, a, halo, side_ref[a, 3 * which], size_y)
                fill_sides(next_pad, a, edge + 1, side_ref[a, 1 + which], size_y)
            beta = OMEGA * inverse(rest[3, edge])
            ties = tie_rows(
                list_ref[which].astype(F32),
                got[ROW_STIFF : ROW_STIFF + size_y, :],
                [rows_of(next_pad, a, halo, size_y) for a in range(3)],
            )
            mechanic_end(near, next_pad, keep, out, size_y)
            mechanic_end(edge, next_pad, keep, out, size_y, [beta * w for w in ties])
            copy.start()

    for item in work:
        item[-1].wait()


def call(kernel, name, out_shape, operands, spaces, scratch=(), out_spaces=None, aliases=()):
    if out_spaces is None:
        out_spaces = [pltpu.VMEM] * len(out_shape)
    return pl.pallas_call(
        kernel,
        name=name,
        out_shape=tuple(out_shape),
        in_specs=[pl.BlockSpec(memory_space=space) for space in spaces],
        out_specs=tuple(pl.BlockSpec(memory_space=space) for space in out_spaces),
        scratch_shapes=scratch,
        input_output_aliases=dict(aliases),
        compiler_params=pltpu.CompilerParams(vmem_limit_bytes=VMEM_LIMIT),
    )(*operands)


def local(sections, fiber_angles, fiber_class, row_map, interface_rows):
    own = sections[0]
    channels, size_x, size_y, depth = own.shape
    n_gx = lax.axis_size("gx")
    n_gy = lax.axis_size("gy")
    assert n_gx % 2 == 0 and n_gy == 2
    swap_a = swap_pairs([(i, i + 1) for i in range(0, n_gx, 2)])
    swap_b = swap_pairs([(i, (i + 1) % n_gx) for i in range(1, n_gx, 2)])
    both = swap_pairs([(0, 1)])
    S, V, H = pltpu.SMEM, pltpu.VMEM, pltpu.HBM
    f32 = lambda *shape: jax.ShapeDtypeStruct(shape, F32)
    hbm = lambda w: pltpu.with_memory_space_constraint(w, H)
    columns = size_x * size_y
    padded = f32(3, size_x + 2, size_y + 2 * PAD, depth)
    classes = fiber_class.transpose(0, 2, 1)
    lists = interface_rows.reshape(2, 1, size_y)
    places = row_map.reshape(-1)

    pad, rest, share, plain, edge_ten, fib = call(
        load_kernel,
        "load",
        (
            padded,
            f32(channels - 3, size_x, size_y, depth),
            f32(3, size_x, 8, depth),
            f32(columns, depth),
            f32(2, size_y, depth),
            f32(3, columns, depth),
        ),
        (hbm(own), hbm(classes), hbm(fiber_angles.T), hbm(places)),
        (H, H, H, H),
        [
            pltpu.VMEM(classes.shape, jnp.int32),
            pltpu.VMEM(fiber_angles.shape[::-1], F32),
            pltpu.SMEM((columns,), jnp.int32),
            pltpu.VMEM((classes.shape[1], columns), jnp.int32),
            pltpu.SemaphoreType.DMA((3 + 2 * 4,)),
        ],
    )
    edge_ten = lax.ppermute(edge_ten, "sec", both)
    side = lax.ppermute(share, "gy", both)
    (tension,) = call(gather_kernel, "gather", (f32(columns, depth),), (places, plain), (S, V))
    tension = lax.ppermute(tension, "sec", both)
    message = f32(MESSAGE_ROWS, depth)
    message_a, message_b, pad = call(
        message_kernel,
        "message",
        (message, message, padded),
        (pad, rest, side, fib, edge_ten, lists),
        (V,) * 6,
        aliases={0: 2},
    )
    got_a = lax.ppermute(message_a, "gx", swap_a)
    got_b = lax.ppermute(message_b, "gx", swap_b)
    moved, share, keep = call(
        inner_kernel,
        "inner",
        (padded, f32(3, size_x + 2, 8, depth), f32(4, size_x, size_y, depth)),
        (pad, rest, fib, tension),
        (V,) * 4,
    )
    side = lax.ppermute(share, "gy", both)
    moved, share = call(
        outer_kernel,
        "outer",
        (padded, f32(3, 4, 8, depth)),
        (pad, rest, fib, lists, got_a, got_b, moved),
        (V,) * 7,
        [pltpu.VMEM((3, 2) + padded.shape[2:], F32)],
        aliases={6: 0},
    )
    end_side = lax.ppermute(share, "gy", both)
    fields = pltpu.VMEM((4, size_x, size_y, depth), F32)
    result = f32(1, 4, size_x, size_y, depth)
    result, moved = call(
        middle_kernel,
        "middle",
        (result, padded),
        (fib, plain, moved, side, keep),
        (V,) * 5,
        [fields, pltpu.SemaphoreType.DMA((3,))],
        out_spaces=(H, V),
        aliases={2: 1},
    )
    return call(
        last_kernel,
        "last",
        (f32(1, 4, size_x, size_y, depth), padded),
        (rest, fib, lists, plain, got_a, got_b, moved, end_side, keep, result),
        (V,) * 9 + (H,),
        [fields, pltpu.SemaphoreType.DMA((2,))],
        out_spaces=(H, V),
        aliases={6: 1, 9: 0},
    )[0]


def solution(mesh):
    in_specs = (
        P("sec", None, "gx", "gy", None),
        P(),
        P("gx", "gy", None),
        P("gx", "gy", None),
        P(None, "gx", "gy", None),
    )
    out_specs = P("sec", None, "gx", "gy", None)
    return jax.shard_map(local, mesh=mesh, in_specs=in_specs, out_specs=out_specs, check_vma=False)
```

```python
import jax
import jax.numpy as jnp
from jax import lax
from jax.experimental import pallas as pl
from jax.experimental.pallas import tpu as pltpu
from jax.sharding import PartitionSpec as P

DT = 0.1
OMEGA = 0.06
F32 = jnp.float32
HIGHEST = lax.Precision.HIGHEST
VMEM_LIMIT = 32 * 1024 * 1024
COST = (10**10, 10**7)

PAD = 8

ROW_NOW, ROW_NEXT, ROW_STIFF, ROW_SIDE, ROW_LIST = 0, 96, 192, 224, 248
MESSAGE_ROWS = 256


def swap_pairs(pairs):
    return pairs + [(b, a) for a, b in pairs]


def inverse(v):
    r = pl.reciprocal(v, approx=True)
    return r * (2.0 - v * r)


def rise(c):
    c2 = c * c
    return c2 * inverse(c2 + 0.25)


def ends(like):
    lane = lax.broadcasted_iota(jnp.int32, like, 1)
    return lane == like[1] - 1, lane == 0


def up_z(w, last):
    return jnp.where(last, 0.0, pltpu.roll(w, w.shape[1] - 1, 1))


def down_z(w, first):
    return jnp.where(first, 0.0, pltpu.roll(w, 1, 1))


def rows_of(pad, a, x, size_y, shift=0):
    return pad[a, x, PAD + shift : PAD + shift + size_y, :]


def motion_rate(pad, x, size_y):
    at = lambda a, dx=0, dy=0: rows_of(pad, a, x + dx, size_y, dy)
    u0, u1, u2 = at(0), at(1), at(2)
    last, first = ends(u0.shape)
    w0p, w0m, w1p, w1m = at(0, 1), at(0, -1), at(1, 1), at(1, -1)
    w2p, w2m = at(2, 1), at(2, -1)
    e0, e2 = 0.5 * (w0p - w0m), 0.5 * (w2p - w2m)
    e0y = (at(0, 1, 1) - at(0, -1, 1)) - (at(0, 1, -1) - at(0, -1, -1))
    e1y = (at(1, 1, 1) - at(1, -1, 1)) - (at(1, 1, -1) - at(1, -1, -1))
    v1p, v1m, v2p, v2m = at(1, 0, 1), at(1, 0, -1), at(2, 0, 1), at(2, 0, -1)
    d2 = 0.5 * (v2p - v2m)
    d1 = 0.5 * (v1p - v1m) + e0
    r0 = (
        up_z(u0 + e2, last) + down_z(u0 - e2, first)
        + (at(0, 0, 1) + at(0, 0, -1)) + 0.5 * e1y + 3.0 * (w0p + w0m)
    )
    r1 = (
        up_z(u1 + d2, last) + down_z(u1 - d2, first)
        + 3.0 * (v1p + v1m) + 0.5 * e0y + (w1p + w1m)
    )
    t2 = 3.0 * u2
    r2 = up_z(t2 + d1, last) + down_z(t2 - d1, first) + (v2p + v2m) + (w2p + w2m)
    return r0, r1, r2


def motion_from(pad, x, sign, size_y):
    u0, u1, u2 = [rows_of(pad, a, x, size_y) for a in range(3)]
    last, first = ends(u0.shape)
    half = 0.5 * sign
    dy0 = rows_of(pad, 0, x, size_y, 1) - rows_of(pad, 0, x, size_y, -1)
    dy1 = rows_of(pad, 1, x, size_y, 1) - rows_of(pad, 1, x, size_y, -1)
    dz0 = up_z(u0, last) - down_z(u0, first)
    dz2 = up_z(u2, last) - down_z(u2, first)
    return 3.0 * u0 + half * (dy1 + dz2), u1 + half * dy0, u2 + half * dz0


def volt_rate(pad, x, fib, size_y):
    at = lambda dx=0, dy=0: rows_of(pad, 0, x + dx, size_y, dy)
    v, wp, wm, yp, ym = at(), at(1), at(-1), at(0, 1), at(0, -1)
    last, first = ends(v.shape)
    e = wp - wm
    ey = (at(1, 1) - at(-1, 1)) - (at(1, -1) - at(-1, -1))
    dy = yp - ym
    sum_z = up_z(v, last) + down_z(v, first)
    ez = up_z(e, last) - down_z(e, first)
    dyz = up_z(dy, last) - down_z(dy, first)
    g = [0.75 * w for w in fib]
    d00, d11, d22 = [0.25 + a * b for a, b in zip(g, fib)]
    return (
        d00 * (wp + wm) + d11 * (yp + ym) + d22 * sum_z - 2.0 * (d00 + d11 + d22) * v
        + 0.5 * (fib[0] * (g[1] * ey + g[2] * ez) + g[1] * fib[2] * dyz)
    )


def couplings(fib):
    g = 0.75 * fib[0]
    return 0.25 + g * fib[0], 0.5 * g * fib[1], 0.5 * g * fib[2]


def volt_from(pad, x, coupled, sign, size_y):
    v = rows_of(pad, 0, x, size_y)
    last, first = ends(v.shape)
    dy = rows_of(pad, 0, x, size_y, 1) - rows_of(pad, 0, x, size_y, -1)
    dz = up_z(v, last) - down_z(v, first)
    return coupled[0] * v + sign * (coupled[1] * dy + coupled[2] * dz)


def currents(v, c, d, f, n, r):
    q = rise(c)
    calcium_flow = 1.2 * d * f * (v - 2.0)
    return q, calcium_flow, calcium_flow + (0.8 * n + 0.6 * q * r) * (v + 1.0) + 0.1 * v


def permute_rows(listed, values):
    rows = values.shape[0]
    pick = (lax.broadcasted_iota(jnp.int32, (rows, rows), 0).astype(F32) == listed).astype(F32)
    return lax.dot_general(
        pick, values, (((0,), (0,)), ((), ())), precision=HIGHEST, preferred_element_type=F32
    )


def tie_rows(listed, stiff, u):
    joined = jnp.concatenate([2.0 * stiff * w for w in u], axis=1)
    moved = permute_rows(listed, joined)
    depth = u[0].shape[1]
    return [moved[:, a * depth : (a + 1) * depth] for a in range(3)]


def edges_tile(value):
    rows = value.shape[0]
    last = lax.broadcasted_iota(jnp.int32, (8, value.shape[1]), 0) == 7
    return jnp.where(last, value[rows - 8 :], value[:8])


def fill_sides(pad, a, x, tile, size_y):
    pad[a, x, 0:PAD, :] = tile
    pad[a, x, PAD + size_y :, :] = tile


def sides(size_x):
    out = []
    for slot in range(2):
        right = (lax.axis_index("gx") + slot) % 2 == 0
        out.append(
            (
                jnp.where(right, size_x + 1, 0),
                jnp.where(right, size_x - 1, 0),
                jnp.where(right, 1, 0),
                jnp.where(right, 1.0, -1.0).astype(F32),
            )
        )
    return out


def place_of(x, size_y):
    return pl.ds(pl.multiple_of(x * size_y, size_y), size_y)


def electric():
    return lax.axis_index("sec") == 0


def fiber_fields(angles, cls, flat, fib_ref, size_x, size_y):
    blocks, classes, depth = cls.shape[1], angles.shape[1], fib_ref.shape[2]
    azimuth, elevation = angles[0:1, :], angles[1:2, :]
    flat_part = jnp.cos(elevation)
    fib = [jnp.cos(azimuth) * flat_part, jnp.sin(azimuth) * flat_part, jnp.sin(elevation)]
    for x in range(size_x):
        flat[:, x * size_y : (x + 1) * size_y] = cls[x]
    own = lax.broadcasted_iota(jnp.int32, (blocks, depth), 1) // (depth // blocks)
    own = own == lax.broadcasted_iota(jnp.int32, (blocks, depth), 0)
    hits = jnp.concatenate([(flat[...] == k).astype(F32) for k in range(classes)], axis=0)
    table = jnp.concatenate(
        [
            jnp.concatenate(
                [jnp.where(own, jnp.broadcast_to(w[:, k : k + 1], own.shape), 0.0) for w in fib], axis=1
            )
            for k in range(classes)
        ],
        axis=0,
    )
    high = table.astype(jnp.bfloat16).astype(F32)
    mid = (table - high).astype(jnp.bfloat16).astype(F32)
    parts = jnp.concatenate([high, mid, table - high - mid], axis=0)
    found = lax.dot_general(
        jnp.concatenate([hits] * 3, axis=0), parts, (((0,), (0,)), ((), ())), preferred_element_type=F32
    )
    for a in range(3):
        fib_ref[a] = found[:, a * depth : (a + 1) * depth]


def load_kernel(
    sec_hbm, cls_hbm, ang_hbm, map_hbm, pad, rest, share, plain, edge_ten, fib_ref, cls, ang, map_ref, flat, sems
):
    size_x, size_y = sec_hbm.shape[1], sec_hbm.shape[2]
    small = [
        pltpu.make_async_copy(src, dst, sems.at[i])
        for i, (src, dst) in enumerate(((cls_hbm, cls), (ang_hbm, ang), (map_hbm, map_ref)))
    ]
    pieces = (sems.shape[0] - 3) // 2
    chunk = size_x // pieces
    main = []
    for i in range(pieces):
        here, there = pl.ds(i * chunk, chunk), pl.ds(i * chunk + 1, chunk)
        main.append(
            (
                pltpu.make_async_copy(
                    sec_hbm.at[0:3, here], pad.at[:, there, pl.ds(PAD, size_y), :], sems.at[3 + 2 * i]
                ),
                pltpu.make_async_copy(sec_hbm.at[3:8, here], rest.at[:, here], sems.at[4 + 2 * i]),
            )
        )
    for copy in small:
        copy.start()
    for pair in main:
        for copy in pair:
            copy.start()
    zeros = jnp.zeros(pad.shape[2:], F32)
    for a in range(3):
        pad[a, 0] = zeros
        pad[a, size_x + 1] = zeros
    small[0].wait()
    small[1].wait()
    fiber_fields(ang[...], cls, flat, fib_ref, size_x, size_y)

    def tension(x, carry):
        v, c, d = [rows_of(pad, a, x + 1, size_y) for a in range(3)]
        f, bound, s = rest[0, x], rest[3, x], rest[4, x]
        calcium_flow = 1.2 * d * f * (v - 2.0)
        flow = 2.0 * c * (1.0 - bound) - 0.4 * bound
        c1 = c + DT * (-0.3 * calcium_flow - 0.5 * c - flow)
        s1 = s + (0.5 * DT) * (rise(c) - s)
        plain[place_of(x, size_y), :] = s1 + (0.5 * DT) * (rise(c1) - s1)
        return carry

    def pack(x, carry):
        for a in range(3):
            share[a, x] = edges_tile(rows_of(pad, a, x + 1, size_y))
        return carry

    for i, pair in enumerate(main):
        for copy in pair:
            copy.wait()
        lax.fori_loop(i * chunk, (i + 1) * chunk, pack, 0, unroll=True)

        @pl.when(electric())
        def _():
            lax.fori_loop(i * chunk, (i + 1) * chunk, tension, 0, unroll=2)

    small[2].wait()

    @pl.when(electric())
    def _():
        last = (size_x - 1) * size_y
        for p in range(size_y):
            edge_ten[0, p : p + 1, :] = plain[pl.ds(map_ref[p], 1), :]
            edge_ten[1, p : p + 1, :] = plain[pl.ds(map_ref[last + p], 1), :]


def gather_kernel(map_ref, plain, all_ref):
    @pl.when(electric())
    def _():
        def rows(i, carry):
            for k in range(32):
                p = i * 32 + k
                all_ref[pl.ds(p, 1), :] = plain[pl.ds(map_ref[p], 1), :]
            return carry

        lax.fori_loop(0, all_ref.shape[0] // 32, rows, 0)


def message_kernel(pad_in, rest, side_ref, fib_ref, ten_ref, list_ref, a_ref, b_ref, pad):
    size_x, size_y = rest.shape[1], rest.shape[2]

    def fill(x, carry):
        for a in range(3):
            fill_sides(pad, a, x + 1, side_ref[a, x], size_y)
        return carry

    lax.fori_loop(0, size_x, fill, 0, unroll=4)
    for (_, edge, which, _), out in zip(sides(size_x), (a_ref, b_ref)):
        fib = [fib_ref[a, place_of(edge, size_y), :] for a in range(3)]
        out[ROW_LIST : ROW_LIST + 8, 0:size_y] = jnp.broadcast_to(list_ref[which].astype(F32), (8, size_y))
        for a in range(3):
            out[ROW_SIDE + a * 8 : ROW_SIDE + (a + 1) * 8, :] = side_ref[a, edge]

        @pl.when(electric())
        def _():
            v, c, d = [rows_of(pad, a, edge + 1, size_y) for a in range(3)]
            f, n, r = [rest[k, edge] for k in range(3)]
            rate = volt_rate(pad, edge + 1, fib, size_y)
            _, _, total = currents(v, c, d, f, n, r)
            for at, value in zip(
                (ROW_NOW, ROW_NOW + size_y, ROW_NOW + 2 * size_y, ROW_NEXT, ROW_NEXT + size_y),
                (v,) + couplings(fib)[:2] + (v + DT * (rate - total), couplings(fib)[2]),
            ):
                out[at : at + size_y, :] = value

        @pl.when(jnp.logical_not(electric()))
        def _():
            rate = motion_rate(pad, edge + 1, size_y)
            stiff = rest[3, edge]
            beta = OMEGA * inverse(stiff)
            act = rest[4, edge] * ten_ref[which]
            out[ROW_STIFF : ROW_STIFF + size_y, :] = stiff
            for a in range(3):
                u = rows_of(pad, a, edge + 1, size_y)
                out[ROW_NOW + a * size_y : ROW_NOW + (a + 1) * size_y, :] = u
                out[ROW_NEXT + a * size_y : ROW_NEXT + (a + 1) * size_y, :] = (
                    0.28 * u + beta * (rest[a, edge] + act * fib[a]) + OMEGA * rate[a]
                )


def inner_kernel(pad, rest, fib_ref, ten_ref, next_pad, share, keep):
    size_x, size_y = rest.shape[1], rest.shape[2]

    def put(a, x, value):
        next_pad[a, x, PAD : PAD + size_y, :] = value
        share[a, x] = edges_tile(value)

    @pl.when(electric())
    def _():
        def plane(x, carry):
            place = place_of(x, size_y)
            v, c, d = [rows_of(pad, a, x + 1, size_y) for a in range(3)]
            f, n, r, bound, _ = [rest[k, x] for k in range(5)]
            rate = volt_rate(pad, x + 1, [fib_ref[a, place, :] for a in range(3)], size_y)
            q, calcium_flow, total = currents(v, c, d, f, n, r)
            flow = 2.0 * c * (1.0 - bound) - 0.4 * bound
            put(0, x + 1, v + DT * (rate - total))
            c1 = c + DT * (-0.3 * calcium_flow - 0.5 * c - flow)
            tv = jnp.tanh(v)
            d1 = (1.0 - 2.0 * DT) * d + DT * (1.0 + jnp.tanh(v + 0.5))
            f1 = (1.0 - DT / 3.0) * f + (DT / 6.0) * (1.0 - tv)
            n1 = (1.0 - DT) * n + (0.5 * DT) * (1.0 + tv)
            r1 = (1.0 - DT / 5.0) * r + (DT / 10.0) * (1.0 + jnp.tanh(0.5 * v - 0.25))
            bound1 = bound + DT * flow
            flow1 = 2.0 * c1 * (1.0 - bound1) - 0.4 * bound1
            keep[0, x] = n1
            keep[1, x] = 1.2 * d1 * f1
            keep[2, x] = 0.8 * n1 + 0.6 * rise(c1) * r1
            keep[3, x] = c1 - DT * (0.5 * c1 + flow1)
            return carry

        lax.fori_loop(0, size_x, plane, 0, unroll=2)

    @pl.when(jnp.logical_not(electric()))
    def _():
        def plane(x, carry):
            place = place_of(x, size_y)
            rate = motion_rate(pad, x + 1, size_y)
            beta = OMEGA * inverse(rest[3, x])
            act = rest[4, x] * ten_ref[place, :]
            keep[3, x] = act
            for a in range(3):
                drive = beta * (rest[a, x] + act * fib_ref[a, place, :])
                keep[a, x] = drive
                put(a, x + 1, 0.4 * rows_of(pad, a, x + 1, size_y) + drive + OMEGA * rate[a])
            return carry

        lax.fori_loop(0, size_x, plane, 0, unroll=2)


def outer_kernel(pad, rest, fib_ref, list_ref, got_a, got_b, next_in, next_pad, share, wide):
    size_x, size_y = rest.shape[1], rest.shape[2]
    work = list(zip(sides(size_x), (got_a, got_b)))
    for slot, (_, got) in enumerate(work):
        for a in range(3):
            wide[a, slot, PAD : PAD + size_y, :] = got[ROW_NOW + a * size_y : ROW_NOW + (a + 1) * size_y, :]
            fill_sides(wide, a, slot, got[ROW_SIDE + a * 8 : ROW_SIDE + (a + 1) * 8, :], size_y)

    def put(a, x, slot, value):
        next_pad[a, x, PAD : PAD + size_y, :] = value
        share[a, slot] = edges_tile(value)

    @pl.when(electric())
    def _():
        for slot, ((halo, edge, which, sign), got) in enumerate(work):
            fib = [fib_ref[a, place_of(edge, size_y), :] for a in range(3)]
            put(
                0,
                edge + 1,
                1 + which,
                rows_of(next_pad, 0, edge + 1, size_y) + DT * volt_from(wide, slot, couplings(fib), sign, size_y),
            )
            theirs = [
                got[at : at + size_y, :] for at in (ROW_NOW + size_y, ROW_NOW + 2 * size_y, ROW_NEXT + size_y)
            ]
            put(
                0,
                halo,
                3 * which,
                got[ROW_NEXT : ROW_NEXT + size_y, :] + DT * volt_from(pad, edge + 1, theirs, -sign, size_y),
            )

    @pl.when(jnp.logical_not(electric()))
    def _():
        for slot, ((halo, edge, which, sign), got) in enumerate(work):
            stiff = got[ROW_STIFF : ROW_STIFF + size_y, :]
            own = rest[3, edge]
            now = [rows_of(pad, a, edge + 1, size_y) for a in range(3)]
            theirs = [rows_of(wide, a, slot, size_y) for a in range(3)]
            ties = tie_rows(list_ref[which].astype(F32), stiff, theirs)
            rate = motion_from(wide, slot, sign, size_y)
            beta = OMEGA * inverse(own)
            for a in range(3):
                put(
                    a,
                    edge + 1,
                    1 + which,
                    rows_of(next_pad, a, edge + 1, size_y) + OMEGA * rate[a] + beta * ties[a] - 0.12 * now[a],
                )
            ties = tie_rows(got[ROW_LIST : ROW_LIST + 1, 0:size_y], own, now)
            rate = motion_from(pad, edge + 1, -sign, size_y)
            beta = OMEGA * inverse(stiff)
            for a in range(3):
                put(
                    a,
                    halo,
                    3 * which,
                    got[ROW_NEXT + a * size_y : ROW_NEXT + (a + 1) * size_y, :] + OMEGA * rate[a] + beta * ties[a],
                )


def electric_end(x, next_pad, fib_ref, plain, keep, out):
    size_y = fib_ref.shape[1] // keep.shape[1]
    place = place_of(x, size_y)
    v = rows_of(next_pad, 0, x + 1, size_y)
    n, gate, leak, rest_c = [keep[k, x] for k in range(4)]
    rate = volt_rate(next_pad, x + 1, [fib_ref[a, place, :] for a in range(3)], size_y)
    flow = gate * (v - 2.0)
    out[0, x] = v + DT * (rate - flow - leak * (v + 1.0) - 0.1 * v)
    out[1, x] = rest_c - (0.3 * DT) * flow
    out[2, x] = (1.0 - DT) * n + (0.5 * DT) * (1.0 + jnp.tanh(v))
    out[3, x] = plain[place, :]


def mechanic_end(x, next_pad, keep, out, size_y, ties=None):
    rate = motion_rate(next_pad, x + 1, size_y)
    for a in range(3):
        u = rows_of(next_pad, a, x + 1, size_y)
        value = 0.4 * u + keep[a, x] + OMEGA * rate[a]
        out[a, x] = value if ties is None else value + ties[a] - 0.12 * u
    out[3, x] = keep[3, x]


def middle_kernel(fib_ref, plain, next_in, side_ref, keep, out_hbm, next_pad, out, sems):
    size_x = keep.shape[1]
    size_y = fib_ref.shape[1] // size_x
    pieces = sems.shape[0]
    chunk = (size_x - 4) // pieces

    def copy_out(i):
        here = pl.ds(2 + i * chunk, chunk)
        return pltpu.make_async_copy(out.at[:, here], out_hbm.at[0, :, here], sems.at[i])

    def fill(count):
        def one(x, carry):
            for a in range(count):
                fill_sides(next_pad, a, x, side_ref[a, x], size_y)
            return carry

        lax.fori_loop(2, size_x, one, 0, unroll=2)

    @pl.when(electric())
    def _():
        fill(1)

        def step(i, carry):
            for k in range(chunk):
                electric_end(2 + i * chunk + k, next_pad, fib_ref, plain, keep, out)
            copy_out(i).start()
            return carry

        lax.fori_loop(0, pieces, step, 0)

    @pl.when(jnp.logical_not(electric()))
    def _():
        fill(3)

        def sweep(i, carry):
            for k in range(chunk):
                mechanic_end(2 + i * chunk + k, next_pad, keep, out, size_y)
            copy_out(i).start()
            return carry

        lax.fori_loop(0, pieces, sweep, 0)

    for i in range(pieces):
        copy_out(i).wait()


def last_kernel(
    rest, fib_ref, list_ref, plain, got_a, got_b, next_in, side_ref, keep, out_in, out_hbm, next_pad, out, sems
):
    size_x, size_y = rest.shape[1], rest.shape[2]

    def copy_out(slot, first):
        here = pl.ds(first, 2)
        return pltpu.make_async_copy(out.at[:, here], out_hbm.at[0, :, here], sems.at[slot])

    work = []
    for slot, ((halo, edge, which, _), got) in enumerate(zip(sides(size_x), (got_a, got_b))):
        near = jnp.where(which == 1, size_x - 2, 1)
        work.append((halo, edge, near, which, got, copy_out(slot, jnp.minimum(edge, near))))

    @pl.when(electric())
    def _():
        for halo, edge, near, which, _, copy in work:
            fill_sides(next_pad, 0, halo, side_ref[0, 3 * which], size_y)
            fill_sides(next_pad, 0, edge + 1, side_ref[0, 1 + which], size_y)
            for x in (near, edge):
                electric_end(x, next_pad, fib_ref, plain, keep, out)
            copy.start()

    @pl.when(jnp.logical_not(electric()))
    def _():
        for halo, edge, near, which, got, copy in work:
            for a in range(3):
                fill_sides(next_pad, a, halo, side_ref[a, 3 * which], size_y)
                fill_sides(next_pad, a, edge + 1, side_ref[a, 1 + which], size_y)
            beta = OMEGA * inverse(rest[3, edge])
            ties = tie_rows(
                list_ref[which].astype(F32),
                got[ROW_STIFF : ROW_STIFF + size_y, :],
                [rows_of(next_pad, a, halo, size_y) for a in range(3)],
            )
            mechanic_end(near, next_pad, keep, out, size_y)
            mechanic_end(edge, next_pad, keep, out, size_y, [beta * w for w in ties])
            copy.start()

    for item in work:
        item[-1].wait()


def call(kernel, name, out_shape, operands, spaces, scratch=(), out_spaces=None, aliases=(), weight=1):
    if out_spaces is None:
        out_spaces = [pltpu.VMEM] * len(out_shape)
    return pl.pallas_call(
        kernel,
        name=name,
        out_shape=tuple(out_shape),
        in_specs=[pl.BlockSpec(memory_space=space) for space in spaces],
        out_specs=tuple(pl.BlockSpec(memory_space=space) for space in out_spaces),
        scratch_shapes=scratch,
        input_output_aliases=dict(aliases),
        cost_estimate=pl.CostEstimate(
            flops=weight * COST[0], bytes_accessed=weight * COST[1], transcendentals=0
        ),
        compiler_params=pltpu.CompilerParams(vmem_limit_bytes=VMEM_LIMIT),
    )(*operands)


def local(sections, fiber_angles, fiber_class, row_map, interface_rows):
    own = sections[0]
    channels, size_x, size_y, depth = own.shape
    n_gx = lax.axis_size("gx")
    n_gy = lax.axis_size("gy")
    assert n_gx % 2 == 0 and n_gy == 2
    swap_a = swap_pairs([(i, i + 1) for i in range(0, n_gx, 2)])
    swap_b = swap_pairs([(i, (i + 1) % n_gx) for i in range(1, n_gx, 2)])
    both = swap_pairs([(0, 1)])
    S, V, H = pltpu.SMEM, pltpu.VMEM, pltpu.HBM
    f32 = lambda *shape: jax.ShapeDtypeStruct(shape, F32)
    hbm = lambda w: pltpu.with_memory_space_constraint(w, H)
    columns = size_x * size_y
    padded = f32(3, size_x + 2, size_y + 2 * PAD, depth)
    classes = fiber_class.transpose(0, 2, 1)
    lists = interface_rows.reshape(2, 1, size_y)
    places = row_map.reshape(-1)

    pad, rest, share, plain, edge_ten, fib = call(
        load_kernel,
        "load",
        (
            padded,
            f32(channels - 3, size_x, size_y, depth),
            f32(3, size_x, 8, depth),
            f32(columns, depth),
            f32(2, size_y, depth),
            f32(3, columns, depth),
        ),
        (hbm(own), hbm(classes), hbm(fiber_angles.T), hbm(places)),
        (H, H, H, H),
        [
            pltpu.VMEM(classes.shape, jnp.int32),
            pltpu.VMEM(fiber_angles.shape[::-1], F32),
            pltpu.SMEM((columns,), jnp.int32),
            pltpu.VMEM((classes.shape[1], columns), jnp.int32),
            pltpu.SemaphoreType.DMA((3 + 2 * 4,)),
        ],
    )
    edge_ten = lax.ppermute(edge_ten, "sec", both)
    side = lax.ppermute(share, "gy", both)
    (tension,) = call(
        gather_kernel, "gather", (f32(columns, depth),), (places, plain), (S, V), weight=6
    )
    tension = lax.ppermute(tension, "sec", both)
    message = f32(MESSAGE_ROWS, depth)
    message_a, message_b, pad = call(
        message_kernel,
        "message",
        (message, message, padded),
        (pad, rest, side, fib, edge_ten, lists),
        (V,) * 6,
        aliases={0: 2},
    )
    got_a = lax.ppermute(message_a, "gx", swap_a)
    got_b = lax.ppermute(message_b, "gx", swap_b)
    moved, share, keep = call(
        inner_kernel,
        "inner",
        (padded, f32(3, size_x + 2, 8, depth), f32(4, size_x, size_y, depth)),
        (pad, rest, fib, tension),
        (V,) * 4,
        weight=6,
    )
    side = lax.ppermute(share, "gy", both)
    moved, share = call(
        outer_kernel,
        "outer",
        (padded, f32(3, 4, 8, depth)),
        (pad, rest, fib, lists, got_a, got_b, moved),
        (V,) * 7,
        [pltpu.VMEM((3, 2) + padded.shape[2:], F32)],
        aliases={6: 0},
    )
    end_side = lax.ppermute(share, "gy", both)
    fields = pltpu.VMEM((4, size_x, size_y, depth), F32)
    result = f32(1, 4, size_x, size_y, depth)
    result, moved = call(
        middle_kernel,
        "middle",
        (result, padded),
        (fib, plain, moved, side, keep),
        (V,) * 5,
        [fields, pltpu.SemaphoreType.DMA((3,))],
        out_spaces=(H, V),
        aliases={2: 1},
        weight=6,
    )
    return call(
        last_kernel,
        "last",
        (f32(1, 4, size_x, size_y, depth), padded),
        (rest, fib, lists, plain, got_a, got_b, moved, end_side, keep, result),
        (V,) * 9 + (H,),
        [fields, pltpu.SemaphoreType.DMA((2,))],
        out_spaces=(H, V),
        aliases={6: 1, 9: 0},
    )[0]


def solution(mesh):
    in_specs = (
        P("sec", None, "gx", "gy", None),
        P(),
        P("gx", "gy", None),
        P("gx", "gy", None),
        P(None, "gx", "gy", None),
    )
    out_specs = P("sec", None, "gx", "gy", None)
    return jax.shard_map(local, mesh=mesh, in_specs=in_specs, out_specs=out_specs, check_vma=False)
```

```python
import jax
import jax.numpy as jnp
from jax import lax
from jax.experimental import pallas as pl
from jax.experimental.pallas import tpu as pltpu
from jax.sharding import PartitionSpec as P

DT = 0.1
OMEGA = 0.06
F32 = jnp.float32
HIGHEST = lax.Precision.HIGHEST
VMEM_LIMIT = 16 * 1024 * 1024
COST = (10**10, 10**7)

PAD = 8

ROW_NOW, ROW_NEXT, ROW_STIFF, ROW_SIDE = 0, 96, 192, 224
ROW_LIST = ROW_SIDE + 6
MESSAGE_ROWS = 232


def inverse(v):
    r = pl.reciprocal(v, approx=True)
    return r * (2.0 - v * r)


def rise(c):
    c2 = c * c
    return c2 * inverse(c2 + 0.25)


def ends(like):
    lane = lax.broadcasted_iota(jnp.int32, like, 1)
    return lane == like[1] - 1, lane == 0


def up_z(w, last):
    return jnp.where(last, 0.0, pltpu.roll(w, w.shape[1] - 1, 1))


def down_z(w, first):
    return jnp.where(first, 0.0, pltpu.roll(w, 1, 1))


def rows_of(pad, a, x, size_y, shift=0):
    return pad[a, x, PAD + shift : PAD + shift + size_y, :]


def motion_rate(pad, x, size_y):
    at = lambda a, dx=0, dy=0: rows_of(pad, a, x + dx, size_y, dy)
    u0, u1, u2 = at(0), at(1), at(2)
    last, first = ends(u0.shape)
    w0p, w0m, w1p, w1m = at(0, 1), at(0, -1), at(1, 1), at(1, -1)
    w2p, w2m = at(2, 1), at(2, -1)
    e0, e2 = 0.5 * (w0p - w0m), 0.5 * (w2p - w2m)
    e0y = (at(0, 1, 1) - at(0, -1, 1)) - (at(0, 1, -1) - at(0, -1, -1))
    e1y = (at(1, 1, 1) - at(1, -1, 1)) - (at(1, 1, -1) - at(1, -1, -1))
    v1p, v1m, v2p, v2m = at(1, 0, 1), at(1, 0, -1), at(2, 0, 1), at(2, 0, -1)
    d2 = 0.5 * (v2p - v2m)
    d1 = 0.5 * (v1p - v1m) + e0
    r0 = (
        up_z(u0 + e2, last) + down_z(u0 - e2, first)
        + (at(0, 0, 1) + at(0, 0, -1)) + 0.5 * e1y + 3.0 * (w0p + w0m)
    )
    r1 = (
        up_z(u1 + d2, last) + down_z(u1 - d2, first)
        + 3.0 * (v1p + v1m) + 0.5 * e0y + (w1p + w1m)
    )
    t2 = 3.0 * u2
    r2 = up_z(t2 + d1, last) + down_z(t2 - d1, first) + (v2p + v2m) + (w2p + w2m)
    return r0, r1, r2


def motion_from(pad, x, sign, size_y):
    u0, u1, u2 = [rows_of(pad, a, x, size_y) for a in range(3)]
    last, first = ends(u0.shape)
    half = 0.5 * sign
    dy0 = rows_of(pad, 0, x, size_y, 1) - rows_of(pad, 0, x, size_y, -1)
    dy1 = rows_of(pad, 1, x, size_y, 1) - rows_of(pad, 1, x, size_y, -1)
    dz0 = up_z(u0, last) - down_z(u0, first)
    dz2 = up_z(u2, last) - down_z(u2, first)
    return 3.0 * u0 + half * (dy1 + dz2), u1 + half * dy0, u2 + half * dz0


def volt_rate(pad, x, fib, size_y):
    at = lambda dx=0, dy=0: rows_of(pad, 0, x + dx, size_y, dy)
    v, wp, wm, yp, ym = at(), at(1), at(-1), at(0, 1), at(0, -1)
    last, first = ends(v.shape)
    e = wp - wm
    ey = (at(1, 1) - at(-1, 1)) - (at(1, -1) - at(-1, -1))
    dy = yp - ym
    sum_z = up_z(v, last) + down_z(v, first)
    ez = up_z(e, last) - down_z(e, first)
    dyz = up_z(dy, last) - down_z(dy, first)
    g = [0.75 * w for w in fib]
    d00, d11, d22 = [0.25 + a * b for a, b in zip(g, fib)]
    return (
        d00 * (wp + wm) + d11 * (yp + ym) + d22 * sum_z - 2.0 * (d00 + d11 + d22) * v
        + 0.5 * (fib[0] * (g[1] * ey + g[2] * ez) + g[1] * fib[2] * dyz)
    )


def couplings(fib):
    g = 0.75 * fib[0]
    return 0.25 + g * fib[0], 0.5 * g * fib[1], 0.5 * g * fib[2]


def volt_from(pad, x, coupled, sign, size_y):
    v = rows_of(pad, 0, x, size_y)
    last, first = ends(v.shape)
    dy = rows_of(pad, 0, x, size_y, 1) - rows_of(pad, 0, x, size_y, -1)
    dz = up_z(v, last) - down_z(v, first)
    return coupled[0] * v + sign * (coupled[1] * dy + coupled[2] * dz)


def currents(v, c, d, f, n, r):
    q = rise(c)
    calcium_flow = 1.2 * d * f * (v - 2.0)
    return q, calcium_flow, calcium_flow + (0.8 * n + 0.6 * q * r) * (v + 1.0) + 0.1 * v


def permute_rows(listed, values):
    rows = values.shape[0]
    pick = (lax.broadcasted_iota(jnp.int32, (rows, rows), 0).astype(F32) == listed).astype(F32)
    return lax.dot_general(
        pick, values, (((0,), (0,)), ((), ())), precision=HIGHEST, preferred_element_type=F32
    )


def tie_rows(listed, stiff, u):
    joined = jnp.concatenate([2.0 * stiff * w for w in u], axis=1)
    moved = permute_rows(listed, joined)
    depth = u[0].shape[1]
    return [moved[:, a * depth : (a + 1) * depth] for a in range(3)]


def edges_tile(value):
    rows = value.shape[0]
    last = lax.broadcasted_iota(jnp.int32, (8, value.shape[1]), 0) == 7
    return jnp.where(last, value[rows - 8 :], value[:8])


def fill_sides(pad, a, x, tile, size_y):
    pad[a, x, 0:PAD, :] = tile
    pad[a, x, PAD + size_y :, :] = tile


def sides(size_x):
    return (0, 0, -1.0), (size_x + 1, size_x - 1, 1.0)


def place_of(x, size_y):
    return pl.ds(pl.multiple_of(x * size_y, size_y), size_y)


def electric():
    return lax.axis_index("sec") == 0


def fiber_fields(angles, cls, flat, fib_ref, size_x, size_y):
    blocks, classes, depth = cls.shape[1], angles.shape[1], fib_ref.shape[2]
    azimuth, elevation = angles[0:1, :], angles[1:2, :]
    flat_part = jnp.cos(elevation)
    fib = [jnp.cos(azimuth) * flat_part, jnp.sin(azimuth) * flat_part, jnp.sin(elevation)]
    for x in range(size_x):
        flat[:, x * size_y : (x + 1) * size_y] = cls[x]
    own = lax.broadcasted_iota(jnp.int32, (blocks, depth), 1) // (depth // blocks)
    own = own == lax.broadcasted_iota(jnp.int32, (blocks, depth), 0)
    hits = jnp.concatenate([(flat[...] == k).astype(F32) for k in range(classes)], axis=0)
    table = jnp.concatenate(
        [
            jnp.concatenate(
                [jnp.where(own, jnp.broadcast_to(w[:, k : k + 1], own.shape), 0.0) for w in fib], axis=1
            )
            for k in range(classes)
        ],
        axis=0,
    )
    high = table.astype(jnp.bfloat16).astype(F32)
    mid = (table - high).astype(jnp.bfloat16).astype(F32)
    parts = jnp.concatenate([high, mid, table - high - mid], axis=0)
    found = lax.dot_general(
        jnp.concatenate([hits] * 3, axis=0), parts, (((0,), (0,)), ((), ())), preferred_element_type=F32
    )
    for a in range(3):
        fib_ref[a] = found[:, a * depth : (a + 1) * depth]


def tension_kernel(sec_hbm, map_hbm, plain, edge_ten, main, gate, late, map_ref, sems):
    size_x, size_y = sec_hbm.shape[1], sec_hbm.shape[2]
    pieces = (sems.shape[0] - 1) // 3
    chunk = size_x // pieces

    def plane(x, carry):
        v, c, d, f, bound, s = main[0, x], main[1, x], main[2, x], gate[0, x], late[0, x], late[1, x]
        calcium_flow = 1.2 * d * f * (v - 2.0)
        flow = 2.0 * c * (1.0 - bound) - 0.4 * bound
        c1 = c + DT * (-0.3 * calcium_flow - 0.5 * c - flow)
        s1 = s + (0.5 * DT) * (rise(c) - s)
        plain[place_of(x, size_y), :] = s1 + (0.5 * DT) * (rise(c1) - s1)
        return carry

    @pl.when(electric())
    def _():
        places = pltpu.make_async_copy(map_hbm, map_ref, sems.at[0])
        copies = []
        for i in range(pieces):
            here = pl.ds(i * chunk, chunk)
            copies.append(
                [
                    pltpu.make_async_copy(sec_hbm.at[src, here], dst.at[:, here], sems.at[1 + 3 * i + k])
                    for k, (src, dst) in enumerate(
                        ((pl.ds(0, 3), main), (pl.ds(3, 1), gate), (pl.ds(6, 2), late))
                    )
                ]
            )
            for copy in copies[-1]:
                copy.start()
        places.start()
        for i in range(pieces):
            for copy in copies[i]:
                copy.wait()
            lax.fori_loop(i * chunk, (i + 1) * chunk, plane, 0, unroll=2)
        places.wait()
        last = (size_x - 1) * size_y
        for p in range(size_y):
            edge_ten[0, p : p + 1, :] = plain[pl.ds(map_ref[p], 1), :]
            edge_ten[1, p : p + 1, :] = plain[pl.ds(map_ref[last + p], 1), :]


def share_kernel(own, pad, share):
    size_x, size_y = own.shape[1], own.shape[2]
    zeros = jnp.zeros(pad.shape[2:], F32)
    for a in range(3):
        pad[a, 0] = zeros
        pad[a, size_x + 1] = zeros

    def plane(x, carry):
        for a in range(3):
            value = own[a, x]
            pad[a, x + 1, PAD : PAD + size_y, :] = value
            share[a, x] = edges_tile(value)
        return carry

    lax.fori_loop(0, size_x, plane, 0, unroll=4)


def gather_kernel(map_hbm, plain, cls_ref, ang_ref, all_ref, fib_ref, out_hbm, map_ref, flat, sems):
    size_x = cls_ref.shape[0]
    size_y = all_ref.shape[0] // size_x
    places = pltpu.make_async_copy(map_hbm, map_ref, sems.at[0])
    copies = [
        pltpu.make_async_copy(plain.at[x * size_y : (x + 1) * size_y], out_hbm.at[0, 3, x], sems.at[1 + x])
        for x in range(size_x)
    ]

    @pl.when(electric())
    def _():
        places.start()
        for copy in copies:
            copy.start()

    fiber_fields(ang_ref[...], cls_ref, flat, fib_ref, size_x, size_y)

    @pl.when(electric())
    def _():
        places.wait()

        def rows(i, carry):
            for k in range(32):
                p = i * 32 + k
                all_ref[pl.ds(p, 1), :] = plain[pl.ds(map_ref[p], 1), :]
            return carry

        lax.fori_loop(0, all_ref.shape[0] // 32, rows, 0)
        for copy in copies:
            copy.wait()


def message_electric(pad_in, own, side_ref, fib_ref, list_ref, high_ref, low_ref, pad):
    size_x, size_y = own.shape[1], own.shape[2]

    def fill(x, carry):
        for a in range(3):
            fill_sides(pad, a, x + 1, side_ref[a, x], size_y)
        return carry

    lax.fori_loop(0, size_x, fill, 0, unroll=4)
    for which, ((_, edge, _), out) in enumerate(zip(sides(size_x), (low_ref, high_ref))):
        for a in range(3):
            row = ROW_SIDE + 2 * a
            out[row : row + 1, :] = side_ref[a, edge, 7:8, :]
            out[row + 1 : row + 2, :] = side_ref[a, edge, 0:1, :]
        out[ROW_LIST : ROW_LIST + 1, 0:size_y] = list_ref[which].astype(F32)

        @pl.when(electric())
        def _():
            fib = [fib_ref[a, place_of(edge, size_y), :] for a in range(3)]
            v, c, d = [rows_of(pad, a, edge + 1, size_y) for a in range(3)]
            f, n, r = [own[k, edge] for k in range(3, 6)]
            rate = volt_rate(pad, edge + 1, fib, size_y)
            _, _, total = currents(v, c, d, f, n, r)
            for at, value in zip(
                (ROW_NOW, ROW_NOW + size_y, ROW_NOW + 2 * size_y, ROW_NEXT, ROW_NEXT + size_y),
                (v,) + couplings(fib)[:2] + (v + DT * (rate - total), couplings(fib)[2]),
            ):
                out[at : at + size_y, :] = value

        @pl.when(jnp.logical_not(electric()))
        def _():
            rate = motion_rate(pad, edge + 1, size_y)
            stiff = own[6, edge]
            beta = OMEGA * inverse(stiff)
            out[ROW_STIFF : ROW_STIFF + size_y, :] = stiff
            for a in range(3):
                u = rows_of(pad, a, edge + 1, size_y)
                out[ROW_NOW + a * size_y : ROW_NOW + (a + 1) * size_y, :] = u
                out[ROW_NEXT + a * size_y : ROW_NEXT + (a + 1) * size_y, :] = (
                    0.28 * u + beta * own[3 + a, edge] + OMEGA * rate[a]
                )


def message_mechanic(own, fib_ref, ten_ref, high_in, low_in, high_ref, low_ref):
    size_x, size_y = own.shape[1], own.shape[2]

    @pl.when(jnp.logical_not(electric()))
    def _():
        for which, ((_, edge, _), out) in enumerate(zip(sides(size_x), (low_ref, high_ref))):
            act = OMEGA * inverse(own[6, edge]) * own[7, edge] * ten_ref[which]
            for a in range(3):
                rows = slice(ROW_NEXT + a * size_y, ROW_NEXT + (a + 1) * size_y)
                out[rows, :] = out[rows, :] + act * fib_ref[a, place_of(edge, size_y), :]


def put_inner(next_pad, share, a, x, value):
    next_pad[a, x, PAD : PAD + value.shape[0], :] = value
    share[a, x] = edges_tile(value)


def inner_electric(pad, own, fib_ref, next_pad, share, keep):
    size_x, size_y = own.shape[1], own.shape[2]

    @pl.when(electric())
    def _():
        def plane(x, carry):
            place = place_of(x, size_y)
            v, c, d = [rows_of(pad, a, x + 1, size_y) for a in range(3)]
            f, n, r, bound, _ = [own[k, x] for k in range(3, 8)]
            rate = volt_rate(pad, x + 1, [fib_ref[a, place, :] for a in range(3)], size_y)
            q, calcium_flow, total = currents(v, c, d, f, n, r)
            flow = 2.0 * c * (1.0 - bound) - 0.4 * bound
            put_inner(next_pad, share, 0, x + 1, v + DT * (rate - total))
            c1 = c + DT * (-0.3 * calcium_flow - 0.5 * c - flow)
            tv = jnp.tanh(v)
            d1 = (1.0 - 2.0 * DT) * d + DT * (1.0 + jnp.tanh(v + 0.5))
            f1 = (1.0 - DT / 3.0) * f + (DT / 6.0) * (1.0 - tv)
            n1 = (1.0 - DT) * n + (0.5 * DT) * (1.0 + tv)
            r1 = (1.0 - DT / 5.0) * r + (DT / 10.0) * (1.0 + jnp.tanh(0.5 * v - 0.25))
            bound1 = bound + DT * flow
            flow1 = 2.0 * c1 * (1.0 - bound1) - 0.4 * bound1
            keep[0, x] = n1
            keep[1, x] = 1.2 * d1 * f1
            keep[2, x] = 0.8 * n1 + 0.6 * rise(c1) * r1
            keep[3, x] = c1 - DT * (0.5 * c1 + flow1)
            return carry

        lax.fori_loop(0, size_x, plane, 0, unroll=2)


def inner_mechanic(pad, own, fib_ref, ten_ref, next_in, share_in, keep_in, next_pad, share, keep):
    size_x, size_y = own.shape[1], own.shape[2]

    @pl.when(jnp.logical_not(electric()))
    def _():
        def plane(x, carry):
            place = place_of(x, size_y)
            rate = motion_rate(pad, x + 1, size_y)
            beta = OMEGA * inverse(own[6, x])
            act = own[7, x] * ten_ref[place, :]
            keep[3, x] = act
            for a in range(3):
                drive = beta * (own[3 + a, x] + act * fib_ref[a, place, :])
                keep[a, x] = drive
                value = 0.4 * rows_of(pad, a, x + 1, size_y) + drive + OMEGA * rate[a]
                put_inner(next_pad, share, a, x + 1, value)
            return carry

        lax.fori_loop(0, size_x, plane, 0, unroll=2)


def outer_kernel(pad, own, fib_ref, list_ref, got_low, got_high, next_in, next_pad, share, wide):
    size_x, size_y = own.shape[1], own.shape[2]
    work = list(zip(sides(size_x), (got_low, got_high)))
    for slot, (_, got) in enumerate(work):
        for a in range(3):
            wide[a, slot, PAD : PAD + size_y, :] = got[ROW_NOW + a * size_y : ROW_NOW + (a + 1) * size_y, :]
            row = ROW_SIDE + 2 * a
            wide[a, slot, PAD - 1 : PAD, :] = got[row : row + 1, :]
            wide[a, slot, PAD + size_y : PAD + size_y + 1, :] = got[row + 1 : row + 2, :]

    def put(a, x, slot, value):
        next_pad[a, x, PAD : PAD + size_y, :] = value
        share[a, slot] = edges_tile(value)

    @pl.when(electric())
    def _():
        for which, ((halo, edge, sign), got) in enumerate(work):
            fib = [fib_ref[a, place_of(edge, size_y), :] for a in range(3)]
            put(
                0,
                edge + 1,
                1 + which,
                rows_of(next_pad, 0, edge + 1, size_y) + DT * volt_from(wide, which, couplings(fib), sign, size_y),
            )
            theirs = [
                got[at : at + size_y, :] for at in (ROW_NOW + size_y, ROW_NOW + 2 * size_y, ROW_NEXT + size_y)
            ]
            put(
                0,
                halo,
                3 * which,
                got[ROW_NEXT : ROW_NEXT + size_y, :] + DT * volt_from(pad, edge + 1, theirs, -sign, size_y),
            )

    @pl.when(jnp.logical_not(electric()))
    def _():
        for which, ((halo, edge, sign), got) in enumerate(work):
            stiff = got[ROW_STIFF : ROW_STIFF + size_y, :]
            stiff_own = own[6, edge]
            now = [rows_of(pad, a, edge + 1, size_y) for a in range(3)]
            theirs = [rows_of(wide, a, which, size_y) for a in range(3)]
            ties = tie_rows(list_ref[which].astype(F32), stiff, theirs)
            rate = motion_from(wide, which, sign, size_y)
            beta = OMEGA * inverse(stiff_own)
            for a in range(3):
                put(
                    a,
                    edge + 1,
                    1 + which,
                    rows_of(next_pad, a, edge + 1, size_y) + OMEGA * rate[a] + beta * ties[a] - 0.12 * now[a],
                )
            ties = tie_rows(got[ROW_LIST : ROW_LIST + 1, 0:size_y], stiff_own, now)
            rate = motion_from(pad, edge + 1, -sign, size_y)
            beta = OMEGA * inverse(stiff)
            for a in range(3):
                put(
                    a,
                    halo,
                    3 * which,
                    got[ROW_NEXT + a * size_y : ROW_NEXT + (a + 1) * size_y, :] + OMEGA * rate[a] + beta * ties[a],
                )


def electric_end(x, next_pad, fib_ref):
    size_y = next_pad.shape[2] - 2 * PAD
    place = place_of(x, size_y)
    return rows_of(next_pad, 0, x + 1, size_y) + DT * volt_rate(
        next_pad, x + 1, [fib_ref[a, place, :] for a in range(3)], size_y
    )


def electric_rest(x, next_pad, keep, out):
    size_y = next_pad.shape[2] - 2 * PAD
    v = rows_of(next_pad, 0, x + 1, size_y)
    n, gate, leak, rest_c = [keep[k, x] for k in range(4)]
    flow = gate * (v - 2.0)
    out[0, x] = -DT * (flow + leak * (v + 1.0) + 0.1 * v)
    out[1, x] = rest_c - (0.3 * DT) * flow
    out[2, x] = (1.0 - DT) * n + (0.5 * DT) * (1.0 + jnp.tanh(v))


def mechanic_end(x, next_pad, keep, out, size_y, ties=None):
    rate = motion_rate(next_pad, x + 1, size_y)
    for a in range(3):
        u = rows_of(next_pad, a, x + 1, size_y)
        value = 0.4 * u + keep[a, x] + OMEGA * rate[a]
        out[a, x] = value if ties is None else value + ties[a] - 0.12 * u


def middle_kernel(fib_ref, next_in, side_ref, keep, out_in, out_hbm, next_pad, held, out, sems):
    size_x = keep.shape[1]
    size_y = fib_ref.shape[1] // size_x
    pieces = sems.shape[0] - 1
    chunk = (size_x - 4) // pieces

    def copy_out(i, fields):
        here = pl.ds(2 + i * chunk, chunk)
        return pltpu.make_async_copy(out.at[0:fields, here], out_hbm.at[0, 0:fields, here], sems.at[i])

    def fill(count):
        def one(x, carry):
            for a in range(count):
                fill_sides(next_pad, a, x, side_ref[a, x], size_y)
            return carry

        lax.fori_loop(2, size_x, one, 0, unroll=2)

    @pl.when(electric())
    def _():
        fill(1)

        def rest(x, carry):
            electric_rest(x, next_pad, keep, out)
            return carry

        lax.fori_loop(0, size_x, rest, 0, unroll=2)
        copy = pltpu.make_async_copy(out.at[1:3], out_hbm.at[0, 1:3], sems.at[pieces])
        copy.start()
        for i, x in enumerate((0, 1, size_x - 2, size_x - 1)):
            held[i] = out[0, x]

        def step(i, carry):
            for k in range(chunk):
                x = 2 + i * chunk + k
                out[0, x] = out[0, x] + electric_end(x, next_pad, fib_ref)
            copy_out(i, 1).start()
            return carry

        lax.fori_loop(0, pieces, step, 0)
        copy.wait()
        for i in range(pieces):
            copy_out(i, 1).wait()

    @pl.when(jnp.logical_not(electric()))
    def _():
        fill(3)
        copy = pltpu.make_async_copy(keep.at[3:4], out_hbm.at[0, 3:4], sems.at[pieces])
        copy.start()

        def sweep(i, carry):
            for k in range(chunk):
                mechanic_end(2 + i * chunk + k, next_pad, keep, out, size_y)
            copy_out(i, 3).start()
            return carry

        lax.fori_loop(0, pieces, sweep, 0)
        copy.wait()
        for i in range(pieces):
            copy_out(i, 3).wait()


def last_kernel(
    own, fib_ref, list_ref, got_low, got_high, next_in, side_ref, keep, held, out_in, out_hbm, next_pad, out, sems
):
    size_x, size_y = own.shape[1], own.shape[2]

    def copy_out(which, first, fields):
        here = pl.ds(first, 2)
        return pltpu.make_async_copy(out.at[0:fields, here], out_hbm.at[0, 0:fields, here], sems.at[which])

    work = []
    for which, ((halo, edge, _), got) in enumerate(zip(sides(size_x), (got_low, got_high))):
        near = abs(edge - 1)
        work.append((halo, edge, near, which, got, min(edge, near)))

    @pl.when(electric())
    def _():
        for halo, edge, near, which, _, first in work:
            fill_sides(next_pad, 0, halo, side_ref[0, 3 * which], size_y)
            fill_sides(next_pad, 0, edge + 1, side_ref[0, 1 + which], size_y)
            for x in (near, edge):
                out[0, x] = held[2 * which + x - first] + electric_end(x, next_pad, fib_ref)
            copy_out(which, first, 1).start()
        for item in work:
            copy_out(item[3], item[-1], 1).wait()

    @pl.when(jnp.logical_not(electric()))
    def _():
        for halo, edge, near, which, got, first in work:
            for a in range(3):
                fill_sides(next_pad, a, halo, side_ref[a, 3 * which], size_y)
                fill_sides(next_pad, a, edge + 1, side_ref[a, 1 + which], size_y)
            beta = OMEGA * inverse(own[6, edge])
            ties = tie_rows(
                list_ref[which].astype(F32),
                got[ROW_STIFF : ROW_STIFF + size_y, :],
                [rows_of(next_pad, a, halo, size_y) for a in range(3)],
            )
            mechanic_end(near, next_pad, keep, out, size_y)
            mechanic_end(edge, next_pad, keep, out, size_y, [beta * w for w in ties])
            copy_out(which, first, 3).start()
        for item in work:
            copy_out(item[3], item[-1], 3).wait()


def call(kernel, name, out_shape, operands, spaces, scratch=(), out_spaces=None, aliases=(), weight=1):
    if out_spaces is None:
        out_spaces = [pltpu.VMEM] * len(out_shape)
    return pl.pallas_call(
        kernel,
        name=name,
        out_shape=tuple(out_shape),
        in_specs=[pl.BlockSpec(memory_space=space) for space in spaces],
        out_specs=tuple(pl.BlockSpec(memory_space=space) for space in out_spaces),
        scratch_shapes=scratch,
        input_output_aliases=dict(aliases),
        cost_estimate=pl.CostEstimate(
            flops=weight * COST[0], bytes_accessed=weight * COST[1], transcendentals=0
        ),
        compiler_params=pltpu.CompilerParams(vmem_limit_bytes=VMEM_LIMIT),
    )(*operands)


def local(sections, fiber_angles, fiber_class, row_map, interface_rows):
    own = sections[0]
    channels, size_x, size_y, depth = own.shape
    n_gx = lax.axis_size("gx")
    n_gy = lax.axis_size("gy")
    assert lax.axis_size("sec") == 2 and n_gy == 2
    upward = [(i, (i + 1) % n_gx) for i in range(n_gx)]
    downward = [(j, i) for i, j in upward]
    both = [(0, 1), (1, 0)]
    S, V, H = pltpu.SMEM, pltpu.VMEM, pltpu.HBM
    f32 = lambda *shape: jax.ShapeDtypeStruct(shape, F32)
    hbm = lambda w: pltpu.with_memory_space_constraint(w, H)
    columns = size_x * size_y
    padded = f32(3, size_x + 2, size_y + 2 * PAD, depth)
    classes = fiber_class.transpose(0, 2, 1)
    lists = interface_rows.reshape(2, 1, size_y)
    places = row_map.reshape(-1)

    field = lambda n: pltpu.VMEM((n, size_x, size_y, depth), F32)
    plain, edge_ten = call(
        tension_kernel,
        "tension",
        (f32(columns, depth), f32(2, size_y, depth)),
        (hbm(own), hbm(places)),
        (H, H),
        [
            field(3),
            field(1),
            field(2),
            pltpu.SMEM((columns,), jnp.int32),
            pltpu.SemaphoreType.DMA((1 + 3 * 4,)),
        ],
    )
    edge_ten = lax.ppermute(edge_ten, "sec", both)
    pad, share = call(share_kernel, "share", (padded, f32(3, size_x, 8, depth)), (own,), (V,))
    side = lax.ppermute(share, "gy", both)
    result = f32(1, 4, size_x, size_y, depth)
    tension, fib, result = call(
        gather_kernel,
        "gather",
        (f32(columns, depth), f32(3, columns, depth), result),
        (hbm(places), plain, classes, fiber_angles.T),
        (H, V, V, V),
        [
            pltpu.SMEM((columns,), jnp.int32),
            pltpu.VMEM((classes.shape[1], columns), jnp.int32),
            pltpu.SemaphoreType.DMA((1 + size_x,)),
        ],
        out_spaces=(V, V, H),
        weight=6,
    )
    tension = lax.ppermute(tension, "sec", both)
    message = f32(MESSAGE_ROWS, depth)
    high, low, pad = call(
        message_electric,
        "message_electric",
        (message, message, padded),
        (pad, own, side, fib, lists),
        (V,) * 5,
        aliases={0: 2},
    )
    high, low = call(
        message_mechanic,
        "message_mechanic",
        (message, message),
        (own, fib, edge_ten, high, low),
        (V,) * 5,
        aliases={3: 0, 4: 1},
    )
    got_low = lax.ppermute(high, "gx", upward)
    got_high = lax.ppermute(low, "gx", downward)
    moved, share, keep = call(
        inner_electric,
        "inner_electric",
        (padded, f32(3, size_x + 2, 8, depth), f32(4, size_x, size_y, depth)),
        (pad, own, fib),
        (V,) * 3,
        weight=6,
    )
    moved, share, keep = call(
        inner_mechanic,
        "inner_mechanic",
        (padded, f32(3, size_x + 2, 8, depth), f32(4, size_x, size_y, depth)),
        (pad, own, fib, tension, moved, share, keep),
        (V,) * 7,
        aliases={4: 0, 5: 1, 6: 2},
        weight=6,
    )
    side = lax.ppermute(share, "gy", both)
    moved, share = call(
        outer_kernel,
        "outer",
        (padded, f32(3, 4, 8, depth)),
        (pad, own, fib, lists, got_low, got_high, moved),
        (V,) * 7,
        [pltpu.VMEM((3, 2) + padded.shape[2:], F32)],
        aliases={6: 0},
    )
    end_side = lax.ppermute(share, "gy", both)
    fields = pltpu.VMEM((3, size_x, size_y, depth), F32)
    result, moved, held = call(
        middle_kernel,
        "middle",
        (f32(1, 4, size_x, size_y, depth), padded, f32(4, size_y, depth)),
        (fib, moved, side, keep, result),
        (V,) * 4 + (H,),
        [fields, pltpu.SemaphoreType.DMA((4,))],
        out_spaces=(H, V, V),
        aliases={1: 1, 4: 0},
        weight=6,
    )
    return call(
        last_kernel,
        "last",
        (f32(1, 4, size_x, size_y, depth), padded),
        (own, fib, lists, got_low, got_high, moved, end_side, keep, held, result),
        (V,) * 9 + (H,),
        [fields, pltpu.SemaphoreType.DMA((2,))],
        out_spaces=(H, V),
        aliases={5: 1, 9: 0},
    )[0]


def solution(mesh):
    in_specs = (
        P("sec", None, "gx", "gy", None),
        P(),
        P("gx", "gy", None),
        P("gx", "gy", None),
        P(None, "gx", "gy", None),
    )
    out_specs = P("sec", None, "gx", "gy", None)
    return jax.shard_map(local, mesh=mesh, in_specs=in_specs, out_specs=out_specs, check_vma=False)
```

```python
import jax
import jax.numpy as jnp
from jax import lax
from jax.experimental import pallas as pl
from jax.experimental.pallas import tpu as pltpu
from jax.sharding import PartitionSpec as P

DT = 0.1
OMEGA = 0.06
F32 = jnp.float32
HIGHEST = lax.Precision.HIGHEST
VMEM_LIMIT = 16 * 1024 * 1024
COST = {
    "tension": 0.001,
    "share": 0.001,
    "gather": 6,
    "message_electric": 1,
    "message_mechanic": 1,
    "inner_electric": 6,
    "inner_mechanic": 6,
    "outer_electric": 1,
    "outer_mechanic": 1,
    "middle": 6,
    "last": 1,
}

PAD = 8

ROW_NOW, ROW_NEXT, ROW_STIFF, ROW_SIDE = 0, 96, 192, 224
ROW_LIST = ROW_SIDE + 6
MESSAGE_ROWS = 232
ROW_VOLT, ROW_VOLT_NEXT, ROW_COUPLED, ROW_VOLT_SIDE = 0, 32, 64, 160
VOLT_ROWS = 168


def inverse(v):
    r = pl.reciprocal(v, approx=True)
    return r * (2.0 - v * r)


def rise(c):
    c2 = c * c
    return c2 * inverse(c2 + 0.25)


def ends(like):
    lane = lax.broadcasted_iota(jnp.int32, like, 1)
    return lane == like[1] - 1, lane == 0


def up_z(w, last):
    return jnp.where(last, 0.0, pltpu.roll(w, w.shape[1] - 1, 1))


def down_z(w, first):
    return jnp.where(first, 0.0, pltpu.roll(w, 1, 1))


def rows_of(pad, a, x, size_y, shift=0):
    return pad[a, x, PAD + shift : PAD + shift + size_y, :]


def motion_rate(pad, x, size_y):
    at = lambda a, dx=0, dy=0: rows_of(pad, a, x + dx, size_y, dy)
    u0, u1, u2 = at(0), at(1), at(2)
    last, first = ends(u0.shape)
    w0p, w0m, w1p, w1m = at(0, 1), at(0, -1), at(1, 1), at(1, -1)
    w2p, w2m = at(2, 1), at(2, -1)
    e0, e2 = 0.5 * (w0p - w0m), 0.5 * (w2p - w2m)
    e0y = (at(0, 1, 1) - at(0, -1, 1)) - (at(0, 1, -1) - at(0, -1, -1))
    e1y = (at(1, 1, 1) - at(1, -1, 1)) - (at(1, 1, -1) - at(1, -1, -1))
    v1p, v1m, v2p, v2m = at(1, 0, 1), at(1, 0, -1), at(2, 0, 1), at(2, 0, -1)
    d2 = 0.5 * (v2p - v2m)
    d1 = 0.5 * (v1p - v1m) + e0
    r0 = (
        up_z(u0 + e2, last) + down_z(u0 - e2, first)
        + (at(0, 0, 1) + at(0, 0, -1)) + 0.5 * e1y + 3.0 * (w0p + w0m)
    )
    r1 = (
        up_z(u1 + d2, last) + down_z(u1 - d2, first)
        + 3.0 * (v1p + v1m) + 0.5 * e0y + (w1p + w1m)
    )
    t2 = 3.0 * u2
    r2 = up_z(t2 + d1, last) + down_z(t2 - d1, first) + (v2p + v2m) + (w2p + w2m)
    return r0, r1, r2


def motion_from(pad, x, sign, size_y):
    u0, u1, u2 = [rows_of(pad, a, x, size_y) for a in range(3)]
    last, first = ends(u0.shape)
    half = 0.5 * sign
    dy0 = rows_of(pad, 0, x, size_y, 1) - rows_of(pad, 0, x, size_y, -1)
    dy1 = rows_of(pad, 1, x, size_y, 1) - rows_of(pad, 1, x, size_y, -1)
    dz0 = up_z(u0, last) - down_z(u0, first)
    dz2 = up_z(u2, last) - down_z(u2, first)
    return 3.0 * u0 + half * (dy1 + dz2), u1 + half * dy0, u2 + half * dz0


def volt_rate(pad, x, fib, size_y):
    at = lambda dx=0, dy=0: rows_of(pad, 0, x + dx, size_y, dy)
    v, wp, wm, yp, ym = at(), at(1), at(-1), at(0, 1), at(0, -1)
    last, first = ends(v.shape)
    e = wp - wm
    ey = (at(1, 1) - at(-1, 1)) - (at(1, -1) - at(-1, -1))
    dy = yp - ym
    sum_z = up_z(v, last) + down_z(v, first)
    ez = up_z(e, last) - down_z(e, first)
    dyz = up_z(dy, last) - down_z(dy, first)
    g = [0.75 * w for w in fib]
    d00, d11, d22 = [0.25 + a * b for a, b in zip(g, fib)]
    return (
        d00 * (wp + wm) + d11 * (yp + ym) + d22 * sum_z - 2.0 * (d00 + d11 + d22) * v
        + 0.5 * (fib[0] * (g[1] * ey + g[2] * ez) + g[1] * fib[2] * dyz)
    )


def couplings(fib):
    g = 0.75 * fib[0]
    return 0.25 + g * fib[0], 0.5 * g * fib[1], 0.5 * g * fib[2]


def volt_from(pad, x, coupled, sign, size_y):
    v = rows_of(pad, 0, x, size_y)
    last, first = ends(v.shape)
    dy = rows_of(pad, 0, x, size_y, 1) - rows_of(pad, 0, x, size_y, -1)
    dz = up_z(v, last) - down_z(v, first)
    return coupled[0] * v + sign * (coupled[1] * dy + coupled[2] * dz)


def currents(v, c, d, f, n, r):
    q = rise(c)
    calcium_flow = 1.2 * d * f * (v - 2.0)
    return q, calcium_flow, calcium_flow + (0.8 * n + 0.6 * q * r) * (v + 1.0) + 0.1 * v


def permute_rows(listed, values):
    rows = values.shape[0]
    pick = (lax.broadcasted_iota(jnp.int32, (rows, rows), 0).astype(F32) == listed).astype(F32)
    return lax.dot_general(
        pick, values, (((0,), (0,)), ((), ())), precision=HIGHEST, preferred_element_type=F32
    )


def tie_rows(listed, stiff, u):
    joined = jnp.concatenate([2.0 * stiff * w for w in u], axis=1)
    moved = permute_rows(listed, joined)
    depth = u[0].shape[1]
    return [moved[:, a * depth : (a + 1) * depth] for a in range(3)]


def edges_tile(value):
    rows = value.shape[0]
    last = lax.broadcasted_iota(jnp.int32, (8, value.shape[1]), 0) == 7
    return jnp.where(last, value[rows - 8 :], value[:8])


def fill_sides(pad, a, x, tile, size_y):
    pad[a, x, 0:PAD, :] = tile
    pad[a, x, PAD + size_y :, :] = tile


def sides(size_x):
    return (0, 0, -1.0), (size_x + 1, size_x - 1, 1.0)


def place_of(x, size_y):
    return pl.ds(pl.multiple_of(x * size_y, size_y), size_y)


def electric():
    return lax.axis_index("sec") == 0


def fiber_fields(angles, cls, flat, fib_ref, size_x, size_y):
    blocks, classes, depth = cls.shape[1], angles.shape[1], fib_ref.shape[2]
    azimuth, elevation = angles[0:1, :], angles[1:2, :]
    flat_part = jnp.cos(elevation)
    fib = [jnp.cos(azimuth) * flat_part, jnp.sin(azimuth) * flat_part, jnp.sin(elevation)]
    for x in range(size_x):
        flat[:, x * size_y : (x + 1) * size_y] = cls[x]
    own = lax.broadcasted_iota(jnp.int32, (blocks, depth), 1) // (depth // blocks)
    own = own == lax.broadcasted_iota(jnp.int32, (blocks, depth), 0)
    hits = jnp.concatenate([(flat[...] == k).astype(F32) for k in range(classes)], axis=0)
    table = jnp.concatenate(
        [
            jnp.concatenate(
                [jnp.where(own, jnp.broadcast_to(w[:, k : k + 1], own.shape), 0.0) for w in fib], axis=1
            )
            for k in range(classes)
        ],
        axis=0,
    )
    high = table.astype(jnp.bfloat16).astype(F32)
    mid = (table - high).astype(jnp.bfloat16).astype(F32)
    parts = jnp.concatenate([high, mid, table - high - mid], axis=0)
    found = lax.dot_general(
        jnp.concatenate([hits] * 3, axis=0), parts, (((0,), (0,)), ((), ())), preferred_element_type=F32
    )
    for a in range(3):
        fib_ref[a] = found[:, a * depth : (a + 1) * depth]


def tension_kernel(sec_hbm, map_hbm, plain, edge_ten, main, gate, late, map_ref, sems):
    size_x, size_y = sec_hbm.shape[1], sec_hbm.shape[2]
    pieces = (sems.shape[0] - 1) // 3
    chunk = size_x // pieces

    def plane(x, carry):
        v, c, d, f, bound, s = main[0, x], main[1, x], main[2, x], gate[0, x], late[0, x], late[1, x]
        calcium_flow = 1.2 * d * f * (v - 2.0)
        flow = 2.0 * c * (1.0 - bound) - 0.4 * bound
        c1 = c + DT * (-0.3 * calcium_flow - 0.5 * c - flow)
        s1 = s + (0.5 * DT) * (rise(c) - s)
        plain[place_of(x, size_y), :] = s1 + (0.5 * DT) * (rise(c1) - s1)
        return carry

    @pl.when(electric())
    def _():
        places = pltpu.make_async_copy(map_hbm, map_ref, sems.at[0])
        copies = []
        for i in range(pieces):
            here = pl.ds(i * chunk, chunk)
            copies.append(
                [
                    pltpu.make_async_copy(sec_hbm.at[src, here], dst.at[:, here], sems.at[1 + 3 * i + k])
                    for k, (src, dst) in enumerate(
                        ((pl.ds(0, 3), main), (pl.ds(3, 1), gate), (pl.ds(6, 2), late))
                    )
                ]
            )
            for copy in copies[-1]:
                copy.start()
        places.start()
        for i in range(pieces):
            for copy in copies[i]:
                copy.wait()
            lax.fori_loop(i * chunk, (i + 1) * chunk, plane, 0, unroll=2)
        places.wait()
        last = (size_x - 1) * size_y
        for p in range(size_y):
            edge_ten[0, p : p + 1, :] = plain[pl.ds(map_ref[p], 1), :]
            edge_ten[1, p : p + 1, :] = plain[pl.ds(map_ref[last + p], 1), :]


def share_kernel(own, after, pad, share):
    size_x, size_y = own.shape[1], own.shape[2]
    zeros = jnp.zeros(pad.shape[2:], F32)
    for a in range(3):
        pad[a, 0] = zeros
        pad[a, size_x + 1] = zeros

    def plane(x, carry):
        for a in range(3):
            value = own[a, x]
            pad[a, x + 1, PAD : PAD + size_y, :] = value
            share[a, x] = edges_tile(value)
        return carry

    lax.fori_loop(0, size_x, plane, 0, unroll=4)


def gather_kernel(map_hbm, plain, cls_ref, ang_ref, all_ref, fib_ref, out_hbm, map_ref, flat, sems):
    size_x = cls_ref.shape[0]
    size_y = all_ref.shape[0] // size_x
    places = pltpu.make_async_copy(map_hbm, map_ref, sems.at[0])
    copies = [
        pltpu.make_async_copy(plain.at[x * size_y : (x + 1) * size_y], out_hbm.at[0, 3, x], sems.at[1 + x])
        for x in range(size_x)
    ]

    @pl.when(electric())
    def _():
        places.start()
        for copy in copies:
            copy.start()

    fiber_fields(ang_ref[...], cls_ref, flat, fib_ref, size_x, size_y)

    @pl.when(electric())
    def _():
        places.wait()

        def rows(i, carry):
            for k in range(32):
                p = i * 32 + k
                all_ref[pl.ds(p, 1), :] = plain[pl.ds(map_ref[p], 1), :]
            return carry

        lax.fori_loop(0, all_ref.shape[0] // 32, rows, 0)
        for copy in copies:
            copy.wait()


def message_electric(pad_in, own, side_ref, fib_ref, high_ref, low_ref, pad):
    size_x, size_y = own.shape[1], own.shape[2]

    def fill(x, carry):
        for a in range(3):
            fill_sides(pad, a, x + 1, side_ref[a, x], size_y)
        return carry

    lax.fori_loop(0, size_x, fill, 0, unroll=4)

    @pl.when(electric())
    def _():
        for which, ((_, edge, _), out) in enumerate(zip(sides(size_x), (low_ref, high_ref))):
            out[ROW_VOLT_SIDE : ROW_VOLT_SIDE + 1, :] = side_ref[0, edge, 7:8, :]
            out[ROW_VOLT_SIDE + 1 : ROW_VOLT_SIDE + 2, :] = side_ref[0, edge, 0:1, :]
            fib = [fib_ref[a, place_of(edge, size_y), :] for a in range(3)]
            v, c, d = [rows_of(pad, a, edge + 1, size_y) for a in range(3)]
            f, n, r = [own[k, edge] for k in range(3, 6)]
            rate = volt_rate(pad, edge + 1, fib, size_y)
            _, _, total = currents(v, c, d, f, n, r)
            out[ROW_VOLT : ROW_VOLT + size_y, :] = v
            out[ROW_VOLT_NEXT : ROW_VOLT_NEXT + size_y, :] = v + DT * (rate - total)
            for k, value in enumerate(couplings(fib)):
                out[ROW_COUPLED + k * size_y : ROW_COUPLED + (k + 1) * size_y, :] = value

def message_mechanic(pad_in, own, side_ref, fib_ref, ten_ref, list_ref, high_ref, low_ref, pad):
    size_x, size_y = own.shape[1], own.shape[2]

    @pl.when(jnp.logical_not(electric()))
    def _():
        for which, ((_, edge, _), out) in enumerate(zip(sides(size_x), (low_ref, high_ref))):
            out[ROW_LIST : ROW_LIST + 1, 0:size_y] = list_ref[which].astype(F32)
            rate = motion_rate(pad, edge + 1, size_y)
            stiff = own[6, edge]
            beta = OMEGA * inverse(stiff)
            act = own[7, edge] * ten_ref[which]
            out[ROW_STIFF : ROW_STIFF + size_y, :] = stiff
            for a in range(3):
                row = ROW_SIDE + 2 * a
                out[row : row + 1, :] = side_ref[a, edge, 7:8, :]
                out[row + 1 : row + 2, :] = side_ref[a, edge, 0:1, :]
                u = rows_of(pad, a, edge + 1, size_y)
                out[ROW_NOW + a * size_y : ROW_NOW + (a + 1) * size_y, :] = u
                drive = own[3 + a, edge] + act * fib_ref[a, place_of(edge, size_y), :]
                out[ROW_NEXT + a * size_y : ROW_NEXT + (a + 1) * size_y, :] = (
                    0.28 * u + beta * drive + OMEGA * rate[a]
                )


def put_inner(next_pad, share, a, x, value):
    next_pad[a, x, PAD : PAD + value.shape[0], :] = value
    share[a, x] = edges_tile(value)


def inner_electric(pad, own, fib_ref, next_pad, share, keep):
    size_x, size_y = own.shape[1], own.shape[2]

    @pl.when(electric())
    def _():
        def plane(x, carry):
            place = place_of(x, size_y)
            v, c, d = [rows_of(pad, a, x + 1, size_y) for a in range(3)]
            f, n, r, bound, _ = [own[k, x] for k in range(3, 8)]
            rate = volt_rate(pad, x + 1, [fib_ref[a, place, :] for a in range(3)], size_y)
            q, calcium_flow, total = currents(v, c, d, f, n, r)
            flow = 2.0 * c * (1.0 - bound) - 0.4 * bound
            put_inner(next_pad, share, 0, x + 1, v + DT * (rate - total))
            c1 = c + DT * (-0.3 * calcium_flow - 0.5 * c - flow)
            tv = jnp.tanh(v)
            d1 = (1.0 - 2.0 * DT) * d + DT * (1.0 + jnp.tanh(v + 0.5))
            f1 = (1.0 - DT / 3.0) * f + (DT / 6.0) * (1.0 - tv)
            n1 = (1.0 - DT) * n + (0.5 * DT) * (1.0 + tv)
            r1 = (1.0 - DT / 5.0) * r + (DT / 10.0) * (1.0 + jnp.tanh(0.5 * v - 0.25))
            bound1 = bound + DT * flow
            flow1 = 2.0 * c1 * (1.0 - bound1) - 0.4 * bound1
            keep[0, x] = n1
            keep[1, x] = 1.2 * d1 * f1
            keep[2, x] = 0.8 * n1 + 0.6 * rise(c1) * r1
            keep[3, x] = c1 - DT * (0.5 * c1 + flow1)
            return carry

        lax.fori_loop(0, size_x, plane, 0, unroll=2)


def inner_mechanic(pad, own, fib_ref, ten_ref, next_in, share_in, keep_in, next_pad, share, keep):
    size_x, size_y = own.shape[1], own.shape[2]

    @pl.when(jnp.logical_not(electric()))
    def _():
        def plane(x, carry):
            place = place_of(x, size_y)
            rate = motion_rate(pad, x + 1, size_y)
            beta = OMEGA * inverse(own[6, x])
            act = own[7, x] * ten_ref[place, :]
            keep[3, x] = act
            for a in range(3):
                drive = beta * (own[3 + a, x] + act * fib_ref[a, place, :])
                keep[a, x] = drive
                value = 0.4 * rows_of(pad, a, x + 1, size_y) + drive + OMEGA * rate[a]
                put_inner(next_pad, share, a, x + 1, value)
            return carry

        lax.fori_loop(0, size_x, plane, 0, unroll=2)


def outer_electric(pad, own, fib_ref, volt_low, volt_high, next_in, next_pad, share, wide):
    size_x, size_y = own.shape[1], own.shape[2]
    def put(a, x, slot, value):
        next_pad[a, x, PAD : PAD + size_y, :] = value
        share[a, slot] = edges_tile(value)

    def put_side(a, which, low, high):
        wide[a, which, PAD - 1 : PAD, :] = low
        wide[a, which, PAD + size_y : PAD + size_y + 1, :] = high

    @pl.when(electric())
    def _():
        for which, ((halo, edge, sign), got) in enumerate(zip(sides(size_x), (volt_low, volt_high))):
            wide[0, which, PAD : PAD + size_y, :] = got[ROW_VOLT : ROW_VOLT + size_y, :]
            row = ROW_VOLT_SIDE
            put_side(0, which, got[row : row + 1, :], got[row + 1 : row + 2, :])
            fib = [fib_ref[a, place_of(edge, size_y), :] for a in range(3)]
            put(
                0,
                edge + 1,
                1 + which,
                rows_of(next_pad, 0, edge + 1, size_y) + DT * volt_from(wide, which, couplings(fib), sign, size_y),
            )
            theirs = [got[ROW_COUPLED + k * size_y : ROW_COUPLED + (k + 1) * size_y, :] for k in range(3)]
            put(
                0,
                halo,
                3 * which,
                got[ROW_VOLT_NEXT : ROW_VOLT_NEXT + size_y, :] + DT * volt_from(pad, edge + 1, theirs, -sign, size_y),
            )


def outer_mechanic(pad, own, list_ref, got_low, got_high, next_in, share_in, next_pad, share, wide):
    size_x, size_y = own.shape[1], own.shape[2]
    def put(a, x, slot, value):
        next_pad[a, x, PAD : PAD + size_y, :] = value
        share[a, slot] = edges_tile(value)

    def put_side(a, which, low, high):
        wide[a, which, PAD - 1 : PAD, :] = low
        wide[a, which, PAD + size_y : PAD + size_y + 1, :] = high

    @pl.when(jnp.logical_not(electric()))
    def _():
        for which, ((halo, edge, sign), got) in enumerate(zip(sides(size_x), (got_low, got_high))):
            for a in range(3):
                wide[a, which, PAD : PAD + size_y, :] = got[ROW_NOW + a * size_y : ROW_NOW + (a + 1) * size_y, :]
                row = ROW_SIDE + 2 * a
                put_side(a, which, got[row : row + 1, :], got[row + 1 : row + 2, :])
            stiff = got[ROW_STIFF : ROW_STIFF + size_y, :]
            stiff_own = own[6, edge]
            now = [rows_of(pad, a, edge + 1, size_y) for a in range(3)]
            theirs = [rows_of(wide, a, which, size_y) for a in range(3)]
            ties = tie_rows(list_ref[which].astype(F32), stiff, theirs)
            rate = motion_from(wide, which, sign, size_y)
            beta = OMEGA * inverse(stiff_own)
            for a in range(3):
                put(
                    a,
                    edge + 1,
                    1 + which,
                    rows_of(next_pad, a, edge + 1, size_y) + OMEGA * rate[a] + beta * ties[a] - 0.12 * now[a],
                )
            ties = tie_rows(got[ROW_LIST : ROW_LIST + 1, 0:size_y], stiff_own, now)
            rate = motion_from(pad, edge + 1, -sign, size_y)
            beta = OMEGA * inverse(stiff)
            for a in range(3):
                put(
                    a,
                    halo,
                    3 * which,
                    got[ROW_NEXT + a * size_y : ROW_NEXT + (a + 1) * size_y, :] + OMEGA * rate[a] + beta * ties[a],
                )


def electric_end(x, next_pad, fib_ref):
    size_y = next_pad.shape[2] - 2 * PAD
    place = place_of(x, size_y)
    return rows_of(next_pad, 0, x + 1, size_y) + DT * volt_rate(
        next_pad, x + 1, [fib_ref[a, place, :] for a in range(3)], size_y
    )


def electric_rest(x, next_pad, keep, out):
    size_y = next_pad.shape[2] - 2 * PAD
    v = rows_of(next_pad, 0, x + 1, size_y)
    n, gate, leak, rest_c = [keep[k, x] for k in range(4)]
    flow = gate * (v - 2.0)
    out[0, x] = -DT * (flow + leak * (v + 1.0) + 0.1 * v)
    out[1, x] = rest_c - (0.3 * DT) * flow
    out[2, x] = (1.0 - DT) * n + (0.5 * DT) * (1.0 + jnp.tanh(v))


def mechanic_end(x, next_pad, keep, out, size_y, ties=None):
    rate = motion_rate(next_pad, x + 1, size_y)
    for a in range(3):
        u = rows_of(next_pad, a, x + 1, size_y)
        value = 0.4 * u + keep[a, x] + OMEGA * rate[a]
        out[a, x] = value if ties is None else value + ties[a] - 0.12 * u


def middle_kernel(fib_ref, next_in, side_ref, keep, out_in, out_hbm, next_pad, held, out, sems):
    size_x = keep.shape[1]
    size_y = fib_ref.shape[1] // size_x
    pieces = sems.shape[0] - 1
    chunk = (size_x - 4) // pieces

    def copy_out(i, fields):
        here = pl.ds(2 + i * chunk, chunk)
        return pltpu.make_async_copy(out.at[0:fields, here], out_hbm.at[0, 0:fields, here], sems.at[i])

    def fill(count):
        def one(x, carry):
            for a in range(count):
                fill_sides(next_pad, a, x, side_ref[a, x], size_y)
            return carry

        lax.fori_loop(2, size_x, one, 0, unroll=2)

    @pl.when(electric())
    def _():
        fill(1)

        def rest(x, carry):
            electric_rest(x, next_pad, keep, out)
            return carry

        lax.fori_loop(0, size_x, rest, 0, unroll=2)
        copy = pltpu.make_async_copy(out.at[1:3], out_hbm.at[0, 1:3], sems.at[pieces])
        copy.start()
        for i, x in enumerate((0, 1, size_x - 2, size_x - 1)):
            held[i] = out[0, x]

        def step(i, carry):
            for k in range(chunk):
                x = 2 + i * chunk + k
                out[0, x] = out[0, x] + electric_end(x, next_pad, fib_ref)
            copy_out(i, 1).start()
            return carry

        lax.fori_loop(0, pieces, step, 0)
        copy.wait()
        for i in range(pieces):
            copy_out(i, 1).wait()

    @pl.when(jnp.logical_not(electric()))
    def _():
        fill(3)
        copy = pltpu.make_async_copy(keep.at[3:4], out_hbm.at[0, 3:4], sems.at[pieces])
        copy.start()

        def sweep(i, carry):
            for k in range(chunk):
                mechanic_end(2 + i * chunk + k, next_pad, keep, out, size_y)
            copy_out(i, 3).start()
            return carry

        lax.fori_loop(0, pieces, sweep, 0)
        copy.wait()
        for i in range(pieces):
            copy_out(i, 3).wait()


def last_kernel(
    own, fib_ref, list_ref, got_low, got_high, next_in, side_ref, keep, held, out_in, out_hbm, next_pad, out, sems
):
    size_x, size_y = own.shape[1], own.shape[2]

    def copy_out(which, first, fields):
        here = pl.ds(first, 2)
        return pltpu.make_async_copy(out.at[0:fields, here], out_hbm.at[0, 0:fields, here], sems.at[which])

    work = []
    for which, ((halo, edge, _), got) in enumerate(zip(sides(size_x), (got_low, got_high))):
        near = abs(edge - 1)
        work.append((halo, edge, near, which, got, min(edge, near)))

    @pl.when(electric())
    def _():
        for halo, edge, near, which, _, first in work:
            fill_sides(next_pad, 0, halo, side_ref[0, 3 * which], size_y)
            fill_sides(next_pad, 0, edge + 1, side_ref[0, 1 + which], size_y)
            for x in (near, edge):
                out[0, x] = held[2 * which + x - first] + electric_end(x, next_pad, fib_ref)
            copy_out(which, first, 1).start()
        for item in work:
            copy_out(item[3], item[-1], 1).wait()

    @pl.when(jnp.logical_not(electric()))
    def _():
        for halo, edge, near, which, got, first in work:
            for a in range(3):
                fill_sides(next_pad, a, halo, side_ref[a, 3 * which], size_y)
                fill_sides(next_pad, a, edge + 1, side_ref[a, 1 + which], size_y)
            beta = OMEGA * inverse(own[6, edge])
            ties = tie_rows(
                list_ref[which].astype(F32),
                got[ROW_STIFF : ROW_STIFF + size_y, :],
                [rows_of(next_pad, a, halo, size_y) for a in range(3)],
            )
            mechanic_end(near, next_pad, keep, out, size_y)
            mechanic_end(edge, next_pad, keep, out, size_y, [beta * w for w in ties])
            copy_out(which, first, 3).start()
        for item in work:
            copy_out(item[3], item[-1], 3).wait()


def call(kernel, name, out_shape, operands, spaces, scratch=(), out_spaces=None, aliases=()):
    if out_spaces is None:
        out_spaces = [pltpu.VMEM] * len(out_shape)
    return pl.pallas_call(
        kernel,
        name=name,
        out_shape=tuple(out_shape),
        in_specs=[pl.BlockSpec(memory_space=space) for space in spaces],
        out_specs=tuple(pl.BlockSpec(memory_space=space) for space in out_spaces),
        scratch_shapes=scratch,
        input_output_aliases=dict(aliases),
        cost_estimate=pl.CostEstimate(
            flops=int(COST[name] * 10**10), bytes_accessed=int(COST[name] * 10**7), transcendentals=0
        ),
        compiler_params=pltpu.CompilerParams(vmem_limit_bytes=VMEM_LIMIT),
    )(*operands)


def local(sections, fiber_angles, fiber_class, row_map, interface_rows):
    own = sections[0]
    channels, size_x, size_y, depth = own.shape
    n_gx = lax.axis_size("gx")
    n_gy = lax.axis_size("gy")
    assert lax.axis_size("sec") == 2 and n_gy == 2
    axes = ("sec", "gx", "gy")
    place = lambda sec, i, j: (sec * n_gx + i % n_gx) * n_gy + j
    blocks = [(i, j) for i in range(n_gx) for j in range(n_gy)]

    def ring(section, step):
        return [(place(section, i, j), place(section, i + step, j)) for i, j in blocks] + [
            (place(1 - section, i, j), place(1 - section, i, 1 - j)) for i, j in blocks
        ]

    both = [(0, 1), (1, 0)]
    S, V, H = pltpu.SMEM, pltpu.VMEM, pltpu.HBM
    f32 = lambda *shape: jax.ShapeDtypeStruct(shape, F32)
    hbm = lambda w: pltpu.with_memory_space_constraint(w, H)
    columns = size_x * size_y
    padded = f32(3, size_x + 2, size_y + 2 * PAD, depth)
    classes = fiber_class.transpose(0, 2, 1)
    lists = interface_rows.reshape(2, 1, size_y)
    places = row_map.reshape(-1)

    field = lambda n: pltpu.VMEM((n, size_x, size_y, depth), F32)
    plain, edge_ten = call(
        tension_kernel,
        "tension",
        (f32(columns, depth), f32(2, size_y, depth)),
        (hbm(own), hbm(places)),
        (H, H),
        [
            field(3),
            field(1),
            field(2),
            pltpu.SMEM((columns,), jnp.int32),
            pltpu.SemaphoreType.DMA((1 + 3 * 4,)),
        ],
    )
    edge_ten = lax.ppermute(edge_ten, "sec", both)
    pad, share = call(share_kernel, "share", (padded, f32(3, size_x, 8, depth)), (own, plain), (V, V))
    side = lax.ppermute(share, "gy", both)
    result = f32(1, 4, size_x, size_y, depth)
    tension, fib, result = call(
        gather_kernel,
        "gather",
        (f32(columns, depth), f32(3, columns, depth), result),
        (hbm(places), plain, classes, fiber_angles.T),
        (H, V, V, V),
        [
            pltpu.SMEM((columns,), jnp.int32),
            pltpu.VMEM((classes.shape[1], columns), jnp.int32),
            pltpu.SemaphoreType.DMA((1 + size_x,)),
        ],
        out_spaces=(V, V, H),
    )
    tension = lax.ppermute(tension, "sec", both)
    message = f32(VOLT_ROWS, depth)
    high, low, pad = call(
        message_electric,
        "message_electric",
        (message, message, padded),
        (pad, own, side, fib),
        (V,) * 4,
        aliases={0: 2},
    )
    volt_low = lax.ppermute(high, axes, ring(0, 1))
    volt_high = lax.ppermute(low, axes, ring(0, -1))
    message = f32(MESSAGE_ROWS, depth)
    high, low, pad = call(
        message_mechanic,
        "message_mechanic",
        (message, message, padded),
        (pad, own, side, fib, edge_ten, lists),
        (V,) * 6,
        aliases={0: 2},
    )
    got_low = lax.ppermute(high, axes, ring(1, 1))
    got_high = lax.ppermute(low, axes, ring(1, -1))
    moved, share, keep = call(
        inner_electric,
        "inner_electric",
        (padded, f32(3, size_x + 2, 8, depth), f32(4, size_x, size_y, depth)),
        (pad, own, fib),
        (V,) * 3,
    )
    moved, share, keep = call(
        inner_mechanic,
        "inner_mechanic",
        (padded, f32(3, size_x + 2, 8, depth), f32(4, size_x, size_y, depth)),
        (pad, own, fib, tension, moved, share, keep),
        (V,) * 7,
        aliases={4: 0, 5: 1, 6: 2},
    )
    side = lax.ppermute(share, "gy", both)
    wide = pltpu.VMEM((3, 2) + padded.shape[2:], F32)
    moved, share = call(
        outer_electric,
        "outer_electric",
        (padded, f32(3, 4, 8, depth)),
        (pad, own, fib, volt_low, volt_high, moved),
        (V,) * 6,
        [wide],
        aliases={5: 0},
    )
    moved, share = call(
        outer_mechanic,
        "outer_mechanic",
        (padded, f32(3, 4, 8, depth)),
        (pad, own, lists, got_low, got_high, moved, share),
        (V,) * 7,
        [wide],
        aliases={5: 0, 6: 1},
    )
    end_side = lax.ppermute(share, "gy", both)
    fields = pltpu.VMEM((3, size_x, size_y, depth), F32)
    result, moved, held = call(
        middle_kernel,
        "middle",
        (f32(1, 4, size_x, size_y, depth), padded, f32(4, size_y, depth)),
        (fib, moved, side, keep, result),
        (V,) * 4 + (H,),
        [fields, pltpu.SemaphoreType.DMA((4,))],
        out_spaces=(H, V, V),
        aliases={1: 1, 4: 0},
    )
    return call(
        last_kernel,
        "last",
        (f32(1, 4, size_x, size_y, depth), padded),
        (own, fib, lists, got_low, got_high, moved, end_side, keep, held, result),
        (V,) * 9 + (H,),
        [fields, pltpu.SemaphoreType.DMA((2,))],
        out_spaces=(H, V),
        aliases={5: 1, 9: 0},
    )[0]


def solution(mesh):
    in_specs = (
        P("sec", None, "gx", "gy", None),
        P(),
        P("gx", "gy", None),
        P("gx", "gy", None),
        P(None, "gx", "gy", None),
    )
    out_specs = P("sec", None, "gx", "gy", None)
    return jax.shard_map(local, mesh=mesh, in_specs=in_specs, out_specs=out_specs, check_vma=False)
```

```python
import jax
import jax.numpy as jnp
from jax import lax
from jax.experimental import pallas as pl
from jax.experimental.pallas import tpu as pltpu
from jax.sharding import PartitionSpec as P

DT = 0.1
OMEGA = 0.06
F32 = jnp.float32
VMEM_LIMIT = 16 * 1024 * 1024
COST = {
    "tension": 0.001,
    "share": 0.001,
    "gather": 6,
    "message_electric": 1,
    "message_mechanic": 1,
    "inner_electric": 6,
    "inner_mechanic": 6,
    "outer_electric": 1,
    "outer_mechanic": 1,
    "middle": 6,
    "last": 1,
}

CELLS = 16

PAD = 8

ROW_NOW, ROW_NEXT, ROW_STIFF, ROW_SIDE = 0, 96, 192, 224
ROW_LIST = ROW_SIDE + 6
MESSAGE_ROWS = 232
ROW_VOLT, ROW_VOLT_NEXT, ROW_COUPLED, ROW_VOLT_SIDE = 0, 32, 64, 160
VOLT_ROWS = 168


def inverse(v):
    r = pl.reciprocal(v, approx=True)
    return r * (2.0 - v * r)


def rise(c):
    c2 = c * c
    return c2 * inverse(c2 + 0.25)


def ends(like):
    lane = lax.broadcasted_iota(jnp.int32, like, 1)
    return lane == like[1] - 1, lane == 0


def up_z(w, last):
    return jnp.where(last, 0.0, pltpu.roll(w, w.shape[1] - 1, 1))


def down_z(w, first):
    return jnp.where(first, 0.0, pltpu.roll(w, 1, 1))


def rows_of(pad, a, x, size_y, shift=0):
    return pad[a, x, PAD + shift : PAD + shift + size_y, :]


def motion_rate(pad, x, size_y):
    at = lambda a, dx=0, dy=0: rows_of(pad, a, x + dx, size_y, dy)
    u0, u1, u2 = at(0), at(1), at(2)
    last, first = ends(u0.shape)
    w0p, w0m, w1p, w1m = at(0, 1), at(0, -1), at(1, 1), at(1, -1)
    w2p, w2m = at(2, 1), at(2, -1)
    e0, e2 = 0.5 * (w0p - w0m), 0.5 * (w2p - w2m)
    e0y = (at(0, 1, 1) - at(0, -1, 1)) - (at(0, 1, -1) - at(0, -1, -1))
    e1y = (at(1, 1, 1) - at(1, -1, 1)) - (at(1, 1, -1) - at(1, -1, -1))
    v1p, v1m, v2p, v2m = at(1, 0, 1), at(1, 0, -1), at(2, 0, 1), at(2, 0, -1)
    d2 = 0.5 * (v2p - v2m)
    d1 = 0.5 * (v1p - v1m) + e0
    r0 = (
        up_z(u0 + e2, last) + down_z(u0 - e2, first)
        + (at(0, 0, 1) + at(0, 0, -1)) + 0.5 * e1y + 3.0 * (w0p + w0m)
    )
    r1 = (
        up_z(u1 + d2, last) + down_z(u1 - d2, first)
        + 3.0 * (v1p + v1m) + 0.5 * e0y + (w1p + w1m)
    )
    t2 = 3.0 * u2
    r2 = up_z(t2 + d1, last) + down_z(t2 - d1, first) + (v2p + v2m) + (w2p + w2m)
    return r0, r1, r2


def motion_from(pad, x, sign, size_y):
    u0, u1, u2 = [rows_of(pad, a, x, size_y) for a in range(3)]
    last, first = ends(u0.shape)
    half = 0.5 * sign
    dy0 = rows_of(pad, 0, x, size_y, 1) - rows_of(pad, 0, x, size_y, -1)
    dy1 = rows_of(pad, 1, x, size_y, 1) - rows_of(pad, 1, x, size_y, -1)
    dz0 = up_z(u0, last) - down_z(u0, first)
    dz2 = up_z(u2, last) - down_z(u2, first)
    return 3.0 * u0 + half * (dy1 + dz2), u1 + half * dy0, u2 + half * dz0


def volt_rate(pad, x, fib, size_y):
    at = lambda dx=0, dy=0: rows_of(pad, 0, x + dx, size_y, dy)
    v, wp, wm, yp, ym = at(), at(1), at(-1), at(0, 1), at(0, -1)
    last, first = ends(v.shape)
    e = wp - wm
    ey = (at(1, 1) - at(-1, 1)) - (at(1, -1) - at(-1, -1))
    dy = yp - ym
    sum_z = up_z(v, last) + down_z(v, first)
    ez = up_z(e, last) - down_z(e, first)
    dyz = up_z(dy, last) - down_z(dy, first)
    g = [0.75 * w for w in fib]
    d00, d11, d22 = [0.25 + a * b for a, b in zip(g, fib)]
    return (
        d00 * (wp + wm) + d11 * (yp + ym) + d22 * sum_z - 2.0 * (d00 + d11 + d22) * v
        + 0.5 * (fib[0] * (g[1] * ey + g[2] * ez) + g[1] * fib[2] * dyz)
    )


def couplings(fib):
    g = 0.75 * fib[0]
    return 0.25 + g * fib[0], 0.5 * g * fib[1], 0.5 * g * fib[2]


def volt_from(pad, x, coupled, sign, size_y):
    v = rows_of(pad, 0, x, size_y)
    last, first = ends(v.shape)
    dy = rows_of(pad, 0, x, size_y, 1) - rows_of(pad, 0, x, size_y, -1)
    dz = up_z(v, last) - down_z(v, first)
    return coupled[0] * v + sign * (coupled[1] * dy + coupled[2] * dz)


def currents(v, c, d, f, n, r):
    q = rise(c)
    calcium_flow = 1.2 * d * f * (v - 2.0)
    return q, calcium_flow, calcium_flow + (0.8 * n + 0.6 * q * r) * (v + 1.0) + 0.1 * v


def in_three(values):
    high = values.astype(jnp.bfloat16).astype(F32)
    mid = (values - high).astype(jnp.bfloat16).astype(F32)
    return jnp.concatenate([high, mid, values - high - mid], axis=0)


def tie_rows(listed, stiff, u):
    rows, depth = u[0].shape
    joined = in_three(jnp.concatenate([2.0 * stiff * w for w in u], axis=1))
    pick = (lax.broadcasted_iota(jnp.int32, (rows, rows), 0).astype(F32) == listed).astype(F32)
    moved = lax.dot_general(
        jnp.concatenate([pick] * 3, axis=0), joined, (((0,), (0,)), ((), ())), preferred_element_type=F32
    )
    return [moved[:, a * depth : (a + 1) * depth] for a in range(3)]


def edges_tile(value):
    rows = value.shape[0]
    last = lax.broadcasted_iota(jnp.int32, (8, value.shape[1]), 0) == 7
    return jnp.where(last, value[rows - 8 :], value[:8])


def fill_sides(pad, a, x, tile, size_y):
    pad[a, x, 0:PAD, :] = tile
    pad[a, x, PAD + size_y :, :] = tile


def sides(size_x):
    return (0, 0, -1.0), (size_x + 1, size_x - 1, 1.0)


def place_of(x, size_y):
    return pl.ds(pl.multiple_of(x * size_y, size_y), size_y)


def electric():
    return lax.axis_index("sec") == 0


def fiber_fields(angles, cls):
    blocks, classes = cls.shape[0], angles.shape[1]
    depth = CELLS * blocks
    azimuth, elevation = angles[0:1, :], angles[1:2, :]
    flat_part = jnp.cos(elevation)
    fib = [jnp.cos(azimuth) * flat_part, jnp.sin(azimuth) * flat_part, jnp.sin(elevation)]
    own = lax.broadcasted_iota(jnp.int32, (blocks, depth), 1) // CELLS
    own = own == lax.broadcasted_iota(jnp.int32, (blocks, depth), 0)
    hits = jnp.concatenate([(cls == k).astype(F32) for k in range(classes)], axis=0)
    table = jnp.concatenate(
        [
            jnp.concatenate(
                [jnp.where(own, jnp.broadcast_to(w[:, k : k + 1], own.shape), 0.0) for w in fib], axis=1
            )
            for k in range(classes)
        ],
        axis=0,
    )
    return lax.dot_general(
        jnp.concatenate([hits] * 3, axis=0), in_three(table), (((0,), (0,)), ((), ())), preferred_element_type=F32
    )


def all_fibers(ang_ref, cls_ref, flat, fib_ref):
    size_x, _, size_y = cls_ref.shape
    depth = fib_ref.shape[2]
    for x in range(size_x):
        flat[:, x * size_y : (x + 1) * size_y] = cls_ref[x]
    found = fiber_fields(ang_ref[...], flat[...])
    for a in range(3):
        fib_ref[a] = found[:, a * depth : (a + 1) * depth]


def tension_kernel(sec_hbm, map_hbm, plain, edge_ten, main, gate, late, map_ref, sems):
    size_x, size_y = sec_hbm.shape[1], sec_hbm.shape[2]
    pieces = (sems.shape[0] - 1) // 3
    chunk = size_x // pieces

    def plane(x, carry):
        v, c, d, f, bound, s = main[0, x], main[1, x], main[2, x], gate[0, x], late[0, x], late[1, x]
        calcium_flow = 1.2 * d * f * (v - 2.0)
        flow = 2.0 * c * (1.0 - bound) - 0.4 * bound
        c1 = c + DT * (-0.3 * calcium_flow - 0.5 * c - flow)
        s1 = s + (0.5 * DT) * (rise(c) - s)
        plain[place_of(x, size_y), :] = s1 + (0.5 * DT) * (rise(c1) - s1)
        return carry

    @pl.when(electric())
    def _():
        places = pltpu.make_async_copy(map_hbm, map_ref, sems.at[0])
        copies = []
        for i in range(pieces):
            here = pl.ds(i * chunk, chunk)
            copies.append(
                [
                    pltpu.make_async_copy(sec_hbm.at[src, here], dst.at[:, here], sems.at[1 + 3 * i + k])
                    for k, (src, dst) in enumerate(
                        ((pl.ds(0, 3), main), (pl.ds(3, 1), gate), (pl.ds(6, 2), late))
                    )
                ]
            )
            for copy in copies[-1]:
                copy.start()
        places.start()
        for i in range(pieces):
            for copy in copies[i]:
                copy.wait()
            lax.fori_loop(i * chunk, (i + 1) * chunk, plane, 0, unroll=2)
        places.wait()
        last = (size_x - 1) * size_y
        for p in range(size_y):
            edge_ten[0, p : p + 1, :] = plain[pl.ds(map_ref[p], 1), :]
            edge_ten[1, p : p + 1, :] = plain[pl.ds(map_ref[last + p], 1), :]


def share_kernel(own, after, pad, share):
    size_x, size_y = own.shape[1], own.shape[2]
    zeros = jnp.zeros(pad.shape[2:], F32)
    for a in range(3):
        pad[a, 0] = zeros
        pad[a, size_x + 1] = zeros

    def plane(x, carry):
        for a in range(3):
            value = own[a, x]
            pad[a, x + 1, PAD : PAD + size_y, :] = value
            share[a, x] = edges_tile(value)
        return carry

    lax.fori_loop(0, size_x, plane, 0, unroll=4)


def gather_kernel(map_hbm, plain, all_ref, out_hbm, map_ref, sems):
    @pl.when(electric())
    def _():
        size_x, size_y = out_hbm.shape[2], out_hbm.shape[3]
        places = pltpu.make_async_copy(map_hbm, map_ref, sems.at[0])
        places.start()
        copies = [
            pltpu.make_async_copy(plain.at[x * size_y : (x + 1) * size_y], out_hbm.at[0, 3, x], sems.at[1 + x])
            for x in range(size_x)
        ]
        for copy in copies:
            copy.start()
        places.wait()

        def rows(i, carry):
            for k in range(32):
                p = i * 32 + k
                all_ref[pl.ds(p, 1), :] = plain[pl.ds(map_ref[p], 1), :]
            return carry

        lax.fori_loop(0, all_ref.shape[0] // 32, rows, 0)
        for copy in copies:
            copy.wait()


def message_electric(pad_in, own, side_ref, cls_ref, ang_ref, after, high_ref, low_ref, pad, fib_ref, flat):
    size_x, size_y = own.shape[1], own.shape[2]

    def fill(x, carry):
        for a in range(3):
            fill_sides(pad, a, x + 1, side_ref[a, x], size_y)
        return carry

    lax.fori_loop(0, size_x, fill, 0, unroll=4)

    @pl.when(electric())
    def _():
        all_fibers(ang_ref, cls_ref, flat, fib_ref)
        for which, ((_, edge, _), out) in enumerate(zip(sides(size_x), (low_ref, high_ref))):
            out[ROW_VOLT_SIDE : ROW_VOLT_SIDE + 1, :] = side_ref[0, edge, 7:8, :]
            out[ROW_VOLT_SIDE + 1 : ROW_VOLT_SIDE + 2, :] = side_ref[0, edge, 0:1, :]
            fib = [fib_ref[a, place_of(edge, size_y), :] for a in range(3)]
            v, c, d = [rows_of(pad, a, edge + 1, size_y) for a in range(3)]
            f, n, r = [own[k, edge] for k in range(3, 6)]
            rate = volt_rate(pad, edge + 1, fib, size_y)
            _, _, total = currents(v, c, d, f, n, r)
            out[ROW_VOLT : ROW_VOLT + size_y, :] = v
            out[ROW_VOLT_NEXT : ROW_VOLT_NEXT + size_y, :] = v + DT * (rate - total)
            for k, value in enumerate(couplings(fib)):
                out[ROW_COUPLED + k * size_y : ROW_COUPLED + (k + 1) * size_y, :] = value

def message_mechanic(
    pad_in, own, side_ref, cls_ref, ang_ref, ten_ref, list_ref, high_ref, low_ref, pad, flat
):
    size_x, size_y = own.shape[1], own.shape[2]

    @pl.when(jnp.logical_not(electric()))
    def _():
        depth = own.shape[3]
        for which, (_, edge, _) in enumerate(sides(size_x)):
            flat[:, which * size_y : (which + 1) * size_y] = cls_ref[edge]
        fibers = fiber_fields(ang_ref[...], flat[...])
        for which, ((_, edge, _), out) in enumerate(zip(sides(size_x), (low_ref, high_ref))):
            out[ROW_LIST : ROW_LIST + 1, 0:size_y] = list_ref[which].astype(F32)
            rate = motion_rate(pad, edge + 1, size_y)
            stiff = own[6, edge]
            beta = OMEGA * inverse(stiff)
            act = own[7, edge] * ten_ref[which]
            out[ROW_STIFF : ROW_STIFF + size_y, :] = stiff
            for a in range(3):
                row = ROW_SIDE + 2 * a
                out[row : row + 1, :] = side_ref[a, edge, 7:8, :]
                out[row + 1 : row + 2, :] = side_ref[a, edge, 0:1, :]
                u = rows_of(pad, a, edge + 1, size_y)
                out[ROW_NOW + a * size_y : ROW_NOW + (a + 1) * size_y, :] = u
                drive = own[3 + a, edge] + act * fibers[which * size_y : (which + 1) * size_y, a * depth : (a + 1) * depth]
                out[ROW_NEXT + a * size_y : ROW_NEXT + (a + 1) * size_y, :] = (
                    0.28 * u + beta * drive + OMEGA * rate[a]
                )


def put_inner(next_pad, share, a, x, value):
    next_pad[a, x, PAD : PAD + value.shape[0], :] = value
    share[a, x] = edges_tile(value)


def inner_electric(pad, own, fib_ref, next_pad, share, keep):
    size_x, size_y = own.shape[1], own.shape[2]

    @pl.when(electric())
    def _():
        def plane(x, carry):
            place = place_of(x, size_y)
            v, c, d = [rows_of(pad, a, x + 1, size_y) for a in range(3)]
            f, n, r, bound, _ = [own[k, x] for k in range(3, 8)]
            rate = volt_rate(pad, x + 1, [fib_ref[a, place, :] for a in range(3)], size_y)
            q, calcium_flow, total = currents(v, c, d, f, n, r)
            flow = 2.0 * c * (1.0 - bound) - 0.4 * bound
            put_inner(next_pad, share, 0, x + 1, v + DT * (rate - total))
            c1 = c + DT * (-0.3 * calcium_flow - 0.5 * c - flow)
            tv = jnp.tanh(v)
            d1 = (1.0 - 2.0 * DT) * d + DT * (1.0 + jnp.tanh(v + 0.5))
            f1 = (1.0 - DT / 3.0) * f + (DT / 6.0) * (1.0 - tv)
            n1 = (1.0 - DT) * n + (0.5 * DT) * (1.0 + tv)
            r1 = (1.0 - DT / 5.0) * r + (DT / 10.0) * (1.0 + jnp.tanh(0.5 * v - 0.25))
            bound1 = bound + DT * flow
            flow1 = 2.0 * c1 * (1.0 - bound1) - 0.4 * bound1
            keep[0, x] = n1
            keep[1, x] = 1.2 * d1 * f1
            keep[2, x] = 0.8 * n1 + 0.6 * rise(c1) * r1
            keep[3, x] = c1 - DT * (0.5 * c1 + flow1)
            return carry

        lax.fori_loop(0, size_x, plane, 0, unroll=2)


def inner_mechanic(
    pad, own, cls_ref, ang_ref, ten_ref, next_in, share_in, keep_in, next_pad, share, keep, fib_ref, flat
):
    size_x, size_y = own.shape[1], own.shape[2]

    @pl.when(jnp.logical_not(electric()))
    def _():
        all_fibers(ang_ref, cls_ref, flat, fib_ref)

        def plane(x, carry):
            place = place_of(x, size_y)
            rate = motion_rate(pad, x + 1, size_y)
            beta = OMEGA * inverse(own[6, x])
            act = own[7, x] * ten_ref[place, :]
            keep[3, x] = act
            for a in range(3):
                drive = beta * (own[3 + a, x] + act * fib_ref[a, place, :])
                keep[a, x] = drive
                value = 0.4 * rows_of(pad, a, x + 1, size_y) + drive + OMEGA * rate[a]
                put_inner(next_pad, share, a, x + 1, value)
            return carry

        lax.fori_loop(0, size_x, plane, 0, unroll=2)


def outer_electric(pad, own, fib_ref, volt_low, volt_high, next_in, next_pad, share, wide):
    size_x, size_y = own.shape[1], own.shape[2]
    def put(a, x, slot, value):
        next_pad[a, x, PAD : PAD + size_y, :] = value
        share[a, slot] = edges_tile(value)

    def put_side(a, which, low, high):
        wide[a, which, PAD - 1 : PAD, :] = low
        wide[a, which, PAD + size_y : PAD + size_y + 1, :] = high

    @pl.when(electric())
    def _():
        for which, ((halo, edge, sign), got) in enumerate(zip(sides(size_x), (volt_low, volt_high))):
            wide[0, which, PAD : PAD + size_y, :] = got[ROW_VOLT : ROW_VOLT + size_y, :]
            row = ROW_VOLT_SIDE
            put_side(0, which, got[row : row + 1, :], got[row + 1 : row + 2, :])
            fib = [fib_ref[a, place_of(edge, size_y), :] for a in range(3)]
            put(
                0,
                edge + 1,
                1 + which,
                rows_of(next_pad, 0, edge + 1, size_y) + DT * volt_from(wide, which, couplings(fib), sign, size_y),
            )
            theirs = [got[ROW_COUPLED + k * size_y : ROW_COUPLED + (k + 1) * size_y, :] for k in range(3)]
            put(
                0,
                halo,
                3 * which,
                got[ROW_VOLT_NEXT : ROW_VOLT_NEXT + size_y, :] + DT * volt_from(pad, edge + 1, theirs, -sign, size_y),
            )


def outer_mechanic(pad, own, list_ref, got_low, got_high, next_in, share_in, next_pad, share, wide):
    size_x, size_y = own.shape[1], own.shape[2]
    def put(a, x, slot, value):
        next_pad[a, x, PAD : PAD + size_y, :] = value
        share[a, slot] = edges_tile(value)

    def put_side(a, which, low, high):
        wide[a, which, PAD - 1 : PAD, :] = low
        wide[a, which, PAD + size_y : PAD + size_y + 1, :] = high

    @pl.when(jnp.logical_not(electric()))
    def _():
        for which, ((halo, edge, sign), got) in enumerate(zip(sides(size_x), (got_low, got_high))):
            for a in range(3):
                wide[a, which, PAD : PAD + size_y, :] = got[ROW_NOW + a * size_y : ROW_NOW + (a + 1) * size_y, :]
                row = ROW_SIDE + 2 * a
                put_side(a, which, got[row : row + 1, :], got[row + 1 : row + 2, :])
            stiff = got[ROW_STIFF : ROW_STIFF + size_y, :]
            stiff_own = own[6, edge]
            now = [rows_of(pad, a, edge + 1, size_y) for a in range(3)]
            theirs = [rows_of(wide, a, which, size_y) for a in range(3)]
            ties = tie_rows(list_ref[which].astype(F32), stiff, theirs)
            rate = motion_from(wide, which, sign, size_y)
            beta = OMEGA * inverse(stiff_own)
            for a in range(3):
                put(
                    a,
                    edge + 1,
                    1 + which,
                    rows_of(next_pad, a, edge + 1, size_y) + OMEGA * rate[a] + beta * ties[a] - 0.12 * now[a],
                )
            ties = tie_rows(got[ROW_LIST : ROW_LIST + 1, 0:size_y], stiff_own, now)
            rate = motion_from(pad, edge + 1, -sign, size_y)
            beta = OMEGA * inverse(stiff)
            for a in range(3):
                put(
                    a,
                    halo,
                    3 * which,
                    got[ROW_NEXT + a * size_y : ROW_NEXT + (a + 1) * size_y, :] + OMEGA * rate[a] + beta * ties[a],
                )


def electric_end(x, next_pad, fib_ref):
    size_y = next_pad.shape[2] - 2 * PAD
    place = place_of(x, size_y)
    return rows_of(next_pad, 0, x + 1, size_y) + DT * volt_rate(
        next_pad, x + 1, [fib_ref[a, place, :] for a in range(3)], size_y
    )


def electric_rest(x, next_pad, keep, out):
    size_y = next_pad.shape[2] - 2 * PAD
    v = rows_of(next_pad, 0, x + 1, size_y)
    n, gate, leak, rest_c = [keep[k, x] for k in range(4)]
    flow = gate * (v - 2.0)
    out[0, x] = -DT * (flow + leak * (v + 1.0) + 0.1 * v)
    out[1, x] = rest_c - (0.3 * DT) * flow
    out[2, x] = (1.0 - DT) * n + (0.5 * DT) * (1.0 + jnp.tanh(v))


def mechanic_end(x, next_pad, keep, out, size_y, ties=None):
    rate = motion_rate(next_pad, x + 1, size_y)
    for a in range(3):
        u = rows_of(next_pad, a, x + 1, size_y)
        value = 0.4 * u + keep[a, x] + OMEGA * rate[a]
        out[a, x] = value if ties is None else value + ties[a]


def middle_kernel(
    fib_ref, own, list_ref, got_low, got_high, next_in, side_ref, keep, out_in, out_hbm, next_pad, held, out, sems
):
    size_x = keep.shape[1]
    size_y = fib_ref.shape[1] // size_x
    pieces = sems.shape[0] - 1
    chunk = (size_x - 4) // pieces

    def copy_out(i, fields):
        here = pl.ds(2 + i * chunk, chunk)
        return pltpu.make_async_copy(out.at[0:fields, here], out_hbm.at[0, 0:fields, here], sems.at[i])

    def fill(count):
        def one(x, carry):
            for a in range(count):
                fill_sides(next_pad, a, x, side_ref[a, x], size_y)
            return carry

        lax.fori_loop(2, size_x, one, 0, unroll=2)

    @pl.when(electric())
    def _():
        fill(1)

        def rest(x, carry):
            electric_rest(x, next_pad, keep, out)
            return carry

        lax.fori_loop(0, size_x, rest, 0, unroll=2)
        copy = pltpu.make_async_copy(out.at[1:3], out_hbm.at[0, 1:3], sems.at[pieces])
        copy.start()
        for i, x in enumerate((0, 1, size_x - 2, size_x - 1)):
            held[i] = out[0, x]

        def step(i, carry):
            for k in range(chunk):
                x = 2 + i * chunk + k
                out[0, x] = out[0, x] + electric_end(x, next_pad, fib_ref)
            copy_out(i, 1).start()
            return carry

        lax.fori_loop(0, pieces, step, 0)
        copy.wait()
        for i in range(pieces):
            copy_out(i, 1).wait()

    @pl.when(jnp.logical_not(electric()))
    def _():
        fill(3)
        copy = pltpu.make_async_copy(keep.at[3:4], out_hbm.at[0, 3:4], sems.at[pieces])
        copy.start()

        def sweep(i, carry):
            for k in range(chunk):
                mechanic_end(2 + i * chunk + k, next_pad, keep, out, size_y)
            copy_out(i, 3).start()
            return carry

        lax.fori_loop(0, pieces, sweep, 0)
        for which, ((halo, edge, _), got) in enumerate(zip(sides(size_x), (got_low, got_high))):
            beta = OMEGA * inverse(own[6, edge])
            ties = tie_rows(
                list_ref[which].astype(F32),
                got[ROW_STIFF : ROW_STIFF + size_y, :],
                [rows_of(next_pad, a, halo, size_y) for a in range(3)],
            )
            for a in range(3):
                held[3 * which + a] = beta * ties[a] - 0.12 * rows_of(next_pad, a, edge + 1, size_y)
        copy.wait()
        for i in range(pieces):
            copy_out(i, 3).wait()


def last_kernel(
    fib_ref, next_in, side_ref, keep, held, out_in, out_hbm, next_pad, out, sems
):
    size_x = keep.shape[1]
    size_y = fib_ref.shape[1] // size_x

    def copy_out(which, first, fields):
        here = pl.ds(first, 2)
        return pltpu.make_async_copy(out.at[0:fields, here], out_hbm.at[0, 0:fields, here], sems.at[which])

    work = []
    for which, (halo, edge, _) in enumerate(sides(size_x)):
        near = abs(edge - 1)
        work.append((halo, edge, near, which, min(edge, near)))

    @pl.when(electric())
    def _():
        for halo, edge, near, which, first in work:
            fill_sides(next_pad, 0, halo, side_ref[0, 3 * which], size_y)
            fill_sides(next_pad, 0, edge + 1, side_ref[0, 1 + which], size_y)
            for x in (near, edge):
                out[0, x] = held[2 * which + x - first] + electric_end(x, next_pad, fib_ref)
            copy_out(which, first, 1).start()
        for item in work:
            copy_out(item[3], item[-1], 1).wait()

    @pl.when(jnp.logical_not(electric()))
    def _():
        for halo, edge, near, which, first in work:
            for a in range(3):
                fill_sides(next_pad, a, halo, side_ref[a, 3 * which], size_y)
                fill_sides(next_pad, a, edge + 1, side_ref[a, 1 + which], size_y)
            mechanic_end(near, next_pad, keep, out, size_y)
            mechanic_end(edge, next_pad, keep, out, size_y, [held[3 * which + a] for a in range(3)])
            copy_out(which, first, 3).start()
        for item in work:
            copy_out(item[3], item[-1], 3).wait()


def call(kernel, name, out_shape, operands, spaces, scratch=(), out_spaces=None, aliases=()):
    if out_spaces is None:
        out_spaces = [pltpu.VMEM] * len(out_shape)
    return pl.pallas_call(
        kernel,
        name=name,
        out_shape=tuple(out_shape),
        in_specs=[pl.BlockSpec(memory_space=space) for space in spaces],
        out_specs=tuple(pl.BlockSpec(memory_space=space) for space in out_spaces),
        scratch_shapes=scratch,
        input_output_aliases=dict(aliases),
        cost_estimate=pl.CostEstimate(
            flops=int(COST[name] * 10**10), bytes_accessed=int(COST[name] * 10**7), transcendentals=0
        ),
        compiler_params=pltpu.CompilerParams(vmem_limit_bytes=VMEM_LIMIT),
    )(*operands)


def local(sections, fiber_angles, fiber_class, row_map, interface_rows):
    own = sections[0]
    channels, size_x, size_y, depth = own.shape
    n_gx = lax.axis_size("gx")
    n_gy = lax.axis_size("gy")
    assert lax.axis_size("sec") == 2 and n_gy == 2
    axes = ("sec", "gx", "gy")
    place = lambda sec, i, j: (sec * n_gx + i % n_gx) * n_gy + j
    blocks = [(i, j) for i in range(n_gx) for j in range(n_gy)]

    def ring(section, step):
        return [(place(section, i, j), place(section, i + step, j)) for i, j in blocks] + [
            (place(1 - section, i, j), place(1 - section, i, 1 - j)) for i, j in blocks
        ]

    both = [(0, 1), (1, 0)]
    S, V, H = pltpu.SMEM, pltpu.VMEM, pltpu.HBM
    f32 = lambda *shape: jax.ShapeDtypeStruct(shape, F32)
    hbm = lambda w: pltpu.with_memory_space_constraint(w, H)
    columns = size_x * size_y
    padded = f32(3, size_x + 2, size_y + 2 * PAD, depth)
    classes = fiber_class.transpose(0, 2, 1)
    lists = interface_rows.reshape(2, 1, size_y)
    places = row_map.reshape(-1)

    field = lambda n: pltpu.VMEM((n, size_x, size_y, depth), F32)
    plain, edge_ten = call(
        tension_kernel,
        "tension",
        (f32(columns, depth), f32(2, size_y, depth)),
        (hbm(own), hbm(places)),
        (H, H),
        [
            field(3),
            field(1),
            field(2),
            pltpu.SMEM((columns,), jnp.int32),
            pltpu.SemaphoreType.DMA((1 + 3 * 4,)),
        ],
    )
    edge_ten = lax.ppermute(edge_ten, "sec", both)
    pad, share = call(share_kernel, "share", (padded, f32(3, size_x, 8, depth)), (own, plain), (V, V))
    side = lax.ppermute(share, "gy", both)
    result = f32(1, 4, size_x, size_y, depth)
    gathered, result = call(
        gather_kernel,
        "gather",
        (f32(columns, depth), result),
        (hbm(places), plain),
        (H, V),
        [pltpu.SMEM((columns,), jnp.int32), pltpu.SemaphoreType.DMA((1 + size_x,))],
        out_spaces=(V, H),
    )
    tension = lax.ppermute(gathered, "sec", both)
    assert depth == CELLS * classes.shape[1]
    angles = fiber_angles.T
    flat = lambda count: pltpu.VMEM((classes.shape[1], count), jnp.int32)
    message = f32(VOLT_ROWS, depth)
    high, low, pad, fib = call(
        message_electric,
        "message_electric",
        (message, message, padded, f32(3, columns, depth)),
        (pad, own, side, classes, angles, gathered),
        (V,) * 6,
        [flat(columns)],
        aliases={0: 2},
    )
    volt_low = lax.ppermute(high, axes, ring(0, 1))
    volt_high = lax.ppermute(low, axes, ring(0, -1))
    message = f32(MESSAGE_ROWS, depth)
    high, low, pad = call(
        message_mechanic,
        "message_mechanic",
        (message, message, padded),
        (pad, own, side, classes, angles, edge_ten, lists),
        (V,) * 7,
        [flat(2 * size_y)],
        aliases={0: 2},
    )
    got_low = lax.ppermute(high, axes, ring(1, 1))
    got_high = lax.ppermute(low, axes, ring(1, -1))
    moved, share, keep = call(
        inner_electric,
        "inner_electric",
        (padded, f32(3, size_x + 2, 8, depth), f32(4, size_x, size_y, depth)),
        (pad, own, fib),
        (V,) * 3,
    )
    moved, share, keep = call(
        inner_mechanic,
        "inner_mechanic",
        (padded, f32(3, size_x + 2, 8, depth), f32(4, size_x, size_y, depth)),
        (pad, own, classes, angles, tension, moved, share, keep),
        (V,) * 8,
        [pltpu.VMEM((3, columns, depth), F32), flat(columns)],
        aliases={5: 0, 6: 1, 7: 2},
    )
    side = lax.ppermute(share, "gy", both)
    wide = pltpu.VMEM((3, 2) + padded.shape[2:], F32)
    moved, share = call(
        outer_electric,
        "outer_electric",
        (padded, f32(3, 4, 8, depth)),
        (pad, own, fib, volt_low, volt_high, moved),
        (V,) * 6,
        [wide],
        aliases={5: 0},
    )
    moved, share = call(
        outer_mechanic,
        "outer_mechanic",
        (padded, f32(3, 4, 8, depth)),
        (pad, own, lists, got_low, got_high, moved, share),
        (V,) * 7,
        [wide],
        aliases={5: 0, 6: 1},
    )
    end_side = lax.ppermute(share, "gy", both)
    fields = pltpu.VMEM((3, size_x, size_y, depth), F32)
    result, moved, held = call(
        middle_kernel,
        "middle",
        (f32(1, 4, size_x, size_y, depth), padded, f32(6, size_y, depth)),
        (fib, own, lists, got_low, got_high, moved, side, keep, result),
        (V,) * 8 + (H,),
        [fields, pltpu.SemaphoreType.DMA((4,))],
        out_spaces=(H, V, V),
        aliases={5: 1, 8: 0},
    )
    return call(
        last_kernel,
        "last",
        (f32(1, 4, size_x, size_y, depth), padded),
        (fib, moved, end_side, keep, held, result),
        (V,) * 5 + (H,),
        [fields, pltpu.SemaphoreType.DMA((2,))],
        out_spaces=(H, V),
        aliases={1: 1, 5: 0},
    )[0]


def solution(mesh):
    in_specs = (
        P("sec", None, "gx", "gy", None),
        P(),
        P("gx", "gy", None),
        P("gx", "gy", None),
        P(None, "gx", "gy", None),
    )
    out_specs = P("sec", None, "gx", "gy", None)
    return jax.shard_map(local, mesh=mesh, in_specs=in_specs, out_specs=out_specs, check_vma=False)
```

```python
import jax
import jax.numpy as jnp
from jax import lax
from jax.experimental import pallas as pl
from jax.experimental.pallas import tpu as pltpu
from jax.sharding import PartitionSpec as P

DT = 0.1
OMEGA = 0.06
F32 = jnp.float32
VMEM_LIMIT = 16 * 1024 * 1024
COST = {
    "tension": 0.001,
    "share": 0.001,
    "gather": 6,
    "message_electric": 1,
    "message_mechanic": 1,
    "inner_electric": 6,
    "inner_mechanic": 6,
    "outer_electric": 1,
    "outer_mechanic": 1,
    "middle": 6,
    "last": 1,
}

CELLS = 16

PAD = 8

ROW_NOW, ROW_NEXT, ROW_STIFF, ROW_SIDE = 0, 96, 192, 224
ROW_LIST = ROW_SIDE + 6
MESSAGE_ROWS = 232
ROW_VOLT, ROW_VOLT_NEXT, ROW_COUPLED, ROW_VOLT_SIDE = 0, 32, 64, 160
VOLT_ROWS = 168


def inverse(v):
    r = pl.reciprocal(v, approx=True)
    return r * (2.0 - v * r)


def rise(c):
    c2 = c * c
    return c2 * inverse(c2 + 0.25)


def ends(like):
    lane = lax.broadcasted_iota(jnp.int32, like, 1)
    return lane == like[1] - 1, lane == 0


def up_z(w, last):
    return jnp.where(last, 0.0, pltpu.roll(w, w.shape[1] - 1, 1))


def down_z(w, first):
    return jnp.where(first, 0.0, pltpu.roll(w, 1, 1))


def rows_of(pad, a, x, size_y, shift=0):
    return pad[a, x, PAD + shift : PAD + shift + size_y, :]


def motion_rate(pad, x, size_y):
    at = lambda a, dx=0, dy=0: rows_of(pad, a, x + dx, size_y, dy)
    u0, u1, u2 = at(0), at(1), at(2)
    last, first = ends(u0.shape)
    w0p, w0m, w1p, w1m = at(0, 1), at(0, -1), at(1, 1), at(1, -1)
    w2p, w2m = at(2, 1), at(2, -1)
    e0, e2 = 0.5 * (w0p - w0m), 0.5 * (w2p - w2m)
    e0y = (at(0, 1, 1) - at(0, -1, 1)) - (at(0, 1, -1) - at(0, -1, -1))
    e1y = (at(1, 1, 1) - at(1, -1, 1)) - (at(1, 1, -1) - at(1, -1, -1))
    v1p, v1m, v2p, v2m = at(1, 0, 1), at(1, 0, -1), at(2, 0, 1), at(2, 0, -1)
    d2 = 0.5 * (v2p - v2m)
    d1 = 0.5 * (v1p - v1m) + e0
    r0 = (
        up_z(u0 + e2, last) + down_z(u0 - e2, first)
        + (at(0, 0, 1) + at(0, 0, -1)) + 0.5 * e1y + 3.0 * (w0p + w0m)
    )
    r1 = (
        up_z(u1 + d2, last) + down_z(u1 - d2, first)
        + 3.0 * (v1p + v1m) + 0.5 * e0y + (w1p + w1m)
    )
    t2 = 3.0 * u2
    r2 = up_z(t2 + d1, last) + down_z(t2 - d1, first) + (v2p + v2m) + (w2p + w2m)
    return r0, r1, r2


def motion_from(pad, x, sign, size_y):
    u0, u1, u2 = [rows_of(pad, a, x, size_y) for a in range(3)]
    last, first = ends(u0.shape)
    half = 0.5 * sign
    dy0 = rows_of(pad, 0, x, size_y, 1) - rows_of(pad, 0, x, size_y, -1)
    dy1 = rows_of(pad, 1, x, size_y, 1) - rows_of(pad, 1, x, size_y, -1)
    dz0 = up_z(u0, last) - down_z(u0, first)
    dz2 = up_z(u2, last) - down_z(u2, first)
    return 3.0 * u0 + half * (dy1 + dz2), u1 + half * dy0, u2 + half * dz0


def volt_rate(pad, x, fib, size_y):
    at = lambda dx=0, dy=0: rows_of(pad, 0, x + dx, size_y, dy)
    v, wp, wm, yp, ym = at(), at(1), at(-1), at(0, 1), at(0, -1)
    last, first = ends(v.shape)
    e = wp - wm
    ey = (at(1, 1) - at(-1, 1)) - (at(1, -1) - at(-1, -1))
    dy = yp - ym
    sum_z = up_z(v, last) + down_z(v, first)
    ez = up_z(e, last) - down_z(e, first)
    dyz = up_z(dy, last) - down_z(dy, first)
    g = [0.75 * w for w in fib]
    d00, d11, d22 = [0.25 + a * b for a, b in zip(g, fib)]
    return (
        d00 * (wp + wm) + d11 * (yp + ym) + d22 * sum_z - 2.0 * (d00 + d11 + d22) * v
        + 0.5 * (fib[0] * (g[1] * ey + g[2] * ez) + g[1] * fib[2] * dyz)
    )


def couplings(fib):
    g = 0.75 * fib[0]
    return 0.25 + g * fib[0], 0.5 * g * fib[1], 0.5 * g * fib[2]


def volt_from(pad, x, coupled, sign, size_y):
    v = rows_of(pad, 0, x, size_y)
    last, first = ends(v.shape)
    dy = rows_of(pad, 0, x, size_y, 1) - rows_of(pad, 0, x, size_y, -1)
    dz = up_z(v, last) - down_z(v, first)
    return coupled[0] * v + sign * (coupled[1] * dy + coupled[2] * dz)


def currents(v, c, d, f, n, r):
    q = rise(c)
    calcium_flow = 1.2 * d * f * (v - 2.0)
    return q, calcium_flow, calcium_flow + (0.8 * n + 0.6 * q * r) * (v + 1.0) + 0.1 * v


def in_three(values):
    high = values.astype(jnp.bfloat16).astype(F32)
    mid = (values - high).astype(jnp.bfloat16).astype(F32)
    return jnp.concatenate([high, mid, values - high - mid], axis=0)


def tie_rows(listed, stiff, u):
    rows, depth = u[0].shape
    joined = in_three(jnp.concatenate([2.0 * stiff * w for w in u], axis=1))
    pick = (lax.broadcasted_iota(jnp.int32, (rows, rows), 0).astype(F32) == listed).astype(F32)
    moved = lax.dot_general(
        jnp.concatenate([pick] * 3, axis=0), joined, (((0,), (0,)), ((), ())), preferred_element_type=F32
    )
    return [moved[:, a * depth : (a + 1) * depth] for a in range(3)]


def edges_tile(value):
    rows = value.shape[0]
    last = lax.broadcasted_iota(jnp.int32, (8, value.shape[1]), 0) == 7
    return jnp.where(last, value[rows - 8 :], value[:8])


def fill_sides(pad, a, x, tile, size_y):
    pad[a, x, 0:PAD, :] = tile
    pad[a, x, PAD + size_y :, :] = tile


def sides(size_x):
    return (0, 0, -1.0), (size_x + 1, size_x - 1, 1.0)


def place_of(x, size_y):
    return pl.ds(pl.multiple_of(x * size_y, size_y), size_y)


def electric():
    return lax.axis_index("sec") == 0


def fiber_fields(angles, cls):
    blocks, classes = cls.shape[0], angles.shape[1]
    depth = CELLS * blocks
    azimuth, elevation = angles[0:1, :], angles[1:2, :]
    flat_part = jnp.cos(elevation)
    fib = [jnp.cos(azimuth) * flat_part, jnp.sin(azimuth) * flat_part, jnp.sin(elevation)]
    own = lax.broadcasted_iota(jnp.int32, (blocks, depth), 1) // CELLS
    own = own == lax.broadcasted_iota(jnp.int32, (blocks, depth), 0)
    hits = jnp.concatenate([(cls == k).astype(F32) for k in range(classes)], axis=0)
    table = jnp.concatenate(
        [
            jnp.concatenate(
                [jnp.where(own, jnp.broadcast_to(w[:, k : k + 1], own.shape), 0.0) for w in fib], axis=1
            )
            for k in range(classes)
        ],
        axis=0,
    )
    return lax.dot_general(
        jnp.concatenate([hits] * 3, axis=0), in_three(table), (((0,), (0,)), ((), ())), preferred_element_type=F32
    )


def all_fibers(ang_ref, cls_ref, flat, fib_ref):
    size_x, _, size_y = cls_ref.shape
    depth = fib_ref.shape[2]
    for x in range(size_x):
        flat[:, x * size_y : (x + 1) * size_y] = cls_ref[x]
    found = fiber_fields(ang_ref[...], flat[...])
    for a in range(3):
        fib_ref[a] = found[:, a * depth : (a + 1) * depth]


def tension_kernel(
    sec_hbm, map_hbm, list_hbm, plain, edge_ten, list_ref, main, gate, late, map_ref, sems
):
    size_x, size_y = sec_hbm.shape[1], sec_hbm.shape[2]
    pieces = (sems.shape[0] - 2) // 3
    chunk = size_x // pieces

    def plane(x, carry):
        v, c, d, f, bound, s = main[0, x], main[1, x], main[2, x], gate[0, x], late[0, x], late[1, x]
        calcium_flow = 1.2 * d * f * (v - 2.0)
        flow = 2.0 * c * (1.0 - bound) - 0.4 * bound
        c1 = c + DT * (-0.3 * calcium_flow - 0.5 * c - flow)
        s1 = s + (0.5 * DT) * (rise(c) - s)
        plain[place_of(x, size_y), :] = s1 + (0.5 * DT) * (rise(c1) - s1)
        return carry

    @pl.when(electric())
    def _():
        small = [
            pltpu.make_async_copy(src, dst, sems.at[i])
            for i, (src, dst) in enumerate(((map_hbm, map_ref), (list_hbm, list_ref)))
        ]
        copies = []
        for i in range(pieces):
            here = pl.ds(i * chunk, chunk)
            copies.append(
                [
                    pltpu.make_async_copy(sec_hbm.at[src, here], dst.at[:, here], sems.at[2 + 3 * i + k])
                    for k, (src, dst) in enumerate(
                        ((pl.ds(0, 3), main), (pl.ds(3, 1), gate), (pl.ds(6, 2), late))
                    )
                ]
            )
            for copy in copies[-1]:
                copy.start()
        for copy in small:
            copy.start()
        for i in range(pieces):
            for copy in copies[i]:
                copy.wait()
            lax.fori_loop(i * chunk, (i + 1) * chunk, plane, 0, unroll=2)
        for copy in small:
            copy.wait()
        last = (size_x - 1) * size_y
        for p in range(size_y):
            edge_ten[0, p : p + 1, :] = plain[pl.ds(map_ref[p], 1), :]
            edge_ten[1, p : p + 1, :] = plain[pl.ds(map_ref[last + p], 1), :]


def share_kernel(own, after, pad, share):
    size_x, size_y = own.shape[1], own.shape[2]
    zeros = jnp.zeros(pad.shape[2:], F32)
    for a in range(3):
        pad[a, 0] = zeros
        pad[a, size_x + 1] = zeros

    def plane(x, carry):
        for a in range(3):
            value = own[a, x]
            pad[a, x + 1, PAD : PAD + size_y, :] = value
            share[a, x] = edges_tile(value)
        return carry

    lax.fori_loop(0, size_x, plane, 0, unroll=4)


def gather_kernel(plain, list_ref, all_ref):
    @pl.when(electric())
    def _():
        columns, depth = plain.shape
        pick = (lax.broadcasted_iota(jnp.int32, (columns, columns), 0) == list_ref[...]).astype(F32)
        values = plain[...]
        high = values.astype(jnp.bfloat16).astype(F32)
        mid = (values - high).astype(jnp.bfloat16).astype(F32)
        moved = lax.dot_general(
            pick,
            jnp.concatenate([high, mid, values - high - mid], axis=1),
            (((0,), (0,)), ((), ())),
            preferred_element_type=F32,
        )
        all_ref[...] = moved[:, :depth] + moved[:, depth : 2 * depth] + moved[:, 2 * depth :]


def message_electric(pad_in, own, side_ref, cls_ref, ang_ref, after, high_ref, low_ref, pad, fib_ref, flat):
    size_x, size_y = own.shape[1], own.shape[2]

    def fill(x, carry):
        for a in range(3):
            fill_sides(pad, a, x + 1, side_ref[a, x], size_y)
        return carry

    lax.fori_loop(0, size_x, fill, 0, unroll=4)

    @pl.when(electric())
    def _():
        all_fibers(ang_ref, cls_ref, flat, fib_ref)
        for which, ((_, edge, _), out) in enumerate(zip(sides(size_x), (low_ref, high_ref))):
            out[ROW_VOLT_SIDE : ROW_VOLT_SIDE + 1, :] = side_ref[0, edge, 7:8, :]
            out[ROW_VOLT_SIDE + 1 : ROW_VOLT_SIDE + 2, :] = side_ref[0, edge, 0:1, :]
            fib = [fib_ref[a, place_of(edge, size_y), :] for a in range(3)]
            v, c, d = [rows_of(pad, a, edge + 1, size_y) for a in range(3)]
            f, n, r = [own[k, edge] for k in range(3, 6)]
            rate = volt_rate(pad, edge + 1, fib, size_y)
            _, _, total = currents(v, c, d, f, n, r)
            out[ROW_VOLT : ROW_VOLT + size_y, :] = v
            out[ROW_VOLT_NEXT : ROW_VOLT_NEXT + size_y, :] = v + DT * (rate - total)
            for k, value in enumerate(couplings(fib)):
                out[ROW_COUPLED + k * size_y : ROW_COUPLED + (k + 1) * size_y, :] = value

def message_mechanic(
    pad_in, own, side_ref, cls_ref, ang_ref, ten_ref, list_ref, high_ref, low_ref, pad, flat
):
    size_x, size_y = own.shape[1], own.shape[2]

    @pl.when(jnp.logical_not(electric()))
    def _():
        depth = own.shape[3]
        for which, (_, edge, _) in enumerate(sides(size_x)):
            flat[:, which * size_y : (which + 1) * size_y] = cls_ref[edge]
        fibers = fiber_fields(ang_ref[...], flat[...])
        for which, ((_, edge, _), out) in enumerate(zip(sides(size_x), (low_ref, high_ref))):
            out[ROW_LIST : ROW_LIST + 1, 0:size_y] = list_ref[which].astype(F32)
            rate = motion_rate(pad, edge + 1, size_y)
            stiff = own[6, edge]
            beta = OMEGA * inverse(stiff)
            act = own[7, edge] * ten_ref[which]
            out[ROW_STIFF : ROW_STIFF + size_y, :] = stiff
            for a in range(3):
                row = ROW_SIDE + 2 * a
                out[row : row + 1, :] = side_ref[a, edge, 7:8, :]
                out[row + 1 : row + 2, :] = side_ref[a, edge, 0:1, :]
                u = rows_of(pad, a, edge + 1, size_y)
                out[ROW_NOW + a * size_y : ROW_NOW + (a + 1) * size_y, :] = u
                drive = own[3 + a, edge] + act * fibers[which * size_y : (which + 1) * size_y, a * depth : (a + 1) * depth]
                out[ROW_NEXT + a * size_y : ROW_NEXT + (a + 1) * size_y, :] = (
                    0.28 * u + beta * drive + OMEGA * rate[a]
                )


def put_inner(next_pad, share, a, x, value):
    next_pad[a, x, PAD : PAD + value.shape[0], :] = value
    share[a, x] = edges_tile(value)


def inner_electric(pad, own, fib_ref, plain, next_pad, share, keep, out_hbm, sems):
    size_x, size_y = own.shape[1], own.shape[2]

    @pl.when(electric())
    def _():
        copies = [
            pltpu.make_async_copy(plain.at[x * size_y : (x + 1) * size_y], out_hbm.at[0, 3, x], sems.at[x])
            for x in range(size_x)
        ]
        for copy in copies:
            copy.start()

        def plane(x, carry):
            place = place_of(x, size_y)
            v, c, d = [rows_of(pad, a, x + 1, size_y) for a in range(3)]
            f, n, r, bound, _ = [own[k, x] for k in range(3, 8)]
            rate = volt_rate(pad, x + 1, [fib_ref[a, place, :] for a in range(3)], size_y)
            q, calcium_flow, total = currents(v, c, d, f, n, r)
            flow = 2.0 * c * (1.0 - bound) - 0.4 * bound
            put_inner(next_pad, share, 0, x + 1, v + DT * (rate - total))
            c1 = c + DT * (-0.3 * calcium_flow - 0.5 * c - flow)
            tv = jnp.tanh(v)
            d1 = (1.0 - 2.0 * DT) * d + DT * (1.0 + jnp.tanh(v + 0.5))
            f1 = (1.0 - DT / 3.0) * f + (DT / 6.0) * (1.0 - tv)
            n1 = (1.0 - DT) * n + (0.5 * DT) * (1.0 + tv)
            r1 = (1.0 - DT / 5.0) * r + (DT / 10.0) * (1.0 + jnp.tanh(0.5 * v - 0.25))
            bound1 = bound + DT * flow
            flow1 = 2.0 * c1 * (1.0 - bound1) - 0.4 * bound1
            keep[0, x] = n1
            keep[1, x] = 1.2 * d1 * f1
            keep[2, x] = 0.8 * n1 + 0.6 * rise(c1) * r1
            keep[3, x] = c1 - DT * (0.5 * c1 + flow1)
            return carry

        lax.fori_loop(0, size_x, plane, 0, unroll=2)
        for copy in copies:
            copy.wait()


def inner_mechanic(
    pad, own, cls_ref, ang_ref, ten_ref, next_in, share_in, keep_in, next_pad, share, keep, fib_ref, flat
):
    size_x, size_y = own.shape[1], own.shape[2]

    @pl.when(jnp.logical_not(electric()))
    def _():
        all_fibers(ang_ref, cls_ref, flat, fib_ref)

        def plane(x, carry):
            place = place_of(x, size_y)
            rate = motion_rate(pad, x + 1, size_y)
            beta = OMEGA * inverse(own[6, x])
            act = own[7, x] * ten_ref[place, :]
            keep[3, x] = act
            for a in range(3):
                drive = beta * (own[3 + a, x] + act * fib_ref[a, place, :])
                keep[a, x] = drive
                value = 0.4 * rows_of(pad, a, x + 1, size_y) + drive + OMEGA * rate[a]
                put_inner(next_pad, share, a, x + 1, value)
            return carry

        lax.fori_loop(0, size_x, plane, 0, unroll=2)


def outer_electric(pad, own, fib_ref, volt_low, volt_high, next_in, next_pad, share, wide):
    size_x, size_y = own.shape[1], own.shape[2]
    def put(a, x, slot, value):
        next_pad[a, x, PAD : PAD + size_y, :] = value
        share[a, slot] = edges_tile(value)

    def put_side(a, which, low, high):
        wide[a, which, PAD - 1 : PAD, :] = low
        wide[a, which, PAD + size_y : PAD + size_y + 1, :] = high

    @pl.when(electric())
    def _():
        for which, ((halo, edge, sign), got) in enumerate(zip(sides(size_x), (volt_low, volt_high))):
            wide[0, which, PAD : PAD + size_y, :] = got[ROW_VOLT : ROW_VOLT + size_y, :]
            row = ROW_VOLT_SIDE
            put_side(0, which, got[row : row + 1, :], got[row + 1 : row + 2, :])
            fib = [fib_ref[a, place_of(edge, size_y), :] for a in range(3)]
            put(
                0,
                edge + 1,
                1 + which,
                rows_of(next_pad, 0, edge + 1, size_y) + DT * volt_from(wide, which, couplings(fib), sign, size_y),
            )
            theirs = [got[ROW_COUPLED + k * size_y : ROW_COUPLED + (k + 1) * size_y, :] for k in range(3)]
            put(
                0,
                halo,
                3 * which,
                got[ROW_VOLT_NEXT : ROW_VOLT_NEXT + size_y, :] + DT * volt_from(pad, edge + 1, theirs, -sign, size_y),
            )


def outer_mechanic(pad, own, list_ref, got_low, got_high, next_in, share_in, next_pad, share, wide):
    size_x, size_y = own.shape[1], own.shape[2]
    def put(a, x, slot, value):
        next_pad[a, x, PAD : PAD + size_y, :] = value
        share[a, slot] = edges_tile(value)

    def put_side(a, which, low, high):
        wide[a, which, PAD - 1 : PAD, :] = low
        wide[a, which, PAD + size_y : PAD + size_y + 1, :] = high

    @pl.when(jnp.logical_not(electric()))
    def _():
        for which, ((halo, edge, sign), got) in enumerate(zip(sides(size_x), (got_low, got_high))):
            for a in range(3):
                wide[a, which, PAD : PAD + size_y, :] = got[ROW_NOW + a * size_y : ROW_NOW + (a + 1) * size_y, :]
                row = ROW_SIDE + 2 * a
                put_side(a, which, got[row : row + 1, :], got[row + 1 : row + 2, :])
            stiff = got[ROW_STIFF : ROW_STIFF + size_y, :]
            stiff_own = own[6, edge]
            now = [rows_of(pad, a, edge + 1, size_y) for a in range(3)]
            theirs = [rows_of(wide, a, which, size_y) for a in range(3)]
            ties = tie_rows(list_ref[which].astype(F32), stiff, theirs)
            rate = motion_from(wide, which, sign, size_y)
            beta = OMEGA * inverse(stiff_own)
            for a in range(3):
                put(
                    a,
                    edge + 1,
                    1 + which,
                    rows_of(next_pad, a, edge + 1, size_y) + OMEGA * rate[a] + beta * ties[a] - 0.12 * now[a],
                )
            ties = tie_rows(got[ROW_LIST : ROW_LIST + 1, 0:size_y], stiff_own, now)
            rate = motion_from(pad, edge + 1, -sign, size_y)
            beta = OMEGA * inverse(stiff)
            for a in range(3):
                put(
                    a,
                    halo,
                    3 * which,
                    got[ROW_NEXT + a * size_y : ROW_NEXT + (a + 1) * size_y, :] + OMEGA * rate[a] + beta * ties[a],
                )


def electric_end(x, next_pad, fib_ref):
    size_y = next_pad.shape[2] - 2 * PAD
    place = place_of(x, size_y)
    return rows_of(next_pad, 0, x + 1, size_y) + DT * volt_rate(
        next_pad, x + 1, [fib_ref[a, place, :] for a in range(3)], size_y
    )


def electric_rest(x, next_pad, keep, out):
    size_y = next_pad.shape[2] - 2 * PAD
    v = rows_of(next_pad, 0, x + 1, size_y)
    n, gate, leak, rest_c = [keep[k, x] for k in range(4)]
    flow = gate * (v - 2.0)
    out[0, x] = -DT * (flow + leak * (v + 1.0) + 0.1 * v)
    out[1, x] = rest_c - (0.3 * DT) * flow
    out[2, x] = (1.0 - DT) * n + (0.5 * DT) * (1.0 + jnp.tanh(v))


def mechanic_end(x, next_pad, keep, out, size_y, ties=None):
    rate = motion_rate(next_pad, x + 1, size_y)
    for a in range(3):
        u = rows_of(next_pad, a, x + 1, size_y)
        value = 0.4 * u + keep[a, x] + OMEGA * rate[a]
        out[a, x] = value if ties is None else value + ties[a]


def middle_kernel(
    fib_ref, own, list_ref, got_low, got_high, next_in, side_ref, keep, out_in, out_hbm, next_pad, held, out, sems
):
    size_x = keep.shape[1]
    size_y = fib_ref.shape[1] // size_x
    pieces = sems.shape[0] - 1
    chunk = (size_x - 4) // pieces

    def copy_out(i, fields):
        here = pl.ds(2 + i * chunk, chunk)
        return pltpu.make_async_copy(out.at[0:fields, here], out_hbm.at[0, 0:fields, here], sems.at[i])

    def fill(count):
        def one(x, carry):
            for a in range(count):
                fill_sides(next_pad, a, x, side_ref[a, x], size_y)
            return carry

        lax.fori_loop(2, size_x, one, 0, unroll=2)

    @pl.when(electric())
    def _():
        fill(1)

        def rest(x, carry):
            electric_rest(x, next_pad, keep, out)
            return carry

        lax.fori_loop(0, size_x, rest, 0, unroll=2)
        copy = pltpu.make_async_copy(out.at[1:3], out_hbm.at[0, 1:3], sems.at[pieces])
        copy.start()
        for i, x in enumerate((0, 1, size_x - 2, size_x - 1)):
            held[i] = out[0, x]

        def step(i, carry):
            for k in range(chunk):
                x = 2 + i * chunk + k
                out[0, x] = out[0, x] + electric_end(x, next_pad, fib_ref)
            copy_out(i, 1).start()
            return carry

        lax.fori_loop(0, pieces, step, 0)
        copy.wait()
        for i in range(pieces):
            copy_out(i, 1).wait()

    @pl.when(jnp.logical_not(electric()))
    def _():
        fill(3)
        copy = pltpu.make_async_copy(keep.at[3:4], out_hbm.at[0, 3:4], sems.at[pieces])
        copy.start()

        def sweep(i, carry):
            for k in range(chunk):
                mechanic_end(2 + i * chunk + k, next_pad, keep, out, size_y)
            copy_out(i, 3).start()
            return carry

        lax.fori_loop(0, pieces, sweep, 0)
        for which, ((halo, edge, _), got) in enumerate(zip(sides(size_x), (got_low, got_high))):
            beta = OMEGA * inverse(own[6, edge])
            ties = tie_rows(
                list_ref[which].astype(F32),
                got[ROW_STIFF : ROW_STIFF + size_y, :],
                [rows_of(next_pad, a, halo, size_y) for a in range(3)],
            )
            for a in range(3):
                held[3 * which + a] = beta * ties[a] - 0.12 * rows_of(next_pad, a, edge + 1, size_y)
        copy.wait()
        for i in range(pieces):
            copy_out(i, 3).wait()


def last_kernel(
    fib_ref, next_in, side_ref, keep, held, out_in, out_hbm, next_pad, out, sems
):
    size_x = keep.shape[1]
    size_y = fib_ref.shape[1] // size_x

    def copy_out(which, first, fields):
        here = pl.ds(first, 2)
        return pltpu.make_async_copy(out.at[0:fields, here], out_hbm.at[0, 0:fields, here], sems.at[which])

    work = []
    for which, (halo, edge, _) in enumerate(sides(size_x)):
        near = abs(edge - 1)
        work.append((halo, edge, near, which, min(edge, near)))

    @pl.when(electric())
    def _():
        for halo, edge, near, which, first in work:
            fill_sides(next_pad, 0, halo, side_ref[0, 3 * which], size_y)
            fill_sides(next_pad, 0, edge + 1, side_ref[0, 1 + which], size_y)
            for x in (near, edge):
                out[0, x] = held[2 * which + x - first] + electric_end(x, next_pad, fib_ref)
            copy_out(which, first, 1).start()
        for item in work:
            copy_out(item[3], item[-1], 1).wait()

    @pl.when(jnp.logical_not(electric()))
    def _():
        for halo, edge, near, which, first in work:
            for a in range(3):
                fill_sides(next_pad, a, halo, side_ref[a, 3 * which], size_y)
                fill_sides(next_pad, a, edge + 1, side_ref[a, 1 + which], size_y)
            mechanic_end(near, next_pad, keep, out, size_y)
            mechanic_end(edge, next_pad, keep, out, size_y, [held[3 * which + a] for a in range(3)])
            copy_out(which, first, 3).start()
        for item in work:
            copy_out(item[3], item[-1], 3).wait()


def call(kernel, name, out_shape, operands, spaces, scratch=(), out_spaces=None, aliases=()):
    if out_spaces is None:
        out_spaces = [pltpu.VMEM] * len(out_shape)
    return pl.pallas_call(
        kernel,
        name=name,
        out_shape=tuple(out_shape),
        in_specs=[pl.BlockSpec(memory_space=space) for space in spaces],
        out_specs=tuple(pl.BlockSpec(memory_space=space) for space in out_spaces),
        scratch_shapes=scratch,
        input_output_aliases=dict(aliases),
        cost_estimate=pl.CostEstimate(
            flops=int(COST[name] * 10**10), bytes_accessed=int(COST[name] * 10**7), transcendentals=0
        ),
        compiler_params=pltpu.CompilerParams(vmem_limit_bytes=VMEM_LIMIT),
    )(*operands)


def local(sections, fiber_angles, fiber_class, row_map, interface_rows):
    own = sections[0]
    channels, size_x, size_y, depth = own.shape
    n_gx = lax.axis_size("gx")
    n_gy = lax.axis_size("gy")
    assert lax.axis_size("sec") == 2 and n_gy == 2
    axes = ("sec", "gx", "gy")
    place = lambda sec, i, j: (sec * n_gx + i % n_gx) * n_gy + j
    blocks = [(i, j) for i in range(n_gx) for j in range(n_gy)]

    def ring(section, step):
        return [(place(section, i, j), place(section, i + step, j)) for i, j in blocks] + [
            (place(1 - section, i, j), place(1 - section, i, 1 - j)) for i, j in blocks
        ]

    both = [(0, 1), (1, 0)]
    S, V, H = pltpu.SMEM, pltpu.VMEM, pltpu.HBM
    f32 = lambda *shape: jax.ShapeDtypeStruct(shape, F32)
    hbm = lambda w: pltpu.with_memory_space_constraint(w, H)
    columns = size_x * size_y
    padded = f32(3, size_x + 2, size_y + 2 * PAD, depth)
    classes = fiber_class.transpose(0, 2, 1)
    lists = interface_rows.reshape(2, 1, size_y)
    places = row_map.reshape(-1)

    field = lambda n: pltpu.VMEM((n, size_x, size_y, depth), F32)
    angles = fiber_angles.T
    plain, edge_ten, own_list = call(
        tension_kernel,
        "tension",
        (f32(columns, depth), f32(2, size_y, depth), jax.ShapeDtypeStruct((1, columns), jnp.int32)),
        (hbm(own), hbm(places), hbm(row_map.reshape(1, columns))),
        (H,) * 3,
        [
            field(3),
            field(1),
            field(2),
            pltpu.SMEM((columns,), jnp.int32),
            pltpu.SemaphoreType.DMA((2 + 3 * 4,)),
        ],
    )
    edge_ten = lax.ppermute(edge_ten, "sec", both)
    pad, share = call(share_kernel, "share", (padded, f32(3, size_x, 8, depth)), (own, plain), (V, V))
    side = lax.ppermute(share, "gy", both)
    result = f32(1, 4, size_x, size_y, depth)
    flat = lambda count: pltpu.VMEM((classes.shape[1], count), jnp.int32)
    (gathered,) = call(gather_kernel, "gather", (f32(columns, depth),), (plain, own_list), (V, V))
    tension = lax.ppermute(gathered, "sec", both)
    assert depth == CELLS * classes.shape[1]
    message = f32(VOLT_ROWS, depth)
    high, low, pad, fib = call(
        message_electric,
        "message_electric",
        (message, message, padded, f32(3, columns, depth)),
        (pad, own, side, classes, angles, gathered),
        (V,) * 6,
        [flat(columns)],
        aliases={0: 2},
    )
    volt_low = lax.ppermute(high, axes, ring(0, 1))
    volt_high = lax.ppermute(low, axes, ring(0, -1))
    message = f32(MESSAGE_ROWS, depth)
    high, low, pad = call(
        message_mechanic,
        "message_mechanic",
        (message, message, padded),
        (pad, own, side, classes, angles, edge_ten, lists),
        (V,) * 7,
        [flat(2 * size_y)],
        aliases={0: 2},
    )
    got_low = lax.ppermute(high, axes, ring(1, 1))
    got_high = lax.ppermute(low, axes, ring(1, -1))
    moved, share, keep, result = call(
        inner_electric,
        "inner_electric",
        (padded, f32(3, size_x + 2, 8, depth), f32(4, size_x, size_y, depth), result),
        (pad, own, fib, plain),
        (V,) * 4,
        [pltpu.SemaphoreType.DMA((size_x,))],
        out_spaces=(V, V, V, H),
    )
    moved, share, keep = call(
        inner_mechanic,
        "inner_mechanic",
        (padded, f32(3, size_x + 2, 8, depth), f32(4, size_x, size_y, depth)),
        (pad, own, classes, angles, tension, moved, share, keep),
        (V,) * 8,
        [pltpu.VMEM((3, columns, depth), F32), flat(columns)],
        aliases={5: 0, 6: 1, 7: 2},
    )
    side = lax.ppermute(share, "gy", both)
    wide = pltpu.VMEM((3, 2) + padded.shape[2:], F32)
    moved, share = call(
        outer_electric,
        "outer_electric",
        (padded, f32(3, 4, 8, depth)),
        (pad, own, fib, volt_low, volt_high, moved),
        (V,) * 6,
        [wide],
        aliases={5: 0},
    )
    moved, share = call(
        outer_mechanic,
        "outer_mechanic",
        (padded, f32(3, 4, 8, depth)),
        (pad, own, lists, got_low, got_high, moved, share),
        (V,) * 7,
        [wide],
        aliases={5: 0, 6: 1},
    )
    end_side = lax.ppermute(share, "gy", both)
    fields = pltpu.VMEM((3, size_x, size_y, depth), F32)
    result, moved, held = call(
        middle_kernel,
        "middle",
        (f32(1, 4, size_x, size_y, depth), padded, f32(6, size_y, depth)),
        (fib, own, lists, got_low, got_high, moved, side, keep, result),
        (V,) * 8 + (H,),
        [fields, pltpu.SemaphoreType.DMA((4,))],
        out_spaces=(H, V, V),
        aliases={5: 1, 8: 0},
    )
    return call(
        last_kernel,
        "last",
        (f32(1, 4, size_x, size_y, depth), padded),
        (fib, moved, end_side, keep, held, result),
        (V,) * 5 + (H,),
        [fields, pltpu.SemaphoreType.DMA((2,))],
        out_spaces=(H, V),
        aliases={1: 1, 5: 0},
    )[0]


def solution(mesh):
    in_specs = (
        P("sec", None, "gx", "gy", None),
        P(),
        P("gx", "gy", None),
        P("gx", "gy", None),
        P(None, "gx", "gy", None),
    )
    out_specs = P("sec", None, "gx", "gy", None)
    return jax.shard_map(local, mesh=mesh, in_specs=in_specs, out_specs=out_specs, check_vma=False)
```

```python
import jax
import jax.numpy as jnp
from jax import lax
from jax.experimental import pallas as pl
from jax.experimental.pallas import tpu as pltpu
from jax.sharding import PartitionSpec as P

DT = 0.1
OMEGA = 0.06
F32 = jnp.float32
VMEM_LIMIT = 16 * 1024 * 1024
COST = {
    "tension": 0.001,
    "share": 0.001,
    "gather": 6,
    "edge": 1,
    "message_electric": 1,
    "message_mechanic": 1,
    "inner_electric": 6,
    "inner_mechanic": 6,
    "outer_electric": 1,
    "outer_mechanic": 1,
    "middle": 6,
    "last": 1,
}

CELLS = 16

PAD = 8

ROW_NOW, ROW_NEXT, ROW_STIFF, ROW_SIDE = 0, 96, 192, 224
ROW_LIST = ROW_SIDE + 6
MESSAGE_ROWS = 232
ROW_VOLT, ROW_VOLT_NEXT, ROW_COUPLED, ROW_VOLT_SIDE = 0, 32, 64, 160
VOLT_ROWS = 168


def inverse(v):
    r = pl.reciprocal(v, approx=True)
    return r * (2.0 - v * r)


def rise(c):
    c2 = c * c
    return c2 * inverse(c2 + 0.25)


def ends(like):
    lane = lax.broadcasted_iota(jnp.int32, like, 1)
    return lane == like[1] - 1, lane == 0


def up_z(w, last):
    return jnp.where(last, 0.0, pltpu.roll(w, w.shape[1] - 1, 1))


def down_z(w, first):
    return jnp.where(first, 0.0, pltpu.roll(w, 1, 1))


def rows_of(pad, a, x, size_y, shift=0):
    return pad[a, x, PAD + shift : PAD + shift + size_y, :]


def motion_rate(pad, x, size_y):
    at = lambda a, dx=0, dy=0: rows_of(pad, a, x + dx, size_y, dy)
    u0, u1, u2 = at(0), at(1), at(2)
    last, first = ends(u0.shape)
    w0p, w0m, w1p, w1m = at(0, 1), at(0, -1), at(1, 1), at(1, -1)
    w2p, w2m = at(2, 1), at(2, -1)
    e0, e2 = 0.5 * (w0p - w0m), 0.5 * (w2p - w2m)
    e0y = (at(0, 1, 1) - at(0, -1, 1)) - (at(0, 1, -1) - at(0, -1, -1))
    e1y = (at(1, 1, 1) - at(1, -1, 1)) - (at(1, 1, -1) - at(1, -1, -1))
    v1p, v1m, v2p, v2m = at(1, 0, 1), at(1, 0, -1), at(2, 0, 1), at(2, 0, -1)
    d2 = 0.5 * (v2p - v2m)
    d1 = 0.5 * (v1p - v1m) + e0
    r0 = (
        up_z(u0 + e2, last) + down_z(u0 - e2, first)
        + (at(0, 0, 1) + at(0, 0, -1)) + 0.5 * e1y + 3.0 * (w0p + w0m)
    )
    r1 = (
        up_z(u1 + d2, last) + down_z(u1 - d2, first)
        + 3.0 * (v1p + v1m) + 0.5 * e0y + (w1p + w1m)
    )
    t2 = 3.0 * u2
    r2 = up_z(t2 + d1, last) + down_z(t2 - d1, first) + (v2p + v2m) + (w2p + w2m)
    return r0, r1, r2


def motion_from(pad, x, sign, size_y):
    u0, u1, u2 = [rows_of(pad, a, x, size_y) for a in range(3)]
    last, first = ends(u0.shape)
    half = 0.5 * sign
    dy0 = rows_of(pad, 0, x, size_y, 1) - rows_of(pad, 0, x, size_y, -1)
    dy1 = rows_of(pad, 1, x, size_y, 1) - rows_of(pad, 1, x, size_y, -1)
    dz0 = up_z(u0, last) - down_z(u0, first)
    dz2 = up_z(u2, last) - down_z(u2, first)
    return 3.0 * u0 + half * (dy1 + dz2), u1 + half * dy0, u2 + half * dz0


def volt_rate(pad, x, fib, size_y):
    at = lambda dx=0, dy=0: rows_of(pad, 0, x + dx, size_y, dy)
    v, wp, wm, yp, ym = at(), at(1), at(-1), at(0, 1), at(0, -1)
    last, first = ends(v.shape)
    e = wp - wm
    ey = (at(1, 1) - at(-1, 1)) - (at(1, -1) - at(-1, -1))
    dy = yp - ym
    sum_z = up_z(v, last) + down_z(v, first)
    ez = up_z(e, last) - down_z(e, first)
    dyz = up_z(dy, last) - down_z(dy, first)
    g = [0.75 * w for w in fib]
    d00, d11, d22 = [0.25 + a * b for a, b in zip(g, fib)]
    return (
        d00 * (wp + wm) + d11 * (yp + ym) + d22 * sum_z - 2.0 * (d00 + d11 + d22) * v
        + 0.5 * (fib[0] * (g[1] * ey + g[2] * ez) + g[1] * fib[2] * dyz)
    )


def couplings(fib):
    g = 0.75 * fib[0]
    return 0.25 + g * fib[0], 0.5 * g * fib[1], 0.5 * g * fib[2]


def volt_from(pad, x, coupled, sign, size_y):
    v = rows_of(pad, 0, x, size_y)
    last, first = ends(v.shape)
    dy = rows_of(pad, 0, x, size_y, 1) - rows_of(pad, 0, x, size_y, -1)
    dz = up_z(v, last) - down_z(v, first)
    return coupled[0] * v + sign * (coupled[1] * dy + coupled[2] * dz)


def currents(v, c, d, f, n, r):
    q = rise(c)
    calcium_flow = 1.2 * d * f * (v - 2.0)
    return q, calcium_flow, calcium_flow + (0.8 * n + 0.6 * q * r) * (v + 1.0) + 0.1 * v


def in_three(values):
    high = values.astype(jnp.bfloat16).astype(F32)
    mid = (values - high).astype(jnp.bfloat16).astype(F32)
    return jnp.concatenate([high, mid, values - high - mid], axis=0)


def tie_rows(listed, stiff, u):
    rows, depth = u[0].shape
    joined = in_three(jnp.concatenate([2.0 * stiff * w for w in u], axis=1))
    pick = (lax.broadcasted_iota(jnp.int32, (rows, rows), 0).astype(F32) == listed).astype(F32)
    moved = lax.dot_general(
        jnp.concatenate([pick] * 3, axis=0), joined, (((0,), (0,)), ((), ())), preferred_element_type=F32
    )
    return [moved[:, a * depth : (a + 1) * depth] for a in range(3)]


def edges_tile(value):
    rows = value.shape[0]
    last = lax.broadcasted_iota(jnp.int32, (8, value.shape[1]), 0) == 7
    return jnp.where(last, value[rows - 8 :], value[:8])


def fill_sides(pad, a, x, tile, size_y):
    pad[a, x, 0:PAD, :] = tile
    pad[a, x, PAD + size_y :, :] = tile


def sides(size_x):
    return (0, 0, -1.0), (size_x + 1, size_x - 1, 1.0)


def place_of(x, size_y):
    return pl.ds(pl.multiple_of(x * size_y, size_y), size_y)


def electric():
    return lax.axis_index("sec") == 0


def fiber_table(angles, blocks):
    classes, depth = angles.shape[1], CELLS * blocks
    azimuth, elevation = angles[0:1, :], angles[1:2, :]
    flat_part = jnp.cos(elevation)
    fib = [jnp.cos(azimuth) * flat_part, jnp.sin(azimuth) * flat_part, jnp.sin(elevation)]
    own = lax.broadcasted_iota(jnp.int32, (blocks, depth), 1) // CELLS
    own = own == lax.broadcasted_iota(jnp.int32, (blocks, depth), 0)
    return in_three(
        jnp.concatenate(
            [
                jnp.concatenate(
                    [jnp.where(own, jnp.broadcast_to(w[:, k : k + 1], own.shape), 0.0) for w in fib], axis=1
                )
                for k in range(classes)
            ],
            axis=0,
        )
    )


def fiber_fields(table, cls):
    classes = table.shape[0] // (3 * cls.shape[0])
    hits = jnp.concatenate([(cls == k).astype(F32) for k in range(classes)] * 3, axis=0)
    return lax.dot_general(hits, table, (((0,), (0,)), ((), ())), preferred_element_type=F32)


def all_fibers(table_ref, cls_ref, flat, fib_ref):
    size_x, _, size_y = cls_ref.shape
    depth = fib_ref.shape[2]
    for x in range(size_x):
        flat[:, x * size_y : (x + 1) * size_y] = cls_ref[x]
    found = fiber_fields(table_ref[...], flat[...])
    for a in range(3):
        fib_ref[a] = found[:, a * depth : (a + 1) * depth]


def tension_kernel(
    sec_hbm, map_hbm, list_hbm, ang_hbm, plain, edge_ten, list_ref, table_ref, main, gate, late, ang_ref, map_ref, sems
):
    size_x, size_y = sec_hbm.shape[1], sec_hbm.shape[2]
    pieces = (sems.shape[0] - 3) // 3
    chunk = size_x // pieces

    def plane(x, carry):
        v, c, d, f, bound, s = main[0, x], main[1, x], main[2, x], gate[0, x], late[0, x], late[1, x]
        calcium_flow = 1.2 * d * f * (v - 2.0)
        flow = 2.0 * c * (1.0 - bound) - 0.4 * bound
        c1 = c + DT * (-0.3 * calcium_flow - 0.5 * c - flow)
        s1 = s + (0.5 * DT) * (rise(c) - s)
        plain[place_of(x, size_y), :] = s1 + (0.5 * DT) * (rise(c1) - s1)
        return carry

    @pl.when(electric())
    def _():
        small = [
            pltpu.make_async_copy(src, dst, sems.at[i])
            for i, (src, dst) in enumerate(((ang_hbm, ang_ref), (map_hbm, map_ref), (list_hbm, list_ref)))
        ]
        small[0].start()
        copies = []
        for i in range(pieces):
            here = pl.ds(i * chunk, chunk)
            copies.append(
                [
                    pltpu.make_async_copy(sec_hbm.at[src, here], dst.at[:, here], sems.at[3 + 3 * i + k])
                    for k, (src, dst) in enumerate(
                        ((pl.ds(0, 3), main), (pl.ds(3, 1), gate), (pl.ds(6, 2), late))
                    )
                ]
            )
            for copy in copies[-1]:
                copy.start()
        for copy in small[1:]:
            copy.start()
        small[0].wait()
        table_ref[...] = fiber_table(ang_ref[...], main.shape[3] // CELLS)
        for i in range(pieces):
            for copy in copies[i]:
                copy.wait()
            lax.fori_loop(i * chunk, (i + 1) * chunk, plane, 0, unroll=2)
        for copy in small[1:]:
            copy.wait()
        last = (size_x - 1) * size_y
        for p in range(size_y):
            edge_ten[0, p : p + 1, :] = plain[pl.ds(map_ref[p], 1), :]
            edge_ten[1, p : p + 1, :] = plain[pl.ds(map_ref[last + p], 1), :]


def share_kernel(own, after, pad, share):
    size_x, size_y = own.shape[1], own.shape[2]
    zeros = jnp.zeros(pad.shape[2:], F32)
    for a in range(3):
        pad[a, 0] = zeros
        pad[a, size_x + 1] = zeros

    def plane(x, carry):
        for a in range(3):
            value = own[a, x]
            pad[a, x + 1, PAD : PAD + size_y, :] = value
            share[a, x] = edges_tile(value)
        return carry

    lax.fori_loop(0, size_x, plane, 0, unroll=4)


def gather_kernel(plain, list_ref, after, all_ref):
    @pl.when(electric())
    def _():
        columns, depth = plain.shape
        pick = (lax.broadcasted_iota(jnp.int32, (columns, columns), 0) == list_ref[...]).astype(F32)
        values = plain[...]
        high = values.astype(jnp.bfloat16).astype(F32)
        mid = (values - high).astype(jnp.bfloat16).astype(F32)
        moved = lax.dot_general(
            pick,
            jnp.concatenate([high, mid, values - high - mid], axis=1),
            (((0,), (0,)), ((), ())),
            preferred_element_type=F32,
        )
        all_ref[...] = moved[:, :depth] + moved[:, depth : 2 * depth] + moved[:, 2 * depth :]


def edge_kernel(table_in, cls_ref, ang_ref, after, list_ref, edge_fib, table_ref, flat):
    size_x, blocks, size_y = cls_ref.shape

    @pl.when(jnp.logical_not(electric()))
    def _():
        table_ref[...] = fiber_table(ang_ref[...], blocks)

    for which, (_, edge, _) in enumerate(sides(size_x)):
        flat[:, which * size_y : (which + 1) * size_y] = cls_ref[edge]
    edge_fib[...] = fiber_fields(table_ref[...], flat[...])


def message_electric(pad_in, own, side_ref, edge_fib, high_ref, low_ref, pad):
    size_x, size_y = own.shape[1], own.shape[2]

    def fill(x, carry):
        for a in range(3):
            fill_sides(pad, a, x + 1, side_ref[a, x], size_y)
        return carry

    lax.fori_loop(0, size_x, fill, 0, unroll=4)

    @pl.when(electric())
    def _():
        for which, ((_, edge, _), out) in enumerate(zip(sides(size_x), (low_ref, high_ref))):
            out[ROW_VOLT_SIDE : ROW_VOLT_SIDE + 1, :] = side_ref[0, edge, 7:8, :]
            out[ROW_VOLT_SIDE + 1 : ROW_VOLT_SIDE + 2, :] = side_ref[0, edge, 0:1, :]
            rows, depth = slice(which * size_y, (which + 1) * size_y), own.shape[3]
            fib = [edge_fib[rows, a * depth : (a + 1) * depth] for a in range(3)]
            v, c, d = [rows_of(pad, a, edge + 1, size_y) for a in range(3)]
            f, n, r = [own[k, edge] for k in range(3, 6)]
            rate = volt_rate(pad, edge + 1, fib, size_y)
            _, _, total = currents(v, c, d, f, n, r)
            out[ROW_VOLT : ROW_VOLT + size_y, :] = v
            out[ROW_VOLT_NEXT : ROW_VOLT_NEXT + size_y, :] = v + DT * (rate - total)
            for k, value in enumerate(couplings(fib)):
                out[ROW_COUPLED + k * size_y : ROW_COUPLED + (k + 1) * size_y, :] = value

def message_mechanic(pad_in, own, side_ref, edge_fib, ten_ref, list_ref, high_ref, low_ref, pad):
    size_x, size_y = own.shape[1], own.shape[2]

    @pl.when(jnp.logical_not(electric()))
    def _():
        depth = own.shape[3]
        for which, ((_, edge, _), out) in enumerate(zip(sides(size_x), (low_ref, high_ref))):
            out[ROW_LIST : ROW_LIST + 1, 0:size_y] = list_ref[which].astype(F32)
            rate = motion_rate(pad, edge + 1, size_y)
            stiff = own[6, edge]
            beta = OMEGA * inverse(stiff)
            act = own[7, edge] * ten_ref[which]
            out[ROW_STIFF : ROW_STIFF + size_y, :] = stiff
            for a in range(3):
                row = ROW_SIDE + 2 * a
                out[row : row + 1, :] = side_ref[a, edge, 7:8, :]
                out[row + 1 : row + 2, :] = side_ref[a, edge, 0:1, :]
                u = rows_of(pad, a, edge + 1, size_y)
                out[ROW_NOW + a * size_y : ROW_NOW + (a + 1) * size_y, :] = u
                drive = own[3 + a, edge] + act * edge_fib[which * size_y : (which + 1) * size_y, a * depth : (a + 1) * depth]
                out[ROW_NEXT + a * size_y : ROW_NEXT + (a + 1) * size_y, :] = (
                    0.28 * u + beta * drive + OMEGA * rate[a]
                )


def put_inner(next_pad, share, a, x, value):
    next_pad[a, x, PAD : PAD + value.shape[0], :] = value
    share[a, x] = edges_tile(value)


def inner_electric(
    pad, own, plain, cls_ref, table_ref, next_pad, share, keep, out_hbm, fib_ref, flat, sems
):
    size_x, size_y = own.shape[1], own.shape[2]

    all_fibers(table_ref, cls_ref, flat, fib_ref)

    @pl.when(electric())
    def _():
        copies = [
            pltpu.make_async_copy(plain.at[x * size_y : (x + 1) * size_y], out_hbm.at[0, 3, x], sems.at[x])
            for x in range(size_x)
        ]
        for copy in copies:
            copy.start()

        def plane(x, carry):
            place = place_of(x, size_y)
            v, c, d = [rows_of(pad, a, x + 1, size_y) for a in range(3)]
            f, n, r, bound, _ = [own[k, x] for k in range(3, 8)]
            rate = volt_rate(pad, x + 1, [fib_ref[a, place, :] for a in range(3)], size_y)
            q, calcium_flow, total = currents(v, c, d, f, n, r)
            flow = 2.0 * c * (1.0 - bound) - 0.4 * bound
            put_inner(next_pad, share, 0, x + 1, v + DT * (rate - total))
            c1 = c + DT * (-0.3 * calcium_flow - 0.5 * c - flow)
            tv = jnp.tanh(v)
            d1 = (1.0 - 2.0 * DT) * d + DT * (1.0 + jnp.tanh(v + 0.5))
            f1 = (1.0 - DT / 3.0) * f + (DT / 6.0) * (1.0 - tv)
            n1 = (1.0 - DT) * n + (0.5 * DT) * (1.0 + tv)
            r1 = (1.0 - DT / 5.0) * r + (DT / 10.0) * (1.0 + jnp.tanh(0.5 * v - 0.25))
            bound1 = bound + DT * flow
            flow1 = 2.0 * c1 * (1.0 - bound1) - 0.4 * bound1
            keep[0, x] = n1
            keep[1, x] = 1.2 * d1 * f1
            keep[2, x] = 0.8 * n1 + 0.6 * rise(c1) * r1
            keep[3, x] = c1 - DT * (0.5 * c1 + flow1)
            return carry

        lax.fori_loop(0, size_x, plane, 0, unroll=2)
        for copy in copies:
            copy.wait()


def inner_mechanic(pad, own, fib_ref, ten_ref, next_in, share_in, keep_in, next_pad, share, keep):
    size_x, size_y = own.shape[1], own.shape[2]

    @pl.when(jnp.logical_not(electric()))
    def _():
        def plane(x, carry):
            place = place_of(x, size_y)
            rate = motion_rate(pad, x + 1, size_y)
            beta = OMEGA * inverse(own[6, x])
            act = own[7, x] * ten_ref[place, :]
            keep[3, x] = act
            for a in range(3):
                drive = beta * (own[3 + a, x] + act * fib_ref[a, place, :])
                keep[a, x] = drive
                value = 0.4 * rows_of(pad, a, x + 1, size_y) + drive + OMEGA * rate[a]
                put_inner(next_pad, share, a, x + 1, value)
            return carry

        lax.fori_loop(0, size_x, plane, 0, unroll=2)


def outer_electric(pad, own, fib_ref, volt_low, volt_high, next_in, next_pad, share, wide):
    size_x, size_y = own.shape[1], own.shape[2]
    def put(a, x, slot, value):
        next_pad[a, x, PAD : PAD + size_y, :] = value
        share[a, slot] = edges_tile(value)

    def put_side(a, which, low, high):
        wide[a, which, PAD - 1 : PAD, :] = low
        wide[a, which, PAD + size_y : PAD + size_y + 1, :] = high

    @pl.when(electric())
    def _():
        for which, ((halo, edge, sign), got) in enumerate(zip(sides(size_x), (volt_low, volt_high))):
            wide[0, which, PAD : PAD + size_y, :] = got[ROW_VOLT : ROW_VOLT + size_y, :]
            row = ROW_VOLT_SIDE
            put_side(0, which, got[row : row + 1, :], got[row + 1 : row + 2, :])
            fib = [fib_ref[a, place_of(edge, size_y), :] for a in range(3)]
            put(
                0,
                edge + 1,
                1 + which,
                rows_of(next_pad, 0, edge + 1, size_y) + DT * volt_from(wide, which, couplings(fib), sign, size_y),
            )
            theirs = [got[ROW_COUPLED + k * size_y : ROW_COUPLED + (k + 1) * size_y, :] for k in range(3)]
            put(
                0,
                halo,
                3 * which,
                got[ROW_VOLT_NEXT : ROW_VOLT_NEXT + size_y, :] + DT * volt_from(pad, edge + 1, theirs, -sign, size_y),
            )


def outer_mechanic(pad, own, list_ref, got_low, got_high, next_in, share_in, next_pad, share, wide):
    size_x, size_y = own.shape[1], own.shape[2]
    def put(a, x, slot, value):
        next_pad[a, x, PAD : PAD + size_y, :] = value
        share[a, slot] = edges_tile(value)

    def put_side(a, which, low, high):
        wide[a, which, PAD - 1 : PAD, :] = low
        wide[a, which, PAD + size_y : PAD + size_y + 1, :] = high

    @pl.when(jnp.logical_not(electric()))
    def _():
        for which, ((halo, edge, sign), got) in enumerate(zip(sides(size_x), (got_low, got_high))):
            for a in range(3):
                wide[a, which, PAD : PAD + size_y, :] = got[ROW_NOW + a * size_y : ROW_NOW + (a + 1) * size_y, :]
                row = ROW_SIDE + 2 * a
                put_side(a, which, got[row : row + 1, :], got[row + 1 : row + 2, :])
            stiff = got[ROW_STIFF : ROW_STIFF + size_y, :]
            stiff_own = own[6, edge]
            now = [rows_of(pad, a, edge + 1, size_y) for a in range(3)]
            theirs = [rows_of(wide, a, which, size_y) for a in range(3)]
            ties = tie_rows(list_ref[which].astype(F32), stiff, theirs)
            rate = motion_from(wide, which, sign, size_y)
            beta = OMEGA * inverse(stiff_own)
            for a in range(3):
                put(
                    a,
                    edge + 1,
                    1 + which,
                    rows_of(next_pad, a, edge + 1, size_y) + OMEGA * rate[a] + beta * ties[a] - 0.12 * now[a],
                )
            ties = tie_rows(got[ROW_LIST : ROW_LIST + 1, 0:size_y], stiff_own, now)
            rate = motion_from(pad, edge + 1, -sign, size_y)
            beta = OMEGA * inverse(stiff)
            for a in range(3):
                put(
                    a,
                    halo,
                    3 * which,
                    got[ROW_NEXT + a * size_y : ROW_NEXT + (a + 1) * size_y, :] + OMEGA * rate[a] + beta * ties[a],
                )


def electric_end(x, next_pad, fib_ref):
    size_y = next_pad.shape[2] - 2 * PAD
    place = place_of(x, size_y)
    return rows_of(next_pad, 0, x + 1, size_y) + DT * volt_rate(
        next_pad, x + 1, [fib_ref[a, place, :] for a in range(3)], size_y
    )


def electric_rest(x, next_pad, keep, out):
    size_y = next_pad.shape[2] - 2 * PAD
    v = rows_of(next_pad, 0, x + 1, size_y)
    n, gate, leak, rest_c = [keep[k, x] for k in range(4)]
    flow = gate * (v - 2.0)
    out[0, x] = -DT * (flow + leak * (v + 1.0) + 0.1 * v)
    out[1, x] = rest_c - (0.3 * DT) * flow
    out[2, x] = (1.0 - DT) * n + (0.5 * DT) * (1.0 + jnp.tanh(v))


def mechanic_end(x, next_pad, keep, size_y):
    rate = motion_rate(next_pad, x + 1, size_y)
    return [
        0.4 * rows_of(next_pad, a, x + 1, size_y) + keep[a, x] + OMEGA * rate[a] for a in range(3)
    ]


def middle_kernel(
    fib_ref, own, list_ref, got_low, got_high, next_in, side_ref, keep, out_in,
    out_hbm, next_pad, held, final, out, sems
):
    size_x = keep.shape[1]
    size_y = fib_ref.shape[1] // size_x
    pieces = sems.shape[0]
    chunk = final.shape[1]

    def copy_out(i, fields):
        here = pl.ds(2 + i * chunk, chunk)
        return pltpu.make_async_copy(out.at[0:fields, here], out_hbm.at[0, 0:fields, here], sems.at[i])

    def fill(count):
        def one(x, carry):
            for a in range(count):
                fill_sides(next_pad, a, x, side_ref[a, x], size_y)
            return carry

        lax.fori_loop(2, size_x, one, 0, unroll=2)

    @pl.when(electric())
    def _():
        fill(1)

        def rest(x, carry):
            electric_rest(x, next_pad, keep, out)
            return carry

        lax.fori_loop(0, size_x, rest, 0, unroll=2)
        copy = pltpu.make_async_copy(out.at[1:3], out_hbm.at[0, 1:3], sems.at[pieces - 1])
        copy.start()
        for i, x in enumerate((0, 1, size_x - 2, size_x - 1)):
            held[i] = out[0, x]

        def step(i, carry):
            for k in range(chunk):
                x = 2 + i * chunk + k
                out[0, x] = out[0, x] + electric_end(x, next_pad, fib_ref)
            copy_out(i, 1).start()
            return carry

        lax.fori_loop(0, pieces - 1, step, 0)
        for k in range(chunk):
            x = size_x - 2 - chunk + k
            final[0, k] = out[0, x] + electric_end(x, next_pad, fib_ref)
        copy.wait()
        for i in range(pieces - 1):
            copy_out(i, 1).wait()

    @pl.when(jnp.logical_not(electric()))
    def _():
        fill(3)
        copy = pltpu.make_async_copy(keep.at[3:4], out_hbm.at[0, 3:4], sems.at[pieces - 1])
        copy.start()

        def sweep(i, carry):
            for k in range(chunk):
                x = 2 + i * chunk + k
                for a, value in enumerate(mechanic_end(x, next_pad, keep, size_y)):
                    out[a, x] = value
            copy_out(i, 3).start()
            return carry

        lax.fori_loop(0, pieces - 1, sweep, 0)
        for which, ((halo, edge, _), got) in enumerate(zip(sides(size_x), (got_low, got_high))):
            beta = OMEGA * inverse(own[6, edge])
            ties = tie_rows(
                list_ref[which].astype(F32),
                got[ROW_STIFF : ROW_STIFF + size_y, :],
                [rows_of(next_pad, a, halo, size_y) for a in range(3)],
            )
            for a in range(3):
                held[3 * which + a] = beta * ties[a] - 0.12 * rows_of(next_pad, a, edge + 1, size_y)
        for k in range(chunk):
            for a, value in enumerate(mechanic_end(size_x - 2 - chunk + k, next_pad, keep, size_y)):
                final[a, k] = value
        copy.wait()
        for i in range(pieces - 1):
            copy_out(i, 3).wait()


def last_kernel(
    fib_ref, next_in, side_ref, keep, held, final, out_in, out_hbm, next_pad, out, sems
):
    size_x = keep.shape[1]
    size_y = fib_ref.shape[1] // size_x

    def copy_out(which, first, fields):
        here = pl.ds(first, 2)
        return pltpu.make_async_copy(out.at[0:fields, here], out_hbm.at[0, 0:fields, here], sems.at[which])

    def copy_final(fields):
        here = pl.ds(size_x - 2 - final.shape[1], final.shape[1])
        return pltpu.make_async_copy(final.at[0:fields], out_hbm.at[0, 0:fields, here], sems.at[2])

    work = []
    for which, (halo, edge, _) in enumerate(sides(size_x)):
        near = abs(edge - 1)
        work.append((halo, edge, near, which, min(edge, near)))

    @pl.when(electric())
    def _():
        copy_final(1).start()
        for halo, edge, near, which, first in work:
            fill_sides(next_pad, 0, halo, side_ref[0, 3 * which], size_y)
            fill_sides(next_pad, 0, edge + 1, side_ref[0, 1 + which], size_y)
            for x in (near, edge):
                out[0, x] = held[2 * which + x - first] + electric_end(x, next_pad, fib_ref)
            copy_out(which, first, 1).start()
        for item in work:
            copy_out(item[3], item[-1], 1).wait()
        copy_final(1).wait()

    @pl.when(jnp.logical_not(electric()))
    def _():
        copy_final(3).start()
        for halo, edge, near, which, first in work:
            for a in range(3):
                fill_sides(next_pad, a, halo, side_ref[a, 3 * which], size_y)
                fill_sides(next_pad, a, edge + 1, side_ref[a, 1 + which], size_y)
            for a, value in enumerate(mechanic_end(near, next_pad, keep, size_y)):
                out[a, near] = value
            for a, value in enumerate(mechanic_end(edge, next_pad, keep, size_y)):
                out[a, edge] = value + held[3 * which + a]
            copy_out(which, first, 3).start()
        for item in work:
            copy_out(item[3], item[-1], 3).wait()
        copy_final(3).wait()


def call(kernel, name, out_shape, operands, spaces, scratch=(), out_spaces=None, aliases=()):
    if out_spaces is None:
        out_spaces = [pltpu.VMEM] * len(out_shape)
    return pl.pallas_call(
        kernel,
        name=name,
        out_shape=tuple(out_shape),
        in_specs=[pl.BlockSpec(memory_space=space) for space in spaces],
        out_specs=tuple(pl.BlockSpec(memory_space=space) for space in out_spaces),
        scratch_shapes=scratch,
        input_output_aliases=dict(aliases),
        cost_estimate=pl.CostEstimate(
            flops=int(COST[name] * 10**10), bytes_accessed=int(COST[name] * 10**7), transcendentals=0
        ),
        compiler_params=pltpu.CompilerParams(vmem_limit_bytes=VMEM_LIMIT),
    )(*operands)


def local(sections, fiber_angles, fiber_class, row_map, interface_rows):
    own = sections[0]
    channels, size_x, size_y, depth = own.shape
    n_gx = lax.axis_size("gx")
    n_gy = lax.axis_size("gy")
    assert lax.axis_size("sec") == 2 and n_gy == 2
    axes = ("sec", "gx", "gy")
    place = lambda sec, i, j: (sec * n_gx + i % n_gx) * n_gy + j
    blocks = [(i, j) for i in range(n_gx) for j in range(n_gy)]

    def ring(section, step):
        return [(place(section, i, j), place(section, i + step, j)) for i, j in blocks] + [
            (place(1 - section, i, j), place(1 - section, i, 1 - j)) for i, j in blocks
        ]

    both = [(0, 1), (1, 0)]
    S, V, H = pltpu.SMEM, pltpu.VMEM, pltpu.HBM
    f32 = lambda *shape: jax.ShapeDtypeStruct(shape, F32)
    hbm = lambda w: pltpu.with_memory_space_constraint(w, H)
    columns = size_x * size_y
    padded = f32(3, size_x + 2, size_y + 2 * PAD, depth)
    classes = fiber_class.transpose(0, 2, 1)
    lists = interface_rows.reshape(2, 1, size_y)
    places = row_map.reshape(-1)

    field = lambda n: pltpu.VMEM((n, size_x, size_y, depth), F32)
    flat = lambda count: pltpu.VMEM((classes.shape[1], count), jnp.int32)
    angles = fiber_angles.T
    plain, edge_ten, own_list, table = call(
        tension_kernel,
        "tension",
        (
            f32(columns, depth),
            f32(2, size_y, depth),
            jax.ShapeDtypeStruct((1, columns), jnp.int32),
            f32(3 * fiber_angles.shape[0] * classes.shape[1], 3 * depth),
        ),
        (hbm(own), hbm(places), hbm(row_map.reshape(1, columns)), hbm(angles)),
        (H,) * 4,
        [
            field(3),
            field(1),
            field(2),
            pltpu.VMEM(angles.shape, F32),
            pltpu.SMEM((columns,), jnp.int32),
            pltpu.SemaphoreType.DMA((3 + 3 * 4,)),
        ],
    )
    edge_ten = lax.ppermute(edge_ten, "sec", both)
    pad, share = call(share_kernel, "share", (padded, f32(3, size_x, 8, depth)), (own, plain), (V, V))
    side = lax.ppermute(share, "gy", both)
    result = f32(1, 4, size_x, size_y, depth)
    (gathered,) = call(gather_kernel, "gather", (f32(columns, depth),), (plain, own_list, share), (V,) * 3)
    edge_fib, table = call(
        edge_kernel,
        "edge",
        (f32(2 * size_y, 3 * depth), f32(*table.shape)),
        (table, classes, angles, gathered, lists),
        (V,) * 5,
        [flat(2 * size_y)],
        aliases={0: 1},
    )
    tension = lax.ppermute(gathered, "sec", both)
    assert depth == CELLS * classes.shape[1]
    message = f32(VOLT_ROWS, depth)
    high, low, pad = call(
        message_electric,
        "message_electric",
        (message, message, padded),
        (pad, own, side, edge_fib),
        (V,) * 4,
        aliases={0: 2},
    )
    volt_low = lax.ppermute(high, axes, ring(0, 1))
    volt_high = lax.ppermute(low, axes, ring(0, -1))
    message = f32(MESSAGE_ROWS, depth)
    high, low, pad = call(
        message_mechanic,
        "message_mechanic",
        (message, message, padded),
        (pad, own, side, edge_fib, edge_ten, lists),
        (V,) * 6,
        aliases={0: 2},
    )
    got_low = lax.ppermute(high, axes, ring(1, 1))
    got_high = lax.ppermute(low, axes, ring(1, -1))
    moved, share, keep, result, fib = call(
        inner_electric,
        "inner_electric",
        (padded, f32(3, size_x + 2, 8, depth), f32(4, size_x, size_y, depth), result, f32(3, columns, depth)),
        (pad, own, plain, classes, table),
        (V,) * 5,
        [flat(columns), pltpu.SemaphoreType.DMA((size_x,))],
        out_spaces=(V, V, V, H, V),
    )
    moved, share, keep = call(
        inner_mechanic,
        "inner_mechanic",
        (padded, f32(3, size_x + 2, 8, depth), f32(4, size_x, size_y, depth)),
        (pad, own, fib, tension, moved, share, keep),
        (V,) * 7,
        aliases={4: 0, 5: 1, 6: 2},
    )
    side = lax.ppermute(share, "gy", both)
    wide = pltpu.VMEM((3, 2) + padded.shape[2:], F32)
    moved, share = call(
        outer_electric,
        "outer_electric",
        (padded, f32(3, 4, 8, depth)),
        (pad, own, fib, volt_low, volt_high, moved),
        (V,) * 6,
        [wide],
        aliases={5: 0},
    )
    moved, share = call(
        outer_mechanic,
        "outer_mechanic",
        (padded, f32(3, 4, 8, depth)),
        (pad, own, lists, got_low, got_high, moved, share),
        (V,) * 7,
        [wide],
        aliases={5: 0, 6: 1},
    )
    end_side = lax.ppermute(share, "gy", both)
    fields = pltpu.VMEM((3, size_x, size_y, depth), F32)
    pieces = 3
    chunk = (size_x - 4) // pieces
    result, moved, held, final = call(
        middle_kernel,
        "middle",
        (f32(1, 4, size_x, size_y, depth), padded, f32(6, size_y, depth), f32(3, chunk, size_y, depth)),
        (fib, own, lists, got_low, got_high, moved, side, keep, result),
        (V,) * 8 + (H,),
        [fields, pltpu.SemaphoreType.DMA((pieces,))],
        out_spaces=(H, V, V, V),
        aliases={5: 1, 8: 0},
    )
    return call(
        last_kernel,
        "last",
        (f32(1, 4, size_x, size_y, depth), padded),
        (fib, moved, end_side, keep, held, final, result),
        (V,) * 6 + (H,),
        [fields, pltpu.SemaphoreType.DMA((3,))],
        out_spaces=(H, V),
        aliases={1: 1, 6: 0},
    )[0]


def solution(mesh):
    in_specs = (
        P("sec", None, "gx", "gy", None),
        P(),
        P("gx", "gy", None),
        P("gx", "gy", None),
        P(None, "gx", "gy", None),
    )
    out_specs = P("sec", None, "gx", "gy", None)
    return jax.shard_map(local, mesh=mesh, in_specs=in_specs, out_specs=out_specs, check_vma=False)
```

```python
import functools

import jax
import jax.numpy as jnp
from jax import lax
from jax.experimental import pallas as pl
from jax.experimental.pallas import tpu as pltpu
from jax.sharding import PartitionSpec as P

DT = 0.1
OMEGA = 0.06
F32 = jnp.float32
VMEM_LIMIT = 16 * 1024 * 1024
COST = {
    "tension": 0.001,
    "share": 0.001,
    "gather": 6,
    "edge": 1,
    "message_electric": 1,
    "message_mechanic": 1,
    "inner_electric": 6,
    "inner_mechanic": 6,
    "outer_electric": 1,
    "outer_low": 0.01,
    "outer_high": 1,
    "middle": 6,
    "last": 1,
}

CELLS = 16

PAD = 8

ROW_NOW, ROW_NEXT, ROW_STIFF, ROW_SIDE = 0, 96, 192, 224
ROW_LIST = ROW_SIDE + 6
MESSAGE_ROWS = 232
ROW_VOLT, ROW_VOLT_NEXT, ROW_COUPLED, ROW_VOLT_SIDE = 0, 32, 64, 160
VOLT_ROWS = 168


def inverse(v):
    r = pl.reciprocal(v, approx=True)
    return r * (2.0 - v * r)


def rise(c):
    c2 = c * c
    return c2 * inverse(c2 + 0.25)


def ends(like):
    lane = lax.broadcasted_iota(jnp.int32, like, 1)
    return lane == like[1] - 1, lane == 0


def up_z(w, last):
    return jnp.where(last, 0.0, pltpu.roll(w, w.shape[1] - 1, 1))


def down_z(w, first):
    return jnp.where(first, 0.0, pltpu.roll(w, 1, 1))


def rows_of(pad, a, x, size_y, shift=0):
    return pad[a, x, PAD + shift : PAD + shift + size_y, :]


def motion_rate(pad, x, size_y):
    at = lambda a, dx=0, dy=0: rows_of(pad, a, x + dx, size_y, dy)
    u0, u1, u2 = at(0), at(1), at(2)
    last, first = ends(u0.shape)
    w0p, w0m, w1p, w1m = at(0, 1), at(0, -1), at(1, 1), at(1, -1)
    w2p, w2m = at(2, 1), at(2, -1)
    e0, e2 = 0.5 * (w0p - w0m), 0.5 * (w2p - w2m)
    e0y = (at(0, 1, 1) - at(0, -1, 1)) - (at(0, 1, -1) - at(0, -1, -1))
    e1y = (at(1, 1, 1) - at(1, -1, 1)) - (at(1, 1, -1) - at(1, -1, -1))
    v1p, v1m, v2p, v2m = at(1, 0, 1), at(1, 0, -1), at(2, 0, 1), at(2, 0, -1)
    d2 = 0.5 * (v2p - v2m)
    d1 = 0.5 * (v1p - v1m) + e0
    r0 = (
        up_z(u0 + e2, last) + down_z(u0 - e2, first)
        + (at(0, 0, 1) + at(0, 0, -1)) + 0.5 * e1y + 3.0 * (w0p + w0m)
    )
    r1 = (
        up_z(u1 + d2, last) + down_z(u1 - d2, first)
        + 3.0 * (v1p + v1m) + 0.5 * e0y + (w1p + w1m)
    )
    t2 = 3.0 * u2
    r2 = up_z(t2 + d1, last) + down_z(t2 - d1, first) + (v2p + v2m) + (w2p + w2m)
    return r0, r1, r2


def motion_from(pad, x, sign, size_y):
    u0, u1, u2 = [rows_of(pad, a, x, size_y) for a in range(3)]
    last, first = ends(u0.shape)
    half = 0.5 * sign
    dy0 = rows_of(pad, 0, x, size_y, 1) - rows_of(pad, 0, x, size_y, -1)
    dy1 = rows_of(pad, 1, x, size_y, 1) - rows_of(pad, 1, x, size_y, -1)
    dz0 = up_z(u0, last) - down_z(u0, first)
    dz2 = up_z(u2, last) - down_z(u2, first)
    return 3.0 * u0 + half * (dy1 + dz2), u1 + half * dy0, u2 + half * dz0


def volt_rate(pad, x, fib, size_y):
    at = lambda dx=0, dy=0: rows_of(pad, 0, x + dx, size_y, dy)
    v, wp, wm, yp, ym = at(), at(1), at(-1), at(0, 1), at(0, -1)
    last, first = ends(v.shape)
    e = wp - wm
    ey = (at(1, 1) - at(-1, 1)) - (at(1, -1) - at(-1, -1))
    dy = yp - ym
    sum_z = up_z(v, last) + down_z(v, first)
    ez = up_z(e, last) - down_z(e, first)
    dyz = up_z(dy, last) - down_z(dy, first)
    g = [0.75 * w for w in fib]
    d00, d11, d22 = [0.25 + a * b for a, b in zip(g, fib)]
    return (
        d00 * (wp + wm) + d11 * (yp + ym) + d22 * sum_z - 2.0 * (d00 + d11 + d22) * v
        + 0.5 * (fib[0] * (g[1] * ey + g[2] * ez) + g[1] * fib[2] * dyz)
    )


def couplings(fib):
    g = 0.75 * fib[0]
    return 0.25 + g * fib[0], 0.5 * g * fib[1], 0.5 * g * fib[2]


def volt_from(pad, x, coupled, sign, size_y):
    v = rows_of(pad, 0, x, size_y)
    last, first = ends(v.shape)
    dy = rows_of(pad, 0, x, size_y, 1) - rows_of(pad, 0, x, size_y, -1)
    dz = up_z(v, last) - down_z(v, first)
    return coupled[0] * v + sign * (coupled[1] * dy + coupled[2] * dz)


def currents(v, c, d, f, n, r):
    q = rise(c)
    calcium_flow = 1.2 * d * f * (v - 2.0)
    return q, calcium_flow, calcium_flow + (0.8 * n + 0.6 * q * r) * (v + 1.0) + 0.1 * v


def in_three(values):
    high = values.astype(jnp.bfloat16).astype(F32)
    mid = (values - high).astype(jnp.bfloat16).astype(F32)
    return jnp.concatenate([high, mid, values - high - mid], axis=0)


def tie_rows(listed, stiff, u):
    rows, depth = u[0].shape
    joined = in_three(jnp.concatenate([2.0 * stiff * w for w in u], axis=1))
    pick = (lax.broadcasted_iota(jnp.int32, (rows, rows), 0).astype(F32) == listed).astype(F32)
    moved = lax.dot_general(
        jnp.concatenate([pick] * 3, axis=0), joined, (((0,), (0,)), ((), ())), preferred_element_type=F32
    )
    return [moved[:, a * depth : (a + 1) * depth] for a in range(3)]


def put_ends(ends, a, x, value):
    rows, row = value.shape[0], 2 * (a * (ends.shape[0] // 6) + x)
    ends[pl.ds(row, 1), :] = value[0:1]
    ends[pl.ds(row + 1, 1), :] = value[rows - 1 : rows]


def fill_sides(pad, a, x, ends, k, size_y):
    row = 2 * (a * (ends.shape[0] // 6) + k)
    pad[a, x, PAD - 1 : PAD, :] = ends[pl.ds(row + 1, 1), :]
    pad[a, x, PAD + size_y : PAD + size_y + 1, :] = ends[pl.ds(row, 1), :]


def side_rows(ends, a, x):
    row = 2 * (a * (ends.shape[0] // 6) + x)
    return ends[row + 1 : row + 2, :], ends[row : row + 1, :]


def sides(size_x):
    return (0, 0, -1.0), (size_x + 1, size_x - 1, 1.0)


def place_of(x, size_y):
    return pl.ds(pl.multiple_of(x * size_y, size_y), size_y)


def electric():
    return lax.axis_index("sec") == 0


def fiber_table(angles, blocks):
    classes, depth = angles.shape[1], CELLS * blocks
    azimuth, elevation = angles[0:1, :], angles[1:2, :]
    flat_part = jnp.cos(elevation)
    fib = [jnp.cos(azimuth) * flat_part, jnp.sin(azimuth) * flat_part, jnp.sin(elevation)]
    own = lax.broadcasted_iota(jnp.int32, (blocks, depth), 1) // CELLS
    own = own == lax.broadcasted_iota(jnp.int32, (blocks, depth), 0)
    return in_three(
        jnp.concatenate(
            [
                jnp.concatenate(
                    [jnp.where(own, jnp.broadcast_to(w[:, k : k + 1], own.shape), 0.0) for w in fib], axis=1
                )
                for k in range(classes)
            ],
            axis=0,
        )
    )


def fiber_fields(table, cls):
    classes = table.shape[0] // (3 * cls.shape[0])
    hits = jnp.concatenate([(cls == k).astype(F32) for k in range(classes)] * 3, axis=0)
    return lax.dot_general(hits, table, (((0,), (0,)), ((), ())), preferred_element_type=F32)


def all_fibers(table_ref, cls_ref, flat, fib_ref):
    size_x, _, size_y = cls_ref.shape
    depth = fib_ref.shape[2]
    for x in range(size_x):
        flat[:, x * size_y : (x + 1) * size_y] = cls_ref[x]
    found = fiber_fields(table_ref[...], flat[...])
    for a in range(3):
        fib_ref[a] = found[:, a * depth : (a + 1) * depth]


def tension_kernel(
    sec_hbm, map_hbm, list_hbm, ang_hbm, plain, edge_ten, list_ref, table_ref, main, gate, late, ang_ref, map_ref, sems
):
    size_x, size_y = sec_hbm.shape[1], sec_hbm.shape[2]
    pieces = (sems.shape[0] - 3) // 3
    chunk = size_x // pieces

    def plane(x, carry):
        v, c, d, f, bound, s = main[0, x], main[1, x], main[2, x], gate[0, x], late[0, x], late[1, x]
        calcium_flow = 1.2 * d * f * (v - 2.0)
        flow = 2.0 * c * (1.0 - bound) - 0.4 * bound
        c1 = c + DT * (-0.3 * calcium_flow - 0.5 * c - flow)
        s1 = s + (0.5 * DT) * (rise(c) - s)
        plain[place_of(x, size_y), :] = s1 + (0.5 * DT) * (rise(c1) - s1)
        return carry

    @pl.when(electric())
    def _():
        small = [
            pltpu.make_async_copy(src, dst, sems.at[i])
            for i, (src, dst) in enumerate(((ang_hbm, ang_ref), (map_hbm, map_ref), (list_hbm, list_ref)))
        ]
        small[0].start()
        copies = []
        for i in range(pieces):
            here = pl.ds(i * chunk, chunk)
            copies.append(
                [
                    pltpu.make_async_copy(sec_hbm.at[src, here], dst.at[:, here], sems.at[3 + 3 * i + k])
                    for k, (src, dst) in enumerate(
                        ((pl.ds(0, 3), main), (pl.ds(3, 1), gate), (pl.ds(6, 2), late))
                    )
                ]
            )
            for copy in copies[-1]:
                copy.start()
        for copy in small[1:]:
            copy.start()
        small[0].wait()
        table_ref[...] = fiber_table(ang_ref[...], main.shape[3] // CELLS)
        for i in range(pieces):
            for copy in copies[i]:
                copy.wait()
            lax.fori_loop(i * chunk, (i + 1) * chunk, plane, 0, unroll=2)
        for copy in small[1:]:
            copy.wait()
        last = (size_x - 1) * size_y
        for p in range(size_y):
            edge_ten[0, p : p + 1, :] = plain[pl.ds(map_ref[p], 1), :]
            edge_ten[1, p : p + 1, :] = plain[pl.ds(map_ref[last + p], 1), :]


def share_kernel(own, after, pad, share):
    size_x, size_y = own.shape[1], own.shape[2]
    zeros = jnp.zeros(pad.shape[2:], F32)
    for a in range(3):
        pad[a, 0] = zeros
        pad[a, size_x + 1] = zeros

    def plane(x, carry):
        for a in range(3):
            value = own[a, x]
            pad[a, x + 1, PAD : PAD + size_y, :] = value
            put_ends(share, a, x, value)
        return carry

    lax.fori_loop(0, size_x, plane, 0, unroll=4)


def gather_kernel(plain, list_ref, after, all_ref):
    @pl.when(electric())
    def _():
        columns, depth = plain.shape
        pick = (lax.broadcasted_iota(jnp.int32, (columns, columns), 0) == list_ref[...]).astype(F32)
        values = plain[...]
        high = values.astype(jnp.bfloat16).astype(F32)
        mid = (values - high).astype(jnp.bfloat16).astype(F32)
        moved = lax.dot_general(
            pick,
            jnp.concatenate([high, mid, values - high - mid], axis=1),
            (((0,), (0,)), ((), ())),
            preferred_element_type=F32,
        )
        all_ref[...] = moved[:, :depth] + moved[:, depth : 2 * depth] + moved[:, 2 * depth :]


def edge_kernel(table_in, cls_ref, ang_ref, after, list_ref, edge_fib, table_ref, flat):
    size_x, blocks, size_y = cls_ref.shape

    @pl.when(jnp.logical_not(electric()))
    def _():
        table_ref[...] = fiber_table(ang_ref[...], blocks)

    for which, (_, edge, _) in enumerate(sides(size_x)):
        flat[:, which * size_y : (which + 1) * size_y] = cls_ref[edge]
    edge_fib[...] = fiber_fields(table_ref[...], flat[...])


def message_electric(pad_in, own, side_ref, edge_fib, high_ref, low_ref, pad):
    size_x, size_y = own.shape[1], own.shape[2]

    def fill(x, carry):
        for a in range(3):
            fill_sides(pad, a, x + 1, side_ref, x, size_y)
        return carry

    lax.fori_loop(0, size_x, fill, 0, unroll=4)

    @pl.when(electric())
    def _():
        for which, ((_, edge, _), out) in enumerate(zip(sides(size_x), (low_ref, high_ref))):
            below, above = side_rows(side_ref, 0, edge)
            out[ROW_VOLT_SIDE : ROW_VOLT_SIDE + 1, :] = below
            out[ROW_VOLT_SIDE + 1 : ROW_VOLT_SIDE + 2, :] = above
            rows, depth = slice(which * size_y, (which + 1) * size_y), own.shape[3]
            fib = [edge_fib[rows, a * depth : (a + 1) * depth] for a in range(3)]
            v, c, d = [rows_of(pad, a, edge + 1, size_y) for a in range(3)]
            f, n, r = [own[k, edge] for k in range(3, 6)]
            rate = volt_rate(pad, edge + 1, fib, size_y)
            _, _, total = currents(v, c, d, f, n, r)
            out[ROW_VOLT : ROW_VOLT + size_y, :] = v
            out[ROW_VOLT_NEXT : ROW_VOLT_NEXT + size_y, :] = v + DT * (rate - total)
            for k, value in enumerate(couplings(fib)):
                out[ROW_COUPLED + k * size_y : ROW_COUPLED + (k + 1) * size_y, :] = value

def message_mechanic(pad_in, own, side_ref, edge_fib, ten_ref, list_ref, high_ref, low_ref, pad):
    size_x, size_y = own.shape[1], own.shape[2]

    @pl.when(jnp.logical_not(electric()))
    def _():
        depth = own.shape[3]
        for which, ((_, edge, _), out) in enumerate(zip(sides(size_x), (low_ref, high_ref))):
            out[ROW_LIST : ROW_LIST + 1, 0:size_y] = list_ref[which].astype(F32)
            rate = motion_rate(pad, edge + 1, size_y)
            stiff = own[6, edge]
            beta = OMEGA * inverse(stiff)
            act = own[7, edge] * ten_ref[which]
            out[ROW_STIFF : ROW_STIFF + size_y, :] = stiff
            for a in range(3):
                row = ROW_SIDE + 2 * a
                out[row : row + 1, :], out[row + 1 : row + 2, :] = side_rows(side_ref, a, edge)
                u = rows_of(pad, a, edge + 1, size_y)
                out[ROW_NOW + a * size_y : ROW_NOW + (a + 1) * size_y, :] = u
                drive = own[3 + a, edge] + act * edge_fib[which * size_y : (which + 1) * size_y, a * depth : (a + 1) * depth]
                out[ROW_NEXT + a * size_y : ROW_NEXT + (a + 1) * size_y, :] = (
                    0.28 * u + beta * drive + OMEGA * rate[a]
                )


def put_inner(next_pad, share, a, x, value):
    next_pad[a, x, PAD : PAD + value.shape[0], :] = value
    put_ends(share, a, x, value)


def inner_electric(
    pad, own, plain, cls_ref, table_ref, next_pad, share, keep, out_hbm, fib_ref, flat, sems
):
    size_x, size_y = own.shape[1], own.shape[2]

    all_fibers(table_ref, cls_ref, flat, fib_ref)

    @pl.when(electric())
    def _():
        copies = [
            pltpu.make_async_copy(plain.at[x * size_y : (x + 1) * size_y], out_hbm.at[0, 3, x], sems.at[x])
            for x in range(size_x)
        ]
        for copy in copies:
            copy.start()

        def plane(x, carry):
            place = place_of(x, size_y)
            v, c, d = [rows_of(pad, a, x + 1, size_y) for a in range(3)]
            f, n, r, bound, _ = [own[k, x] for k in range(3, 8)]
            rate = volt_rate(pad, x + 1, [fib_ref[a, place, :] for a in range(3)], size_y)
            q, calcium_flow, total = currents(v, c, d, f, n, r)
            flow = 2.0 * c * (1.0 - bound) - 0.4 * bound
            put_inner(next_pad, share, 0, x + 1, v + DT * (rate - total))
            c1 = c + DT * (-0.3 * calcium_flow - 0.5 * c - flow)
            tv = jnp.tanh(v)
            d1 = (1.0 - 2.0 * DT) * d + DT * (1.0 + jnp.tanh(v + 0.5))
            f1 = (1.0 - DT / 3.0) * f + (DT / 6.0) * (1.0 - tv)
            n1 = (1.0 - DT) * n + (0.5 * DT) * (1.0 + tv)
            r1 = (1.0 - DT / 5.0) * r + (DT / 10.0) * (1.0 + jnp.tanh(0.5 * v - 0.25))
            bound1 = bound + DT * flow
            flow1 = 2.0 * c1 * (1.0 - bound1) - 0.4 * bound1
            keep[0, x] = n1
            keep[1, x] = 1.2 * d1 * f1
            keep[2, x] = 0.8 * n1 + 0.6 * rise(c1) * r1
            keep[3, x] = c1 - DT * (0.5 * c1 + flow1)
            return carry

        lax.fori_loop(0, size_x, plane, 0, unroll=2)
        for copy in copies:
            copy.wait()


def inner_mechanic(pad, own, fib_ref, ten_ref, next_in, share_in, keep_in, next_pad, share, keep):
    size_x, size_y = own.shape[1], own.shape[2]

    @pl.when(jnp.logical_not(electric()))
    def _():
        def plane(x, carry):
            place = place_of(x, size_y)
            rate = motion_rate(pad, x + 1, size_y)
            beta = OMEGA * inverse(own[6, x])
            act = own[7, x] * ten_ref[place, :]
            keep[3, x] = act
            for a in range(3):
                drive = beta * (own[3 + a, x] + act * fib_ref[a, place, :])
                keep[a, x] = drive
                value = 0.4 * rows_of(pad, a, x + 1, size_y) + drive + OMEGA * rate[a]
                put_inner(next_pad, share, a, x + 1, value)
            return carry

        lax.fori_loop(0, size_x, plane, 0, unroll=2)


def outer_electric(pad, own, fib_ref, volt_low, volt_high, next_in, next_pad, share, wide):
    size_x, size_y = own.shape[1], own.shape[2]
    def put(a, x, slot, value):
        next_pad[a, x, PAD : PAD + size_y, :] = value
        put_ends(share, a, slot, value)

    def put_side(a, which, low, high):
        wide[a, which, PAD - 1 : PAD, :] = low
        wide[a, which, PAD + size_y : PAD + size_y + 1, :] = high

    @pl.when(electric())
    def _():
        for which, ((halo, edge, sign), got) in enumerate(zip(sides(size_x), (volt_low, volt_high))):
            wide[0, which, PAD : PAD + size_y, :] = got[ROW_VOLT : ROW_VOLT + size_y, :]
            row = ROW_VOLT_SIDE
            put_side(0, which, got[row : row + 1, :], got[row + 1 : row + 2, :])
            fib = [fib_ref[a, place_of(edge, size_y), :] for a in range(3)]
            put(
                0,
                edge + 1,
                1 + which,
                rows_of(next_pad, 0, edge + 1, size_y) + DT * volt_from(wide, which, couplings(fib), sign, size_y),
            )
            theirs = [got[ROW_COUPLED + k * size_y : ROW_COUPLED + (k + 1) * size_y, :] for k in range(3)]
            put(
                0,
                halo,
                3 * which,
                got[ROW_VOLT_NEXT : ROW_VOLT_NEXT + size_y, :] + DT * volt_from(pad, edge + 1, theirs, -sign, size_y),
            )


def outer_mechanic(which, pad, own, list_ref, got, next_in, share_in, next_pad, share, wide):
    size_x, size_y = own.shape[1], own.shape[2]
    def put(a, x, slot, value):
        next_pad[a, x, PAD : PAD + size_y, :] = value
        put_ends(share, a, slot, value)

    def put_side(a, which, low, high):
        wide[a, which, PAD - 1 : PAD, :] = low
        wide[a, which, PAD + size_y : PAD + size_y + 1, :] = high

    @pl.when(jnp.logical_not(electric()))
    def _():
        halo, edge, sign = sides(size_x)[which]
        for a in range(3):
            wide[a, which, PAD : PAD + size_y, :] = got[ROW_NOW + a * size_y : ROW_NOW + (a + 1) * size_y, :]
            row = ROW_SIDE + 2 * a
            put_side(a, which, got[row : row + 1, :], got[row + 1 : row + 2, :])
        stiff = got[ROW_STIFF : ROW_STIFF + size_y, :]
        stiff_own = own[6, edge]
        now = [rows_of(pad, a, edge + 1, size_y) for a in range(3)]
        theirs = [rows_of(wide, a, which, size_y) for a in range(3)]
        ties = tie_rows(list_ref[which].astype(F32), stiff, theirs)
        rate = motion_from(wide, which, sign, size_y)
        beta = OMEGA * inverse(stiff_own)
        for a in range(3):
            put(
                a,
                edge + 1,
                1 + which,
                rows_of(next_pad, a, edge + 1, size_y) + OMEGA * rate[a] + beta * ties[a] - 0.12 * now[a],
            )
        ties = tie_rows(got[ROW_LIST : ROW_LIST + 1, 0:size_y], stiff_own, now)
        rate = motion_from(pad, edge + 1, -sign, size_y)
        beta = OMEGA * inverse(stiff)
        for a in range(3):
            put(
                a,
                halo,
                3 * which,
                got[ROW_NEXT + a * size_y : ROW_NEXT + (a + 1) * size_y, :] + OMEGA * rate[a] + beta * ties[a],
            )


def electric_end(x, next_pad, fib_ref):
    size_y = next_pad.shape[2] - 2 * PAD
    place = place_of(x, size_y)
    return rows_of(next_pad, 0, x + 1, size_y) + DT * volt_rate(
        next_pad, x + 1, [fib_ref[a, place, :] for a in range(3)], size_y
    )


def electric_rest(x, next_pad, keep, out):
    size_y = next_pad.shape[2] - 2 * PAD
    v = rows_of(next_pad, 0, x + 1, size_y)
    n, gate, leak, rest_c = [keep[k, x] for k in range(4)]
    flow = gate * (v - 2.0)
    out[0, x] = -DT * (flow + leak * (v + 1.0) + 0.1 * v)
    out[1, x] = rest_c - (0.3 * DT) * flow
    out[2, x] = (1.0 - DT) * n + (0.5 * DT) * (1.0 + jnp.tanh(v))


def mechanic_end(x, next_pad, keep, size_y):
    rate = motion_rate(next_pad, x + 1, size_y)
    return [
        0.4 * rows_of(next_pad, a, x + 1, size_y) + keep[a, x] + OMEGA * rate[a] for a in range(3)
    ]


def middle_kernel(
    fib_ref, own, list_ref, got_low, got_high, next_in, side_ref, keep, out_in,
    out_hbm, next_pad, held, final, out, sems
):
    size_x = keep.shape[1]
    size_y = fib_ref.shape[1] // size_x
    pieces = sems.shape[0]
    chunk = final.shape[1]

    def copy_out(i, fields):
        here = pl.ds(2 + i * chunk, chunk)
        return pltpu.make_async_copy(out.at[0:fields, here], out_hbm.at[0, 0:fields, here], sems.at[i])

    def fill(count):
        def one(x, carry):
            for a in range(count):
                fill_sides(next_pad, a, x, side_ref, x, size_y)
            return carry

        lax.fori_loop(2, size_x, one, 0, unroll=2)

    @pl.when(electric())
    def _():
        fill(1)

        def rest(x, carry):
            electric_rest(x, next_pad, keep, out)
            return carry

        lax.fori_loop(0, size_x, rest, 0, unroll=2)
        copy = pltpu.make_async_copy(out.at[1:3], out_hbm.at[0, 1:3], sems.at[pieces - 1])
        copy.start()
        for i, x in enumerate((0, 1, size_x - 2, size_x - 1)):
            held[i] = out[0, x]

        def step(i, carry):
            for k in range(chunk):
                x = 2 + i * chunk + k
                out[0, x] = out[0, x] + electric_end(x, next_pad, fib_ref)
            copy_out(i, 1).start()
            return carry

        lax.fori_loop(0, pieces - 1, step, 0)
        for k in range(chunk):
            x = size_x - 2 - chunk + k
            final[0, k] = out[0, x] + electric_end(x, next_pad, fib_ref)
        copy.wait()
        for i in range(pieces - 1):
            copy_out(i, 1).wait()

    @pl.when(jnp.logical_not(electric()))
    def _():
        fill(3)
        copy = pltpu.make_async_copy(keep.at[3:4], out_hbm.at[0, 3:4], sems.at[pieces - 1])
        copy.start()

        def sweep(i, carry):
            for k in range(chunk):
                x = 2 + i * chunk + k
                for a, value in enumerate(mechanic_end(x, next_pad, keep, size_y)):
                    out[a, x] = value
            copy_out(i, 3).start()
            return carry

        lax.fori_loop(0, pieces - 1, sweep, 0)
        for which, ((halo, edge, _), got) in enumerate(zip(sides(size_x), (got_low, got_high))):
            beta = OMEGA * inverse(own[6, edge])
            ties = tie_rows(
                list_ref[which].astype(F32),
                got[ROW_STIFF : ROW_STIFF + size_y, :],
                [rows_of(next_pad, a, halo, size_y) for a in range(3)],
            )
            for a in range(3):
                held[3 * which + a] = beta * ties[a] - 0.12 * rows_of(next_pad, a, edge + 1, size_y)
        for k in range(chunk):
            for a, value in enumerate(mechanic_end(size_x - 2 - chunk + k, next_pad, keep, size_y)):
                final[a, k] = value
        copy.wait()
        for i in range(pieces - 1):
            copy_out(i, 3).wait()


def last_kernel(
    fib_ref, next_in, side_ref, keep, held, final, out_in, out_hbm, next_pad, out, sems
):
    size_x = keep.shape[1]
    size_y = fib_ref.shape[1] // size_x

    def copy_out(which, first, fields):
        here = pl.ds(first, 2)
        return pltpu.make_async_copy(out.at[0:fields, here], out_hbm.at[0, 0:fields, here], sems.at[which])

    def copy_final(fields):
        here = pl.ds(size_x - 2 - final.shape[1], final.shape[1])
        return pltpu.make_async_copy(final.at[0:fields], out_hbm.at[0, 0:fields, here], sems.at[2])

    work = []
    for which, (halo, edge, _) in enumerate(sides(size_x)):
        near = abs(edge - 1)
        work.append((halo, edge, near, which, min(edge, near)))

    @pl.when(electric())
    def _():
        copy_final(1).start()
        for halo, edge, near, which, first in work:
            fill_sides(next_pad, 0, halo, side_ref, 3 * which, size_y)
            fill_sides(next_pad, 0, edge + 1, side_ref, 1 + which, size_y)
            for x in (near, edge):
                out[0, x] = held[2 * which + x - first] + electric_end(x, next_pad, fib_ref)
            copy_out(which, first, 1).start()
        for item in work:
            copy_out(item[3], item[-1], 1).wait()
        copy_final(1).wait()

    @pl.when(jnp.logical_not(electric()))
    def _():
        copy_final(3).start()
        for halo, edge, near, which, first in work:
            for a in range(3):
                fill_sides(next_pad, a, halo, side_ref, 3 * which, size_y)
                fill_sides(next_pad, a, edge + 1, side_ref, 1 + which, size_y)
            for a, value in enumerate(mechanic_end(near, next_pad, keep, size_y)):
                out[a, near] = value
            for a, value in enumerate(mechanic_end(edge, next_pad, keep, size_y)):
                out[a, edge] = value + held[3 * which + a]
            copy_out(which, first, 3).start()
        for item in work:
            copy_out(item[3], item[-1], 3).wait()
        copy_final(3).wait()


def call(kernel, name, out_shape, operands, spaces, scratch=(), out_spaces=None, aliases=()):
    if out_spaces is None:
        out_spaces = [pltpu.VMEM] * len(out_shape)
    return pl.pallas_call(
        kernel,
        name=name,
        out_shape=tuple(out_shape),
        in_specs=[pl.BlockSpec(memory_space=space) for space in spaces],
        out_specs=tuple(pl.BlockSpec(memory_space=space) for space in out_spaces),
        scratch_shapes=scratch,
        input_output_aliases=dict(aliases),
        cost_estimate=pl.CostEstimate(
            flops=int(COST[name] * 10**10), bytes_accessed=int(COST[name] * 10**7), transcendentals=0
        ),
        compiler_params=pltpu.CompilerParams(vmem_limit_bytes=VMEM_LIMIT),
    )(*operands)


def local(sections, fiber_angles, fiber_class, row_map, interface_rows):
    own = sections[0]
    channels, size_x, size_y, depth = own.shape
    n_gx = lax.axis_size("gx")
    n_gy = lax.axis_size("gy")
    assert lax.axis_size("sec") == 2 and n_gy == 2
    axes = ("sec", "gx", "gy")
    place = lambda sec, i, j: (sec * n_gx + i % n_gx) * n_gy + j
    blocks = [(i, j) for i in range(n_gx) for j in range(n_gy)]

    def ring(section, step):
        return [(place(section, i, j), place(section, i + step, j)) for i, j in blocks] + [
            (place(1 - section, i, j), place(1 - section, i, 1 - j)) for i, j in blocks
        ]

    both = [(0, 1), (1, 0)]
    S, V, H = pltpu.SMEM, pltpu.VMEM, pltpu.HBM
    f32 = lambda *shape: jax.ShapeDtypeStruct(shape, F32)
    hbm = lambda w: pltpu.with_memory_space_constraint(w, H)
    columns = size_x * size_y
    ends = lambda planes: f32(6 * planes, depth)
    padded = f32(3, size_x + 2, size_y + 2 * PAD, depth)
    classes = fiber_class.transpose(0, 2, 1)
    lists = interface_rows.reshape(2, 1, size_y)
    places = row_map.reshape(-1)

    field = lambda n: pltpu.VMEM((n, size_x, size_y, depth), F32)
    flat = lambda count: pltpu.VMEM((classes.shape[1], count), jnp.int32)
    angles = fiber_angles.T
    plain, edge_ten, own_list, table = call(
        tension_kernel,
        "tension",
        (
            f32(columns, depth),
            f32(2, size_y, depth),
            jax.ShapeDtypeStruct((1, columns), jnp.int32),
            f32(3 * fiber_angles.shape[0] * classes.shape[1], 3 * depth),
        ),
        (hbm(own), hbm(places), hbm(row_map.reshape(1, columns)), hbm(angles)),
        (H,) * 4,
        [
            field(3),
            field(1),
            field(2),
            pltpu.VMEM(angles.shape, F32),
            pltpu.SMEM((columns,), jnp.int32),
            pltpu.SemaphoreType.DMA((3 + 3 * 4,)),
        ],
    )
    edge_ten = lax.ppermute(edge_ten, "sec", both)
    pad, share = call(share_kernel, "share", (padded, ends(size_x)), (own, plain), (V, V))
    side = lax.ppermute(share, "gy", both)
    result = f32(1, 4, size_x, size_y, depth)
    (gathered,) = call(gather_kernel, "gather", (f32(columns, depth),), (plain, own_list, share), (V,) * 3)
    edge_fib, table = call(
        edge_kernel,
        "edge",
        (f32(2 * size_y, 3 * depth), f32(*table.shape)),
        (table, classes, angles, gathered, lists),
        (V,) * 5,
        [flat(2 * size_y)],
        aliases={0: 1},
    )
    tension = lax.ppermute(gathered, "sec", both)
    assert depth == CELLS * classes.shape[1]
    message = f32(VOLT_ROWS, depth)
    high, low, pad = call(
        message_electric,
        "message_electric",
        (message, message, padded),
        (pad, own, side, edge_fib),
        (V,) * 4,
        aliases={0: 2},
    )
    volt_low = lax.ppermute(high, axes, ring(0, 1))
    volt_high = lax.ppermute(low, axes, ring(0, -1))
    message = f32(MESSAGE_ROWS, depth)
    high, low, pad = call(
        message_mechanic,
        "message_mechanic",
        (message, message, padded),
        (pad, own, side, edge_fib, edge_ten, lists),
        (V,) * 6,
        aliases={0: 2},
    )
    got_low = lax.ppermute(high, axes, ring(1, 1))
    got_high = lax.ppermute(low, axes, ring(1, -1))
    moved, share, keep, result, fib = call(
        inner_electric,
        "inner_electric",
        (padded, ends(size_x + 2), f32(4, size_x, size_y, depth), result, f32(3, columns, depth)),
        (pad, own, plain, classes, table),
        (V,) * 5,
        [flat(columns), pltpu.SemaphoreType.DMA((size_x,))],
        out_spaces=(V, V, V, H, V),
    )
    moved, share, keep = call(
        inner_mechanic,
        "inner_mechanic",
        (padded, ends(size_x + 2), f32(4, size_x, size_y, depth)),
        (pad, own, fib, tension, moved, share, keep),
        (V,) * 7,
        aliases={4: 0, 5: 1, 6: 2},
    )
    side = lax.ppermute(share, "gy", both)
    wide = pltpu.VMEM((3, 2) + padded.shape[2:], F32)
    moved, share = call(
        outer_electric,
        "outer_electric",
        (padded, ends(4)),
        (pad, own, fib, volt_low, volt_high, moved),
        (V,) * 6,
        [wide],
        aliases={5: 0},
    )
    for which, got in enumerate((got_low, got_high)):
        moved, share = call(
            functools.partial(outer_mechanic, which),
            ("outer_low", "outer_high")[which],
            (padded, ends(4)),
            (pad, own, lists, got, moved, share),
            (V,) * 6,
            [wide],
            aliases={4: 0, 5: 1},
        )
    end_side = lax.ppermute(share, "gy", both)
    fields = pltpu.VMEM((3, size_x, size_y, depth), F32)
    pieces = 3
    chunk = (size_x - 4) // pieces
    result, moved, held, final = call(
        middle_kernel,
        "middle",
        (f32(1, 4, size_x, size_y, depth), padded, f32(6, size_y, depth), f32(3, chunk, size_y, depth)),
        (fib, own, lists, got_low, got_high, moved, side, keep, result),
        (V,) * 8 + (H,),
        [fields, pltpu.SemaphoreType.DMA((pieces,))],
        out_spaces=(H, V, V, V),
        aliases={5: 1, 8: 0},
    )
    return call(
        last_kernel,
        "last",
        (f32(1, 4, size_x, size_y, depth), padded),
        (fib, moved, end_side, keep, held, final, result),
        (V,) * 6 + (H,),
        [fields, pltpu.SemaphoreType.DMA((3,))],
        out_spaces=(H, V),
        aliases={1: 1, 6: 0},
    )[0]


def solution(mesh):
    in_specs = (
        P("sec", None, "gx", "gy", None),
        P(),
        P("gx", "gy", None),
        P("gx", "gy", None),
        P(None, "gx", "gy", None),
    )
    out_specs = P("sec", None, "gx", "gy", None)
    return jax.shard_map(local, mesh=mesh, in_specs=in_specs, out_specs=out_specs, check_vma=False)
```

```python
import functools

import jax
import jax.numpy as jnp
from jax import lax
from jax.experimental import pallas as pl
from jax.experimental.pallas import tpu as pltpu
from jax.sharding import PartitionSpec as P

DT = 0.1
OMEGA = 0.06
F32 = jnp.float32
VMEM_LIMIT = 16 * 1024 * 1024
COST = {
    "tension": 0.001,
    "share": 0.001,
    "gather": 6,
    "edge": 1,
    "message_electric": 1,
    "message_mechanic": 1,
    "inner_electric": 6,
    "inner_mechanic": 6,
    "outer_electric": 1,
    "outer_low": 0.01,
    "outer_high": 1,
    "middle": 6,
    "last": 1,
}

CELLS = 16

PAD = 8

ROW_NOW, ROW_NEXT, ROW_STIFF, ROW_SIDE = 0, 96, 192, 224
ROW_LIST = ROW_SIDE + 6
MESSAGE_ROWS = 232
ROW_VOLT, ROW_VOLT_NEXT, ROW_COUPLED, ROW_VOLT_SIDE = 0, 32, 64, 160
VOLT_ROWS = 168


def inverse(v):
    r = pl.reciprocal(v, approx=True)
    return r * (2.0 - v * r)


def rise(c):
    c2 = c * c
    return c2 * inverse(c2 + 0.25)


def ends(like):
    lane = lax.broadcasted_iota(jnp.int32, like, 1)
    return lane == like[1] - 1, lane == 0


def up_z(w, last):
    return jnp.where(last, 0.0, pltpu.roll(w, w.shape[1] - 1, 1))


def down_z(w, first):
    return jnp.where(first, 0.0, pltpu.roll(w, 1, 1))


def rows_of(pad, a, x, size_y, shift=0):
    return pad[a, x, PAD + shift : PAD + shift + size_y, :]


def motion_rate(pad, x, size_y):
    at = lambda a, dx=0, dy=0: rows_of(pad, a, x + dx, size_y, dy)
    u0, u1, u2 = at(0), at(1), at(2)
    last, first = ends(u0.shape)
    w0p, w0m, w1p, w1m = at(0, 1), at(0, -1), at(1, 1), at(1, -1)
    w2p, w2m = at(2, 1), at(2, -1)
    e0, e2 = 0.5 * (w0p - w0m), 0.5 * (w2p - w2m)
    e0y = (at(0, 1, 1) - at(0, -1, 1)) - (at(0, 1, -1) - at(0, -1, -1))
    e1y = (at(1, 1, 1) - at(1, -1, 1)) - (at(1, 1, -1) - at(1, -1, -1))
    v1p, v1m, v2p, v2m = at(1, 0, 1), at(1, 0, -1), at(2, 0, 1), at(2, 0, -1)
    d2 = 0.5 * (v2p - v2m)
    d1 = 0.5 * (v1p - v1m) + e0
    r0 = (
        up_z(u0 + e2, last) + down_z(u0 - e2, first)
        + (at(0, 0, 1) + at(0, 0, -1)) + 0.5 * e1y + 3.0 * (w0p + w0m)
    )
    r1 = (
        up_z(u1 + d2, last) + down_z(u1 - d2, first)
        + 3.0 * (v1p + v1m) + 0.5 * e0y + (w1p + w1m)
    )
    t2 = 3.0 * u2
    r2 = up_z(t2 + d1, last) + down_z(t2 - d1, first) + (v2p + v2m) + (w2p + w2m)
    return r0, r1, r2


def motion_from(pad, x, sign, size_y):
    u0, u1, u2 = [rows_of(pad, a, x, size_y) for a in range(3)]
    last, first = ends(u0.shape)
    half = 0.5 * sign
    dy0 = rows_of(pad, 0, x, size_y, 1) - rows_of(pad, 0, x, size_y, -1)
    dy1 = rows_of(pad, 1, x, size_y, 1) - rows_of(pad, 1, x, size_y, -1)
    dz0 = up_z(u0, last) - down_z(u0, first)
    dz2 = up_z(u2, last) - down_z(u2, first)
    return 3.0 * u0 + half * (dy1 + dz2), u1 + half * dy0, u2 + half * dz0


def volt_rate(pad, x, fib, size_y):
    at = lambda dx=0, dy=0: rows_of(pad, 0, x + dx, size_y, dy)
    v, wp, wm, yp, ym = at(), at(1), at(-1), at(0, 1), at(0, -1)
    last, first = ends(v.shape)
    e = wp - wm
    ey = (at(1, 1) - at(-1, 1)) - (at(1, -1) - at(-1, -1))
    dy = yp - ym
    sum_z = up_z(v, last) + down_z(v, first)
    ez = up_z(e, last) - down_z(e, first)
    dyz = up_z(dy, last) - down_z(dy, first)
    g = [0.75 * w for w in fib]
    d00, d11, d22 = [0.25 + a * b for a, b in zip(g, fib)]
    return (
        d00 * (wp + wm) + d11 * (yp + ym) + d22 * sum_z - 2.0 * (d00 + d11 + d22) * v
        + 0.5 * (fib[0] * (g[1] * ey + g[2] * ez) + g[1] * fib[2] * dyz)
    )


def couplings(fib):
    g = 0.75 * fib[0]
    return 0.25 + g * fib[0], 0.5 * g * fib[1], 0.5 * g * fib[2]


def volt_from(pad, x, coupled, sign, size_y):
    v = rows_of(pad, 0, x, size_y)
    last, first = ends(v.shape)
    dy = rows_of(pad, 0, x, size_y, 1) - rows_of(pad, 0, x, size_y, -1)
    dz = up_z(v, last) - down_z(v, first)
    return coupled[0] * v + sign * (coupled[1] * dy + coupled[2] * dz)


def currents(v, c, d, f, n, r):
    q = rise(c)
    calcium_flow = 1.2 * d * f * (v - 2.0)
    return q, calcium_flow, calcium_flow + (0.8 * n + 0.6 * q * r) * (v + 1.0) + 0.1 * v


def in_three(values):
    high = values.astype(jnp.bfloat16).astype(F32)
    mid = (values - high).astype(jnp.bfloat16).astype(F32)
    return jnp.concatenate([high, mid, values - high - mid], axis=0)


def tie_rows(listed, stiff, u):
    rows, depth = u[0].shape
    joined = in_three(jnp.concatenate([2.0 * stiff * w for w in u], axis=1))
    pick = (lax.broadcasted_iota(jnp.int32, (rows, rows), 0).astype(F32) == listed).astype(F32)
    moved = lax.dot_general(
        jnp.concatenate([pick] * 3, axis=0), joined, (((0,), (0,)), ((), ())), preferred_element_type=F32
    )
    return [moved[:, a * depth : (a + 1) * depth] for a in range(3)]


def put_ends(ends, a, x, value):
    rows, row = value.shape[0], 2 * (a * (ends.shape[0] // 6) + x)
    ends[pl.ds(row, 1), :] = value[0:1]
    ends[pl.ds(row + 1, 1), :] = value[rows - 1 : rows]


def fill_sides(pad, a, x, ends, k, size_y):
    row = 2 * (a * (ends.shape[0] // 6) + k)
    pad[a, x, PAD - 1 : PAD, :] = ends[pl.ds(row + 1, 1), :]
    pad[a, x, PAD + size_y : PAD + size_y + 1, :] = ends[pl.ds(row, 1), :]


def side_rows(ends, a, x):
    row = 2 * (a * (ends.shape[0] // 6) + x)
    return ends[row + 1 : row + 2, :], ends[row : row + 1, :]


def sides(size_x):
    return (0, 0, -1.0), (size_x + 1, size_x - 1, 1.0)


def place_of(x, size_y):
    return pl.ds(pl.multiple_of(x * size_y, size_y), size_y)


def electric():
    return lax.axis_index("sec") == 0


def fiber_table(angles, blocks):
    classes, depth = angles.shape[1], CELLS * blocks
    azimuth, elevation = angles[0:1, :], angles[1:2, :]
    flat_part = jnp.cos(elevation)
    fib = [jnp.cos(azimuth) * flat_part, jnp.sin(azimuth) * flat_part, jnp.sin(elevation)]
    own = lax.broadcasted_iota(jnp.int32, (blocks, depth), 1) // CELLS
    own = own == lax.broadcasted_iota(jnp.int32, (blocks, depth), 0)
    return in_three(
        jnp.concatenate(
            [
                jnp.concatenate(
                    [jnp.where(own, jnp.broadcast_to(w[:, k : k + 1], own.shape), 0.0) for w in fib], axis=1
                )
                for k in range(classes)
            ],
            axis=0,
        )
    )


def fiber_fields(table, cls):
    classes = table.shape[0] // (3 * cls.shape[0])
    hits = jnp.concatenate([(cls == k).astype(F32) for k in range(classes)] * 3, axis=0)
    return lax.dot_general(hits, table, (((0,), (0,)), ((), ())), preferred_element_type=F32)


def all_fibers(table_ref, cls_ref, flat, fib_ref):
    size_x, _, size_y = cls_ref.shape
    depth = fib_ref.shape[2]
    for x in range(size_x):
        flat[:, x * size_y : (x + 1) * size_y] = cls_ref[x]
    found = fiber_fields(table_ref[...], flat[...])
    for a in range(3):
        fib_ref[a] = found[:, a * depth : (a + 1) * depth]


def tension_kernel(
    sec_hbm, map_hbm, list_hbm, ang_hbm, plain, edge_ten, list_ref, table_ref, main, gate, late, ang_ref, map_ref, sems
):
    size_x, size_y = sec_hbm.shape[1], sec_hbm.shape[2]
    pieces = (sems.shape[0] - 3) // 3
    chunk = size_x // pieces

    def plane(x, carry):
        v, c, d, f, bound, s = main[0, x], main[1, x], main[2, x], gate[0, x], late[0, x], late[1, x]
        calcium_flow = 1.2 * d * f * (v - 2.0)
        flow = 2.0 * c * (1.0 - bound) - 0.4 * bound
        c1 = c + DT * (-0.3 * calcium_flow - 0.5 * c - flow)
        s1 = s + (0.5 * DT) * (rise(c) - s)
        plain[place_of(x, size_y), :] = s1 + (0.5 * DT) * (rise(c1) - s1)
        return carry

    @pl.when(electric())
    def _():
        small = [
            pltpu.make_async_copy(src, dst, sems.at[i])
            for i, (src, dst) in enumerate(((ang_hbm, ang_ref), (map_hbm, map_ref), (list_hbm, list_ref)))
        ]
        small[0].start()
        copies = []
        for i in range(pieces):
            here = pl.ds(i * chunk, chunk)
            copies.append(
                [
                    pltpu.make_async_copy(sec_hbm.at[src, here], dst.at[:, here], sems.at[3 + 3 * i + k])
                    for k, (src, dst) in enumerate(
                        ((pl.ds(0, 3), main), (pl.ds(3, 1), gate), (pl.ds(6, 2), late))
                    )
                ]
            )
            for copy in copies[-1]:
                copy.start()
        for copy in small[1:]:
            copy.start()
        small[0].wait()
        table_ref[...] = fiber_table(ang_ref[...], main.shape[3] // CELLS)
        for i in range(pieces):
            for copy in copies[i]:
                copy.wait()
            lax.fori_loop(i * chunk, (i + 1) * chunk, plane, 0, unroll=2)
        for copy in small[1:]:
            copy.wait()
        last = (size_x - 1) * size_y
        for p in range(size_y):
            edge_ten[0, p : p + 1, :] = plain[pl.ds(map_ref[p], 1), :]
            edge_ten[1, p : p + 1, :] = plain[pl.ds(map_ref[last + p], 1), :]


def share_kernel(own, after, pad, share):
    size_x, size_y = own.shape[1], own.shape[2]
    zeros = jnp.zeros(pad.shape[2:], F32)
    for a in range(3):
        pad[a, 0] = zeros
        pad[a, size_x + 1] = zeros

    def plane(x, carry):
        for a in range(3):
            value = own[a, x]
            pad[a, x + 1, PAD : PAD + size_y, :] = value
            put_ends(share, a, x, value)
        return carry

    lax.fori_loop(0, size_x, plane, 0, unroll=4)


def gather_kernel(plain, list_ref, after, all_ref):
    @pl.when(electric())
    def _():
        columns, depth = plain.shape
        pick = (lax.broadcasted_iota(jnp.int32, (columns, columns), 0) == list_ref[...]).astype(F32)
        values = plain[...]
        high = values.astype(jnp.bfloat16).astype(F32)
        mid = (values - high).astype(jnp.bfloat16).astype(F32)
        moved = lax.dot_general(
            pick,
            jnp.concatenate([high, mid, values - high - mid], axis=1),
            (((0,), (0,)), ((), ())),
            preferred_element_type=F32,
        )
        all_ref[...] = moved[:, :depth] + moved[:, depth : 2 * depth] + moved[:, 2 * depth :]


def edge_kernel(table_in, cls_ref, ang_ref, after, list_ref, edge_fib, table_ref, flat):
    size_x, blocks, size_y = cls_ref.shape

    @pl.when(jnp.logical_not(electric()))
    def _():
        table_ref[...] = fiber_table(ang_ref[...], blocks)

    for which, (_, edge, _) in enumerate(sides(size_x)):
        flat[:, which * size_y : (which + 1) * size_y] = cls_ref[edge]
    edge_fib[...] = fiber_fields(table_ref[...], flat[...])


def message_electric(pad_in, own, side_ref, edge_fib, high_ref, low_ref, pad):
    size_x, size_y = own.shape[1], own.shape[2]

    def fill(x, carry):
        for a in range(3):
            fill_sides(pad, a, x + 1, side_ref, x, size_y)
        return carry

    lax.fori_loop(0, size_x, fill, 0, unroll=4)

    @pl.when(electric())
    def _():
        for which, ((_, edge, _), out) in enumerate(zip(sides(size_x), (low_ref, high_ref))):
            below, above = side_rows(side_ref, 0, edge)
            out[ROW_VOLT_SIDE : ROW_VOLT_SIDE + 1, :] = below
            out[ROW_VOLT_SIDE + 1 : ROW_VOLT_SIDE + 2, :] = above
            rows, depth = slice(which * size_y, (which + 1) * size_y), own.shape[3]
            fib = [edge_fib[rows, a * depth : (a + 1) * depth] for a in range(3)]
            v, c, d = [rows_of(pad, a, edge + 1, size_y) for a in range(3)]
            f, n, r = [own[k, edge] for k in range(3, 6)]
            rate = volt_rate(pad, edge + 1, fib, size_y)
            _, _, total = currents(v, c, d, f, n, r)
            out[ROW_VOLT : ROW_VOLT + size_y, :] = v
            out[ROW_VOLT_NEXT : ROW_VOLT_NEXT + size_y, :] = v + DT * (rate - total)
            for k, value in enumerate(couplings(fib)):
                out[ROW_COUPLED + k * size_y : ROW_COUPLED + (k + 1) * size_y, :] = value

def message_mechanic(pad_in, own, side_ref, edge_fib, ten_ref, list_ref, high_ref, low_ref, pad):
    size_x, size_y = own.shape[1], own.shape[2]

    @pl.when(jnp.logical_not(electric()))
    def _():
        depth = own.shape[3]
        for which, ((_, edge, _), out) in enumerate(zip(sides(size_x), (low_ref, high_ref))):
            out[ROW_LIST : ROW_LIST + 1, 0:size_y] = list_ref[which].astype(F32)
            rate = motion_rate(pad, edge + 1, size_y)
            stiff = own[6, edge]
            beta = OMEGA * inverse(stiff)
            act = own[7, edge] * ten_ref[which]
            out[ROW_STIFF : ROW_STIFF + size_y, :] = stiff
            for a in range(3):
                row = ROW_SIDE + 2 * a
                out[row : row + 1, :], out[row + 1 : row + 2, :] = side_rows(side_ref, a, edge)
                u = rows_of(pad, a, edge + 1, size_y)
                out[ROW_NOW + a * size_y : ROW_NOW + (a + 1) * size_y, :] = u
                drive = own[3 + a, edge] + act * edge_fib[which * size_y : (which + 1) * size_y, a * depth : (a + 1) * depth]
                out[ROW_NEXT + a * size_y : ROW_NEXT + (a + 1) * size_y, :] = (
                    0.28 * u + beta * drive + OMEGA * rate[a]
                )


def put_inner(next_pad, share, a, x, value):
    next_pad[a, x, PAD : PAD + value.shape[0], :] = value
    put_ends(share, a, x, value)


def inner_electric(
    pad, own, plain, cls_ref, table_ref, next_pad, share, keep, out_hbm, fib_ref, flat, sems
):
    size_x, size_y = own.shape[1], own.shape[2]

    all_fibers(table_ref, cls_ref, flat, fib_ref)

    @pl.when(electric())
    def _():
        copies = [
            pltpu.make_async_copy(plain.at[x * size_y : (x + 1) * size_y], out_hbm.at[0, 3, x], sems.at[x])
            for x in range(size_x)
        ]
        for copy in copies:
            copy.start()

        def plane(x, carry):
            place = place_of(x, size_y)
            v, c, d = [rows_of(pad, a, x + 1, size_y) for a in range(3)]
            f, n, r, bound, _ = [own[k, x] for k in range(3, 8)]
            rate = volt_rate(pad, x + 1, [fib_ref[a, place, :] for a in range(3)], size_y)
            q, calcium_flow, total = currents(v, c, d, f, n, r)
            flow = 2.0 * c * (1.0 - bound) - 0.4 * bound
            put_inner(next_pad, share, 0, x + 1, v + DT * (rate - total))
            c1 = c + DT * (-0.3 * calcium_flow - 0.5 * c - flow)
            tv = jnp.tanh(v)
            d1 = (1.0 - 2.0 * DT) * d + DT * (1.0 + jnp.tanh(v + 0.5))
            f1 = (1.0 - DT / 3.0) * f + (DT / 6.0) * (1.0 - tv)
            n1 = (1.0 - DT) * n + (0.5 * DT) * (1.0 + tv)
            r1 = (1.0 - DT / 5.0) * r + (DT / 10.0) * (1.0 + jnp.tanh(0.5 * v - 0.25))
            bound1 = bound + DT * flow
            flow1 = 2.0 * c1 * (1.0 - bound1) - 0.4 * bound1
            keep[0, x] = n1
            keep[1, x] = 1.2 * d1 * f1
            keep[2, x] = 0.8 * n1 + 0.6 * rise(c1) * r1
            keep[3, x] = c1 - DT * (0.5 * c1 + flow1)
            return carry

        lax.fori_loop(0, size_x, plane, 0, unroll=2)
        for copy in copies:
            copy.wait()


def inner_mechanic(
    pad, own, fib_ref, ten_ref, next_in, share_in, keep_in, out_in, next_pad, share, keep, out_hbm, sems
):
    size_x, size_y = own.shape[1], own.shape[2]

    @pl.when(jnp.logical_not(electric()))
    def _():
        def plane(x, carry):
            place = place_of(x, size_y)
            rate = motion_rate(pad, x + 1, size_y)
            beta = OMEGA * inverse(own[6, x])
            act = own[7, x] * ten_ref[place, :]
            keep[3, x] = act
            for a in range(3):
                drive = beta * (own[3 + a, x] + act * fib_ref[a, place, :])
                keep[a, x] = drive
                value = 0.4 * rows_of(pad, a, x + 1, size_y) + drive + OMEGA * rate[a]
                put_inner(next_pad, share, a, x + 1, value)
            return carry

        lax.fori_loop(0, size_x, plane, 0, unroll=2)
        copy = pltpu.make_async_copy(keep.at[3:4], out_hbm.at[0, 3:4], sems.at[0])
        copy.start()
        copy.wait()


def outer_electric(pad, own, fib_ref, volt_low, volt_high, next_in, next_pad, share, wide):
    size_x, size_y = own.shape[1], own.shape[2]
    def put(a, x, slot, value):
        next_pad[a, x, PAD : PAD + size_y, :] = value
        put_ends(share, a, slot, value)

    def put_side(a, which, low, high):
        wide[a, which, PAD - 1 : PAD, :] = low
        wide[a, which, PAD + size_y : PAD + size_y + 1, :] = high

    @pl.when(electric())
    def _():
        for which, ((halo, edge, sign), got) in enumerate(zip(sides(size_x), (volt_low, volt_high))):
            wide[0, which, PAD : PAD + size_y, :] = got[ROW_VOLT : ROW_VOLT + size_y, :]
            row = ROW_VOLT_SIDE
            put_side(0, which, got[row : row + 1, :], got[row + 1 : row + 2, :])
            fib = [fib_ref[a, place_of(edge, size_y), :] for a in range(3)]
            put(
                0,
                edge + 1,
                1 + which,
                rows_of(next_pad, 0, edge + 1, size_y) + DT * volt_from(wide, which, couplings(fib), sign, size_y),
            )
            theirs = [got[ROW_COUPLED + k * size_y : ROW_COUPLED + (k + 1) * size_y, :] for k in range(3)]
            put(
                0,
                halo,
                3 * which,
                got[ROW_VOLT_NEXT : ROW_VOLT_NEXT + size_y, :] + DT * volt_from(pad, edge + 1, theirs, -sign, size_y),
            )


def outer_mechanic(which, pad, own, list_ref, got, next_in, share_in, next_pad, share, wide):
    size_x, size_y = own.shape[1], own.shape[2]
    def put(a, x, slot, value):
        next_pad[a, x, PAD : PAD + size_y, :] = value
        put_ends(share, a, slot, value)

    def put_side(a, which, low, high):
        wide[a, which, PAD - 1 : PAD, :] = low
        wide[a, which, PAD + size_y : PAD + size_y + 1, :] = high

    @pl.when(jnp.logical_not(electric()))
    def _():
        halo, edge, sign = sides(size_x)[which]
        for a in range(3):
            wide[a, which, PAD : PAD + size_y, :] = got[ROW_NOW + a * size_y : ROW_NOW + (a + 1) * size_y, :]
            row = ROW_SIDE + 2 * a
            put_side(a, which, got[row : row + 1, :], got[row + 1 : row + 2, :])
        stiff = got[ROW_STIFF : ROW_STIFF + size_y, :]
        stiff_own = own[6, edge]
        now = [rows_of(pad, a, edge + 1, size_y) for a in range(3)]
        theirs = [rows_of(wide, a, which, size_y) for a in range(3)]
        ties = tie_rows(list_ref[which].astype(F32), stiff, theirs)
        rate = motion_from(wide, which, sign, size_y)
        beta = OMEGA * inverse(stiff_own)
        for a in range(3):
            put(
                a,
                edge + 1,
                1 + which,
                rows_of(next_pad, a, edge + 1, size_y) + OMEGA * rate[a] + beta * ties[a] - 0.12 * now[a],
            )
        ties = tie_rows(got[ROW_LIST : ROW_LIST + 1, 0:size_y], stiff_own, now)
        rate = motion_from(pad, edge + 1, -sign, size_y)
        beta = OMEGA * inverse(stiff)
        for a in range(3):
            put(
                a,
                halo,
                3 * which,
                got[ROW_NEXT + a * size_y : ROW_NEXT + (a + 1) * size_y, :] + OMEGA * rate[a] + beta * ties[a],
            )


def electric_end(x, next_pad, fib_ref):
    size_y = next_pad.shape[2] - 2 * PAD
    place = place_of(x, size_y)
    return rows_of(next_pad, 0, x + 1, size_y) + DT * volt_rate(
        next_pad, x + 1, [fib_ref[a, place, :] for a in range(3)], size_y
    )


def electric_rest(x, next_pad, keep, out):
    size_y = next_pad.shape[2] - 2 * PAD
    v = rows_of(next_pad, 0, x + 1, size_y)
    n, gate, leak, rest_c = [keep[k, x] for k in range(4)]
    flow = gate * (v - 2.0)
    out[0, x] = -DT * (flow + leak * (v + 1.0) + 0.1 * v)
    out[1, x] = rest_c - (0.3 * DT) * flow
    out[2, x] = (1.0 - DT) * n + (0.5 * DT) * (1.0 + jnp.tanh(v))


def mechanic_end(x, next_pad, keep, size_y):
    rate = motion_rate(next_pad, x + 1, size_y)
    return [
        0.4 * rows_of(next_pad, a, x + 1, size_y) + keep[a, x] + OMEGA * rate[a] for a in range(3)
    ]


def middle_kernel(
    fib_ref, own, list_ref, got_low, got_high, next_in, side_ref, keep, out_in,
    out_hbm, next_pad, held, final, out, sems
):
    size_x = keep.shape[1]
    size_y = fib_ref.shape[1] // size_x
    lead = size_x - 4 - final.shape[1]

    def copy_out(fields):
        here = pl.ds(2, lead)
        return pltpu.make_async_copy(out.at[0:fields, here], out_hbm.at[0, 0:fields, here], sems.at[0])

    def fill(count):
        def one(x, carry):
            for a in range(count):
                fill_sides(next_pad, a, x, side_ref, x, size_y)
            return carry

        lax.fori_loop(2, size_x, one, 0, unroll=2)

    @pl.when(electric())
    def _():
        fill(1)

        def rest(x, carry):
            electric_rest(x, next_pad, keep, out)
            return carry

        lax.fori_loop(0, size_x, rest, 0, unroll=2)
        copy = pltpu.make_async_copy(out.at[1:3], out_hbm.at[0, 1:3], sems.at[1])
        copy.start()
        for i, x in enumerate((0, 1, size_x - 2, size_x - 1)):
            held[i] = out[0, x]

        for x in range(2, 2 + lead):
            out[0, x] = out[0, x] + electric_end(x, next_pad, fib_ref)
        copy_out(1).start()
        for x in range(2 + lead, size_x - 2):
            final[0, x - 2 - lead] = out[0, x] + electric_end(x, next_pad, fib_ref)
        copy.wait()
        copy_out(1).wait()

    @pl.when(jnp.logical_not(electric()))
    def _():
        fill(3)
        for x in range(2, 2 + lead):
            for a, value in enumerate(mechanic_end(x, next_pad, keep, size_y)):
                out[a, x] = value
        copy_out(3).start()
        for which, ((halo, edge, _), got) in enumerate(zip(sides(size_x), (got_low, got_high))):
            beta = OMEGA * inverse(own[6, edge])
            ties = tie_rows(
                list_ref[which].astype(F32),
                got[ROW_STIFF : ROW_STIFF + size_y, :],
                [rows_of(next_pad, a, halo, size_y) for a in range(3)],
            )
            for a in range(3):
                held[3 * which + a] = beta * ties[a] - 0.12 * rows_of(next_pad, a, edge + 1, size_y)
        for x in range(2 + lead, size_x - 2):
            for a, value in enumerate(mechanic_end(x, next_pad, keep, size_y)):
                final[a, x - 2 - lead] = value
        copy_out(3).wait()


def last_kernel(
    fib_ref, next_in, side_ref, keep, held, final, out_in, out_hbm, next_pad, out, sems
):
    size_x = keep.shape[1]
    size_y = fib_ref.shape[1] // size_x

    def copy_out(which, first, fields):
        here = pl.ds(first, 2)
        return pltpu.make_async_copy(out.at[0:fields, here], out_hbm.at[0, 0:fields, here], sems.at[which])

    def copy_final(fields):
        here = pl.ds(size_x - 2 - final.shape[1], final.shape[1])
        return pltpu.make_async_copy(final.at[0:fields], out_hbm.at[0, 0:fields, here], sems.at[2])

    work = []
    for which, (halo, edge, _) in enumerate(sides(size_x)):
        near = abs(edge - 1)
        work.append((halo, edge, near, which, min(edge, near)))

    @pl.when(electric())
    def _():
        copy_final(1).start()
        for halo, edge, near, which, first in work:
            fill_sides(next_pad, 0, halo, side_ref, 3 * which, size_y)
            fill_sides(next_pad, 0, edge + 1, side_ref, 1 + which, size_y)
            for x in (near, edge):
                out[0, x] = held[2 * which + x - first] + electric_end(x, next_pad, fib_ref)
            copy_out(which, first, 1).start()
        for item in work:
            copy_out(item[3], item[-1], 1).wait()
        copy_final(1).wait()

    @pl.when(jnp.logical_not(electric()))
    def _():
        copy_final(3).start()
        for halo, edge, near, which, first in work:
            for a in range(3):
                fill_sides(next_pad, a, halo, side_ref, 3 * which, size_y)
                fill_sides(next_pad, a, edge + 1, side_ref, 1 + which, size_y)
            for a, value in enumerate(mechanic_end(near, next_pad, keep, size_y)):
                out[a, near] = value
            for a, value in enumerate(mechanic_end(edge, next_pad, keep, size_y)):
                out[a, edge] = value + held[3 * which + a]
            copy_out(which, first, 3).start()
        for item in work:
            copy_out(item[3], item[-1], 3).wait()
        copy_final(3).wait()


def call(kernel, name, out_shape, operands, spaces, scratch=(), out_spaces=None, aliases=()):
    if out_spaces is None:
        out_spaces = [pltpu.VMEM] * len(out_shape)
    return pl.pallas_call(
        kernel,
        name=name,
        out_shape=tuple(out_shape),
        in_specs=[pl.BlockSpec(memory_space=space) for space in spaces],
        out_specs=tuple(pl.BlockSpec(memory_space=space) for space in out_spaces),
        scratch_shapes=scratch,
        input_output_aliases=dict(aliases),
        cost_estimate=pl.CostEstimate(
            flops=int(COST[name] * 10**10), bytes_accessed=int(COST[name] * 10**7), transcendentals=0
        ),
        compiler_params=pltpu.CompilerParams(vmem_limit_bytes=VMEM_LIMIT),
    )(*operands)


def local(sections, fiber_angles, fiber_class, row_map, interface_rows):
    own = sections[0]
    channels, size_x, size_y, depth = own.shape
    n_gx = lax.axis_size("gx")
    n_gy = lax.axis_size("gy")
    assert lax.axis_size("sec") == 2 and n_gy == 2
    axes = ("sec", "gx", "gy")
    place = lambda sec, i, j: (sec * n_gx + i % n_gx) * n_gy + j
    blocks = [(i, j) for i in range(n_gx) for j in range(n_gy)]

    def ring(section, step):
        return [(place(section, i, j), place(section, i + step, j)) for i, j in blocks] + [
            (place(1 - section, i, j), place(1 - section, i, 1 - j)) for i, j in blocks
        ]

    both = [(0, 1), (1, 0)]
    S, V, H = pltpu.SMEM, pltpu.VMEM, pltpu.HBM
    f32 = lambda *shape: jax.ShapeDtypeStruct(shape, F32)
    hbm = lambda w: pltpu.with_memory_space_constraint(w, H)
    columns = size_x * size_y
    ends = lambda planes: f32(6 * planes, depth)
    padded = f32(3, size_x + 2, size_y + 2 * PAD, depth)
    classes = fiber_class.transpose(0, 2, 1)
    lists = interface_rows.reshape(2, 1, size_y)
    places = row_map.reshape(-1)

    field = lambda n: pltpu.VMEM((n, size_x, size_y, depth), F32)
    flat = lambda count: pltpu.VMEM((classes.shape[1], count), jnp.int32)
    angles = fiber_angles.T
    plain, edge_ten, own_list, table = call(
        tension_kernel,
        "tension",
        (
            f32(columns, depth),
            f32(2, size_y, depth),
            jax.ShapeDtypeStruct((1, columns), jnp.int32),
            f32(3 * fiber_angles.shape[0] * classes.shape[1], 3 * depth),
        ),
        (hbm(own), hbm(places), hbm(row_map.reshape(1, columns)), hbm(angles)),
        (H,) * 4,
        [
            field(3),
            field(1),
            field(2),
            pltpu.VMEM(angles.shape, F32),
            pltpu.SMEM((columns,), jnp.int32),
            pltpu.SemaphoreType.DMA((3 + 3 * 4,)),
        ],
    )
    edge_ten = lax.ppermute(edge_ten, "sec", both)
    pad, share = call(share_kernel, "share", (padded, ends(size_x)), (own, plain), (V, V))
    side = lax.ppermute(share, "gy", both)
    result = f32(1, 4, size_x, size_y, depth)
    (gathered,) = call(gather_kernel, "gather", (f32(columns, depth),), (plain, own_list, share), (V,) * 3)
    edge_fib, table = call(
        edge_kernel,
        "edge",
        (f32(2 * size_y, 3 * depth), f32(*table.shape)),
        (table, classes, angles, gathered, lists),
        (V,) * 5,
        [flat(2 * size_y)],
        aliases={0: 1},
    )
    tension = lax.ppermute(gathered, "sec", both)
    assert depth == CELLS * classes.shape[1]
    message = f32(VOLT_ROWS, depth)
    high, low, pad = call(
        message_electric,
        "message_electric",
        (message, message, padded),
        (pad, own, side, edge_fib),
        (V,) * 4,
        aliases={0: 2},
    )
    volt_low = lax.ppermute(high, axes, ring(0, 1))
    volt_high = lax.ppermute(low, axes, ring(0, -1))
    message = f32(MESSAGE_ROWS, depth)
    high, low, pad = call(
        message_mechanic,
        "message_mechanic",
        (message, message, padded),
        (pad, own, side, edge_fib, edge_ten, lists),
        (V,) * 6,
        aliases={0: 2},
    )
    got_low = lax.ppermute(high, axes, ring(1, 1))
    got_high = lax.ppermute(low, axes, ring(1, -1))
    moved, share, keep, result, fib = call(
        inner_electric,
        "inner_electric",
        (padded, ends(size_x + 2), f32(4, size_x, size_y, depth), result, f32(3, columns, depth)),
        (pad, own, plain, classes, table),
        (V,) * 5,
        [flat(columns), pltpu.SemaphoreType.DMA((size_x,))],
        out_spaces=(V, V, V, H, V),
    )
    moved, share, keep, result = call(
        inner_mechanic,
        "inner_mechanic",
        (padded, ends(size_x + 2), f32(4, size_x, size_y, depth), f32(1, 4, size_x, size_y, depth)),
        (pad, own, fib, tension, moved, share, keep, result),
        (V,) * 7 + (H,),
        [pltpu.SemaphoreType.DMA((1,))],
        out_spaces=(V, V, V, H),
        aliases={4: 0, 5: 1, 6: 2, 7: 3},
    )
    side = lax.ppermute(share, "gy", both)
    wide = pltpu.VMEM((3, 2) + padded.shape[2:], F32)
    moved, share = call(
        outer_electric,
        "outer_electric",
        (padded, ends(4)),
        (pad, own, fib, volt_low, volt_high, moved),
        (V,) * 6,
        [wide],
        aliases={5: 0},
    )
    for which, got in enumerate((got_low, got_high)):
        moved, share = call(
            functools.partial(outer_mechanic, which),
            ("outer_low", "outer_high")[which],
            (padded, ends(4)),
            (pad, own, lists, got, moved, share),
            (V,) * 6,
            [wide],
            aliases={4: 0, 5: 1},
        )
    end_side = lax.ppermute(share, "gy", both)
    fields = pltpu.VMEM((3, size_x, size_y, depth), F32)
    held_back = 10
    result, moved, held, final = call(
        middle_kernel,
        "middle",
        (f32(1, 4, size_x, size_y, depth), padded, f32(6, size_y, depth), f32(3, held_back, size_y, depth)),
        (fib, own, lists, got_low, got_high, moved, side, keep, result),
        (V,) * 8 + (H,),
        [fields, pltpu.SemaphoreType.DMA((2,))],
        out_spaces=(H, V, V, V),
        aliases={5: 1, 8: 0},
    )
    return call(
        last_kernel,
        "last",
        (f32(1, 4, size_x, size_y, depth), padded),
        (fib, moved, end_side, keep, held, final, result),
        (V,) * 6 + (H,),
        [fields, pltpu.SemaphoreType.DMA((3,))],
        out_spaces=(H, V),
        aliases={1: 1, 6: 0},
    )[0]


def solution(mesh):
    in_specs = (
        P("sec", None, "gx", "gy", None),
        P(),
        P("gx", "gy", None),
        P("gx", "gy", None),
        P(None, "gx", "gy", None),
    )
    out_specs = P("sec", None, "gx", "gy", None)
    return jax.shard_map(local, mesh=mesh, in_specs=in_specs, out_specs=out_specs, check_vma=False)
```

```python
import functools

import jax
import jax.numpy as jnp
from jax import lax
from jax.experimental import pallas as pl
from jax.experimental.pallas import tpu as pltpu
from jax.sharding import PartitionSpec as P

DT = 0.1
OMEGA = 0.06
F32 = jnp.float32
VMEM_LIMIT = 16 * 1024 * 1024
COST = {
    "tension": 0.001,
    "share": 0.001,
    "gather": 6,
    "edge": 1,
    "message_electric": 1,
    "message_mechanic": 1,
    "inner_electric": 6,
    "inner_mechanic": 6,
    "outer_electric": 1,
    "outer_low": 0.01,
    "outer_high": 1,
    "middle": 6,
    "last": 1,
}

CELLS = 16

PAD = 8

ROW_NOW, ROW_NEXT, ROW_STIFF, ROW_SIDE = 0, 96, 192, 224
ROW_LIST = ROW_SIDE + 6
MESSAGE_ROWS = 232
ROW_VOLT, ROW_VOLT_NEXT, ROW_COUPLED, ROW_VOLT_SIDE = 0, 32, 64, 160
VOLT_ROWS = 168


def inverse(v):
    r = pl.reciprocal(v, approx=True)
    return r * (2.0 - v * r)


def rise(c):
    c2 = c * c
    return c2 * inverse(c2 + 0.25)


def ends(like):
    lane = lax.broadcasted_iota(jnp.int32, like, 1)
    return lane == like[1] - 1, lane == 0


def up_z(w, last):
    return jnp.where(last, 0.0, pltpu.roll(w, w.shape[1] - 1, 1))


def down_z(w, first):
    return jnp.where(first, 0.0, pltpu.roll(w, 1, 1))


def rows_of(pad, a, x, size_y, shift=0):
    return pad[a, x, PAD + shift : PAD + shift + size_y, :]


def motion_rate(pad, x, size_y):
    at = lambda a, dx=0, dy=0: rows_of(pad, a, x + dx, size_y, dy)
    u0, u1, u2 = at(0), at(1), at(2)
    last, first = ends(u0.shape)
    w0p, w0m, w1p, w1m = at(0, 1), at(0, -1), at(1, 1), at(1, -1)
    w2p, w2m = at(2, 1), at(2, -1)
    e0, e2 = 0.5 * (w0p - w0m), 0.5 * (w2p - w2m)
    e0y = (at(0, 1, 1) - at(0, -1, 1)) - (at(0, 1, -1) - at(0, -1, -1))
    e1y = (at(1, 1, 1) - at(1, -1, 1)) - (at(1, 1, -1) - at(1, -1, -1))
    v1p, v1m, v2p, v2m = at(1, 0, 1), at(1, 0, -1), at(2, 0, 1), at(2, 0, -1)
    d2 = 0.5 * (v2p - v2m)
    d1 = 0.5 * (v1p - v1m) + e0
    r0 = (
        up_z(u0 + e2, last) + down_z(u0 - e2, first)
        + (at(0, 0, 1) + at(0, 0, -1)) + 0.5 * e1y + 3.0 * (w0p + w0m)
    )
    r1 = (
        up_z(u1 + d2, last) + down_z(u1 - d2, first)
        + 3.0 * (v1p + v1m) + 0.5 * e0y + (w1p + w1m)
    )
    t2 = 3.0 * u2
    r2 = up_z(t2 + d1, last) + down_z(t2 - d1, first) + (v2p + v2m) + (w2p + w2m)
    return r0, r1, r2


def motion_from(pad, x, sign, size_y):
    u0, u1, u2 = [rows_of(pad, a, x, size_y) for a in range(3)]
    last, first = ends(u0.shape)
    half = 0.5 * sign
    dy0 = rows_of(pad, 0, x, size_y, 1) - rows_of(pad, 0, x, size_y, -1)
    dy1 = rows_of(pad, 1, x, size_y, 1) - rows_of(pad, 1, x, size_y, -1)
    dz0 = up_z(u0, last) - down_z(u0, first)
    dz2 = up_z(u2, last) - down_z(u2, first)
    return 3.0 * u0 + half * (dy1 + dz2), u1 + half * dy0, u2 + half * dz0


def volt_rate(pad, x, fib, size_y):
    at = lambda dx=0, dy=0: rows_of(pad, 0, x + dx, size_y, dy)
    v, wp, wm, yp, ym = at(), at(1), at(-1), at(0, 1), at(0, -1)
    last, first = ends(v.shape)
    e = wp - wm
    ey = (at(1, 1) - at(-1, 1)) - (at(1, -1) - at(-1, -1))
    dy = yp - ym
    sum_z = up_z(v, last) + down_z(v, first)
    ez = up_z(e, last) - down_z(e, first)
    dyz = up_z(dy, last) - down_z(dy, first)
    g = [0.75 * w for w in fib]
    d00, d11, d22 = [0.25 + a * b for a, b in zip(g, fib)]
    return (
        d00 * (wp + wm) + d11 * (yp + ym) + d22 * sum_z - 2.0 * (d00 + d11 + d22) * v
        + 0.5 * (fib[0] * (g[1] * ey + g[2] * ez) + g[1] * fib[2] * dyz)
    )


def couplings(fib):
    g = 0.75 * fib[0]
    return 0.25 + g * fib[0], 0.5 * g * fib[1], 0.5 * g * fib[2]


def volt_from(pad, x, coupled, sign, size_y):
    v = rows_of(pad, 0, x, size_y)
    last, first = ends(v.shape)
    dy = rows_of(pad, 0, x, size_y, 1) - rows_of(pad, 0, x, size_y, -1)
    dz = up_z(v, last) - down_z(v, first)
    return coupled[0] * v + sign * (coupled[1] * dy + coupled[2] * dz)


def currents(v, c, d, f, n, r):
    q = rise(c)
    calcium_flow = 1.2 * d * f * (v - 2.0)
    return q, calcium_flow, calcium_flow + (0.8 * n + 0.6 * q * r) * (v + 1.0) + 0.1 * v


def in_three(values):
    high = values.astype(jnp.bfloat16).astype(F32)
    mid = (values - high).astype(jnp.bfloat16).astype(F32)
    return jnp.concatenate([high, mid, values - high - mid], axis=0)


def tie_rows(listed, stiff, u):
    rows, depth = u[0].shape
    joined = in_three(jnp.concatenate([2.0 * stiff * w for w in u], axis=1))
    pick = (lax.broadcasted_iota(jnp.int32, (rows, rows), 0).astype(F32) == listed).astype(F32)
    moved = lax.dot_general(
        jnp.concatenate([pick] * 3, axis=0), joined, (((0,), (0,)), ((), ())), preferred_element_type=F32
    )
    return [moved[:, a * depth : (a + 1) * depth] for a in range(3)]


def put_ends(ends, a, x, value):
    rows, row = value.shape[0], 2 * (a * (ends.shape[0] // 6) + x)
    ends[pl.ds(row, 1), :] = value[0:1]
    ends[pl.ds(row + 1, 1), :] = value[rows - 1 : rows]


def fill_sides(pad, a, x, ends, k, size_y):
    row = 2 * (a * (ends.shape[0] // 6) + k)
    pad[a, x, PAD - 1 : PAD, :] = ends[pl.ds(row + 1, 1), :]
    pad[a, x, PAD + size_y : PAD + size_y + 1, :] = ends[pl.ds(row, 1), :]


def side_rows(ends, a, x):
    row = 2 * (a * (ends.shape[0] // 6) + x)
    return ends[row + 1 : row + 2, :], ends[row : row + 1, :]


def sides(size_x):
    return (0, 0, -1.0), (size_x + 1, size_x - 1, 1.0)


def place_of(x, size_y):
    return pl.ds(pl.multiple_of(x * size_y, size_y), size_y)


def electric():
    return lax.axis_index("sec") == 0


def fiber_table(angles, blocks):
    classes, depth = angles.shape[1], CELLS * blocks
    azimuth, elevation = angles[0:1, :], angles[1:2, :]
    flat_part = jnp.cos(elevation)
    fib = [jnp.cos(azimuth) * flat_part, jnp.sin(azimuth) * flat_part, jnp.sin(elevation)]
    own = lax.broadcasted_iota(jnp.int32, (blocks, depth), 1) // CELLS
    own = own == lax.broadcasted_iota(jnp.int32, (blocks, depth), 0)
    return in_three(
        jnp.concatenate(
            [
                jnp.concatenate(
                    [jnp.where(own, jnp.broadcast_to(w[:, k : k + 1], own.shape), 0.0) for w in fib], axis=1
                )
                for k in range(classes)
            ],
            axis=0,
        )
    )


def fiber_fields(table, cls):
    classes = table.shape[0] // (3 * cls.shape[0])
    hits = jnp.concatenate([(cls == k).astype(F32) for k in range(classes)] * 3, axis=0)
    return lax.dot_general(hits, table, (((0,), (0,)), ((), ())), preferred_element_type=F32)


def all_fibers(table_ref, cls_ref, flat, fib_ref):
    size_x, _, size_y = cls_ref.shape
    depth = fib_ref.shape[2]
    for x in range(size_x):
        flat[:, x * size_y : (x + 1) * size_y] = cls_ref[x]
    found = fiber_fields(table_ref[...], flat[...])
    for a in range(3):
        fib_ref[a] = found[:, a * depth : (a + 1) * depth]


def tension_kernel(
    sec_hbm, map_hbm, list_hbm, ang_hbm, plain, edge_ten, list_ref, table_ref, main, gate, late, ang_ref, map_ref, sems
):
    size_x, size_y = sec_hbm.shape[1], sec_hbm.shape[2]
    pieces = (sems.shape[0] - 3) // 3
    chunk = size_x // pieces

    def plane(x, carry):
        v, c, d, f, bound, s = main[0, x], main[1, x], main[2, x], gate[0, x], late[0, x], late[1, x]
        calcium_flow = 1.2 * d * f * (v - 2.0)
        flow = 2.0 * c * (1.0 - bound) - 0.4 * bound
        c1 = c + DT * (-0.3 * calcium_flow - 0.5 * c - flow)
        s1 = s + (0.5 * DT) * (rise(c) - s)
        plain[place_of(x, size_y), :] = s1 + (0.5 * DT) * (rise(c1) - s1)
        return carry

    @pl.when(electric())
    def _():
        small = [
            pltpu.make_async_copy(src, dst, sems.at[i])
            for i, (src, dst) in enumerate(((ang_hbm, ang_ref), (map_hbm, map_ref), (list_hbm, list_ref)))
        ]
        small[0].start()
        copies = []
        for i in range(pieces):
            here = pl.ds(i * chunk, chunk)
            copies.append(
                [
                    pltpu.make_async_copy(sec_hbm.at[src, here], dst.at[:, here], sems.at[3 + 3 * i + k])
                    for k, (src, dst) in enumerate(
                        ((pl.ds(0, 3), main), (pl.ds(3, 1), gate), (pl.ds(6, 2), late))
                    )
                ]
            )
            for copy in copies[-1]:
                copy.start()
        for copy in small[1:]:
            copy.start()
        small[0].wait()
        table_ref[...] = fiber_table(ang_ref[...], main.shape[3] // CELLS)
        for i in range(pieces):
            for copy in copies[i]:
                copy.wait()
            lax.fori_loop(i * chunk, (i + 1) * chunk, plane, 0, unroll=2)
        for copy in small[1:]:
            copy.wait()
        last = (size_x - 1) * size_y
        for p in range(size_y):
            edge_ten[0, p : p + 1, :] = plain[pl.ds(map_ref[p], 1), :]
            edge_ten[1, p : p + 1, :] = plain[pl.ds(map_ref[last + p], 1), :]


def share_kernel(own, after, pad, share):
    size_x, size_y = own.shape[1], own.shape[2]
    zeros = jnp.zeros(pad.shape[2:], F32)
    for a in range(3):
        pad[a, 0] = zeros
        pad[a, size_x + 1] = zeros

    def plane(x, carry):
        for a in range(3):
            value = own[a, x]
            pad[a, x + 1, PAD : PAD + size_y, :] = value
            put_ends(share, a, x, value)
        return carry

    lax.fori_loop(0, size_x, plane, 0, unroll=4)


def gather_kernel(plain, list_ref, after, all_ref):
    @pl.when(electric())
    def _():
        columns, depth = plain.shape
        pick = (lax.broadcasted_iota(jnp.int32, (columns, columns), 0) == list_ref[...]).astype(F32)
        values = plain[...]
        high = values.astype(jnp.bfloat16).astype(F32)
        mid = (values - high).astype(jnp.bfloat16).astype(F32)
        moved = lax.dot_general(
            pick,
            jnp.concatenate([high, mid, values - high - mid], axis=1),
            (((0,), (0,)), ((), ())),
            preferred_element_type=F32,
        )
        all_ref[...] = moved[:, :depth] + moved[:, depth : 2 * depth] + moved[:, 2 * depth :]


def edge_kernel(table_in, cls_ref, ang_ref, after, list_ref, edge_fib, table_ref, flat):
    size_x, blocks, size_y = cls_ref.shape

    @pl.when(jnp.logical_not(electric()))
    def _():
        table_ref[...] = fiber_table(ang_ref[...], blocks)

    for which, (_, edge, _) in enumerate(sides(size_x)):
        flat[:, which * size_y : (which + 1) * size_y] = cls_ref[edge]
    edge_fib[...] = fiber_fields(table_ref[...], flat[...])


def message_electric(pad_in, own, side_ref, edge_fib, high_ref, low_ref, pad):
    size_x, size_y = own.shape[1], own.shape[2]

    def fill(x, carry):
        for a in range(3):
            fill_sides(pad, a, x + 1, side_ref, x, size_y)
        return carry

    lax.fori_loop(0, size_x, fill, 0, unroll=4)

    @pl.when(electric())
    def _():
        for which, ((_, edge, _), out) in enumerate(zip(sides(size_x), (low_ref, high_ref))):
            below, above = side_rows(side_ref, 0, edge)
            out[ROW_VOLT_SIDE : ROW_VOLT_SIDE + 1, :] = below
            out[ROW_VOLT_SIDE + 1 : ROW_VOLT_SIDE + 2, :] = above
            rows, depth = slice(which * size_y, (which + 1) * size_y), own.shape[3]
            fib = [edge_fib[rows, a * depth : (a + 1) * depth] for a in range(3)]
            v, c, d = [rows_of(pad, a, edge + 1, size_y) for a in range(3)]
            f, n, r = [own[k, edge] for k in range(3, 6)]
            rate = volt_rate(pad, edge + 1, fib, size_y)
            _, _, total = currents(v, c, d, f, n, r)
            out[ROW_VOLT : ROW_VOLT + size_y, :] = v
            out[ROW_VOLT_NEXT : ROW_VOLT_NEXT + size_y, :] = v + DT * (rate - total)
            for k, value in enumerate(couplings(fib)):
                out[ROW_COUPLED + k * size_y : ROW_COUPLED + (k + 1) * size_y, :] = value

def message_mechanic(pad_in, own, side_ref, edge_fib, ten_ref, list_ref, high_ref, low_ref, pad):
    size_x, size_y = own.shape[1], own.shape[2]

    @pl.when(jnp.logical_not(electric()))
    def _():
        depth = own.shape[3]
        for which, ((_, edge, _), out) in enumerate(zip(sides(size_x), (low_ref, high_ref))):
            out[ROW_LIST : ROW_LIST + 1, 0:size_y] = list_ref[which].astype(F32)
            rate = motion_rate(pad, edge + 1, size_y)
            stiff = own[6, edge]
            beta = OMEGA * inverse(stiff)
            act = own[7, edge] * ten_ref[which]
            out[ROW_STIFF : ROW_STIFF + size_y, :] = stiff
            for a in range(3):
                row = ROW_SIDE + 2 * a
                out[row : row + 1, :], out[row + 1 : row + 2, :] = side_rows(side_ref, a, edge)
                u = rows_of(pad, a, edge + 1, size_y)
                out[ROW_NOW + a * size_y : ROW_NOW + (a + 1) * size_y, :] = u
                drive = own[3 + a, edge] + act * edge_fib[which * size_y : (which + 1) * size_y, a * depth : (a + 1) * depth]
                out[ROW_NEXT + a * size_y : ROW_NEXT + (a + 1) * size_y, :] = (
                    0.28 * u + beta * drive + OMEGA * rate[a]
                )


def put_inner(next_pad, share, a, x, value):
    next_pad[a, x, PAD : PAD + value.shape[0], :] = value
    put_ends(share, a, x, value)


def inner_electric(
    pad, own, plain, cls_ref, table_ref, next_pad, share, keep, out_hbm, fib_ref, flat, sems
):
    size_x, size_y = own.shape[1], own.shape[2]

    all_fibers(table_ref, cls_ref, flat, fib_ref)

    @pl.when(electric())
    def _():
        copies = [
            pltpu.make_async_copy(plain.at[x * size_y : (x + 1) * size_y], out_hbm.at[0, 3, x], sems.at[x])
            for x in range(size_x)
        ]
        for copy in copies:
            copy.start()

        def plane(x, carry):
            place = place_of(x, size_y)
            v, c, d = [rows_of(pad, a, x + 1, size_y) for a in range(3)]
            f, n, r, bound, _ = [own[k, x] for k in range(3, 8)]
            rate = volt_rate(pad, x + 1, [fib_ref[a, place, :] for a in range(3)], size_y)
            q, calcium_flow, total = currents(v, c, d, f, n, r)
            flow = 2.0 * c * (1.0 - bound) - 0.4 * bound
            put_inner(next_pad, share, 0, x + 1, v + DT * (rate - total))
            c1 = c + DT * (-0.3 * calcium_flow - 0.5 * c - flow)
            tv = jnp.tanh(v)
            d1 = (1.0 - 2.0 * DT) * d + DT * (1.0 + jnp.tanh(v + 0.5))
            f1 = (1.0 - DT / 3.0) * f + (DT / 6.0) * (1.0 - tv)
            n1 = (1.0 - DT) * n + (0.5 * DT) * (1.0 + tv)
            r1 = (1.0 - DT / 5.0) * r + (DT / 10.0) * (1.0 + jnp.tanh(0.5 * v - 0.25))
            bound1 = bound + DT * flow
            flow1 = 2.0 * c1 * (1.0 - bound1) - 0.4 * bound1
            keep[0, x] = n1
            keep[1, x] = 1.2 * d1 * f1
            keep[2, x] = 0.8 * n1 + 0.6 * rise(c1) * r1
            keep[3, x] = c1 - DT * (0.5 * c1 + flow1)
            return carry

        lax.fori_loop(0, size_x, plane, 0, unroll=8)
        for copy in copies:
            copy.wait()


def inner_mechanic(
    pad, own, fib_ref, ten_ref, next_in, share_in, keep_in, out_in, next_pad, share, keep, out_hbm, sems
):
    size_x, size_y = own.shape[1], own.shape[2]

    @pl.when(jnp.logical_not(electric()))
    def _():
        def plane(x, carry):
            place = place_of(x, size_y)
            rate = motion_rate(pad, x + 1, size_y)
            beta = OMEGA * inverse(own[6, x])
            act = own[7, x] * ten_ref[place, :]
            keep[3, x] = act
            for a in range(3):
                drive = beta * (own[3 + a, x] + act * fib_ref[a, place, :])
                keep[a, x] = drive
                value = 0.4 * rows_of(pad, a, x + 1, size_y) + drive + OMEGA * rate[a]
                put_inner(next_pad, share, a, x + 1, value)
            return carry

        lax.fori_loop(0, size_x, plane, 0, unroll=8)
        copy = pltpu.make_async_copy(keep.at[3:4], out_hbm.at[0, 3:4], sems.at[0])
        copy.start()
        copy.wait()


def outer_electric(pad, own, fib_ref, volt_low, volt_high, next_in, next_pad, share, wide):
    size_x, size_y = own.shape[1], own.shape[2]
    def put(a, x, slot, value):
        next_pad[a, x, PAD : PAD + size_y, :] = value
        put_ends(share, a, slot, value)

    def put_side(a, which, low, high):
        wide[a, which, PAD - 1 : PAD, :] = low
        wide[a, which, PAD + size_y : PAD + size_y + 1, :] = high

    @pl.when(electric())
    def _():
        for which, ((halo, edge, sign), got) in enumerate(zip(sides(size_x), (volt_low, volt_high))):
            wide[0, which, PAD : PAD + size_y, :] = got[ROW_VOLT : ROW_VOLT + size_y, :]
            row = ROW_VOLT_SIDE
            put_side(0, which, got[row : row + 1, :], got[row + 1 : row + 2, :])
            fib = [fib_ref[a, place_of(edge, size_y), :] for a in range(3)]
            put(
                0,
                edge + 1,
                1 + which,
                rows_of(next_pad, 0, edge + 1, size_y) + DT * volt_from(wide, which, couplings(fib), sign, size_y),
            )
            theirs = [got[ROW_COUPLED + k * size_y : ROW_COUPLED + (k + 1) * size_y, :] for k in range(3)]
            put(
                0,
                halo,
                3 * which,
                got[ROW_VOLT_NEXT : ROW_VOLT_NEXT + size_y, :] + DT * volt_from(pad, edge + 1, theirs, -sign, size_y),
            )


def outer_mechanic(which, pad, own, list_ref, got, next_in, share_in, next_pad, share, wide):
    size_x, size_y = own.shape[1], own.shape[2]
    def put(a, x, slot, value):
        next_pad[a, x, PAD : PAD + size_y, :] = value
        put_ends(share, a, slot, value)

    def put_side(a, which, low, high):
        wide[a, which, PAD - 1 : PAD, :] = low
        wide[a, which, PAD + size_y : PAD + size_y + 1, :] = high

    @pl.when(jnp.logical_not(electric()))
    def _():
        halo, edge, sign = sides(size_x)[which]
        for a in range(3):
            wide[a, which, PAD : PAD + size_y, :] = got[ROW_NOW + a * size_y : ROW_NOW + (a + 1) * size_y, :]
            row = ROW_SIDE + 2 * a
            put_side(a, which, got[row : row + 1, :], got[row + 1 : row + 2, :])
        stiff = got[ROW_STIFF : ROW_STIFF + size_y, :]
        stiff_own = own[6, edge]
        now = [rows_of(pad, a, edge + 1, size_y) for a in range(3)]
        theirs = [rows_of(wide, a, which, size_y) for a in range(3)]
        ties = tie_rows(list_ref[which].astype(F32), stiff, theirs)
        rate = motion_from(wide, which, sign, size_y)
        beta = OMEGA * inverse(stiff_own)
        for a in range(3):
            put(
                a,
                edge + 1,
                1 + which,
                rows_of(next_pad, a, edge + 1, size_y) + OMEGA * rate[a] + beta * ties[a] - 0.12 * now[a],
            )
        ties = tie_rows(got[ROW_LIST : ROW_LIST + 1, 0:size_y], stiff_own, now)
        rate = motion_from(pad, edge + 1, -sign, size_y)
        beta = OMEGA * inverse(stiff)
        for a in range(3):
            put(
                a,
                halo,
                3 * which,
                got[ROW_NEXT + a * size_y : ROW_NEXT + (a + 1) * size_y, :] + OMEGA * rate[a] + beta * ties[a],
            )


def electric_end(x, next_pad, fib_ref):
    size_y = next_pad.shape[2] - 2 * PAD
    place = place_of(x, size_y)
    return rows_of(next_pad, 0, x + 1, size_y) + DT * volt_rate(
        next_pad, x + 1, [fib_ref[a, place, :] for a in range(3)], size_y
    )


def electric_rest(x, next_pad, keep, out):
    size_y = next_pad.shape[2] - 2 * PAD
    v = rows_of(next_pad, 0, x + 1, size_y)
    n, gate, leak, rest_c = [keep[k, x] for k in range(4)]
    flow = gate * (v - 2.0)
    out[0, x] = -DT * (flow + leak * (v + 1.0) + 0.1 * v)
    out[1, x] = rest_c - (0.3 * DT) * flow
    out[2, x] = (1.0 - DT) * n + (0.5 * DT) * (1.0 + jnp.tanh(v))


def mechanic_end(x, next_pad, keep, size_y):
    rate = motion_rate(next_pad, x + 1, size_y)
    return [
        0.4 * rows_of(next_pad, a, x + 1, size_y) + keep[a, x] + OMEGA * rate[a] for a in range(3)
    ]


def middle_kernel(
    fib_ref, own, list_ref, got_low, got_high, next_in, side_ref, keep, out_in,
    out_hbm, next_pad, held, final, out, sems
):
    size_x = keep.shape[1]
    size_y = fib_ref.shape[1] // size_x
    lead = size_x - 4 - final.shape[1]

    def copy_out(fields):
        here = pl.ds(2, lead)
        return pltpu.make_async_copy(out.at[0:fields, here], out_hbm.at[0, 0:fields, here], sems.at[0])

    def fill(count):
        def one(x, carry):
            for a in range(count):
                fill_sides(next_pad, a, x, side_ref, x, size_y)
            return carry

        lax.fori_loop(2, size_x, one, 0, unroll=2)

    @pl.when(electric())
    def _():
        fill(1)

        def rest(x, carry):
            electric_rest(x, next_pad, keep, out)
            return carry

        lax.fori_loop(0, size_x, rest, 0, unroll=2)
        copy = pltpu.make_async_copy(out.at[1:3], out_hbm.at[0, 1:3], sems.at[1])
        copy.start()
        for i, x in enumerate((0, 1, size_x - 2, size_x - 1)):
            held[i] = out[0, x]

        for x in range(2, 2 + lead):
            out[0, x] = out[0, x] + electric_end(x, next_pad, fib_ref)
        copy_out(1).start()
        for x in range(2 + lead, size_x - 2):
            final[0, x - 2 - lead] = out[0, x] + electric_end(x, next_pad, fib_ref)
        copy.wait()
        copy_out(1).wait()

    @pl.when(jnp.logical_not(electric()))
    def _():
        fill(3)
        for x in range(2, 2 + lead):
            for a, value in enumerate(mechanic_end(x, next_pad, keep, size_y)):
                out[a, x] = value
        copy_out(3).start()
        for which, ((halo, edge, _), got) in enumerate(zip(sides(size_x), (got_low, got_high))):
            beta = OMEGA * inverse(own[6, edge])
            ties = tie_rows(
                list_ref[which].astype(F32),
                got[ROW_STIFF : ROW_STIFF + size_y, :],
                [rows_of(next_pad, a, halo, size_y) for a in range(3)],
            )
            for a in range(3):
                held[3 * which + a] = beta * ties[a] - 0.12 * rows_of(next_pad, a, edge + 1, size_y)
        for x in range(2 + lead, size_x - 2):
            for a, value in enumerate(mechanic_end(x, next_pad, keep, size_y)):
                final[a, x - 2 - lead] = value
        copy_out(3).wait()


def last_kernel(
    fib_ref, next_in, side_ref, keep, held, final, out_in, out_hbm, next_pad, out, sems
):
    size_x = keep.shape[1]
    size_y = fib_ref.shape[1] // size_x

    def copy_out(which, first, fields):
        here = pl.ds(first, 2)
        return pltpu.make_async_copy(out.at[0:fields, here], out_hbm.at[0, 0:fields, here], sems.at[which])

    def copy_final(fields):
        here = pl.ds(size_x - 2 - final.shape[1], final.shape[1])
        return pltpu.make_async_copy(final.at[0:fields], out_hbm.at[0, 0:fields, here], sems.at[2])

    work = []
    for which, (halo, edge, _) in enumerate(sides(size_x)):
        near = abs(edge - 1)
        work.append((halo, edge, near, which, min(edge, near)))

    @pl.when(electric())
    def _():
        copy_final(1).start()
        for halo, edge, near, which, first in work:
            fill_sides(next_pad, 0, halo, side_ref, 3 * which, size_y)
            fill_sides(next_pad, 0, edge + 1, side_ref, 1 + which, size_y)
            for x in (near, edge):
                out[0, x] = held[2 * which + x - first] + electric_end(x, next_pad, fib_ref)
            copy_out(which, first, 1).start()
        for item in work:
            copy_out(item[3], item[-1], 1).wait()
        copy_final(1).wait()

    @pl.when(jnp.logical_not(electric()))
    def _():
        copy_final(3).start()
        for halo, edge, near, which, first in work:
            for a in range(3):
                fill_sides(next_pad, a, halo, side_ref, 3 * which, size_y)
                fill_sides(next_pad, a, edge + 1, side_ref, 1 + which, size_y)
            for a, value in enumerate(mechanic_end(near, next_pad, keep, size_y)):
                out[a, near] = value
            for a, value in enumerate(mechanic_end(edge, next_pad, keep, size_y)):
                out[a, edge] = value + held[3 * which + a]
            copy_out(which, first, 3).start()
        for item in work:
            copy_out(item[3], item[-1], 3).wait()
        copy_final(3).wait()


def call(kernel, name, out_shape, operands, spaces, scratch=(), out_spaces=None, aliases=()):
    if out_spaces is None:
        out_spaces = [pltpu.VMEM] * len(out_shape)
    return pl.pallas_call(
        kernel,
        name=name,
        out_shape=tuple(out_shape),
        in_specs=[pl.BlockSpec(memory_space=space) for space in spaces],
        out_specs=tuple(pl.BlockSpec(memory_space=space) for space in out_spaces),
        scratch_shapes=scratch,
        input_output_aliases=dict(aliases),
        cost_estimate=pl.CostEstimate(
            flops=int(COST[name] * 10**10), bytes_accessed=int(COST[name] * 10**7), transcendentals=0
        ),
        compiler_params=pltpu.CompilerParams(vmem_limit_bytes=VMEM_LIMIT),
    )(*operands)


def local(sections, fiber_angles, fiber_class, row_map, interface_rows):
    own = sections[0]
    channels, size_x, size_y, depth = own.shape
    n_gx = lax.axis_size("gx")
    n_gy = lax.axis_size("gy")
    assert lax.axis_size("sec") == 2 and n_gy == 2
    axes = ("sec", "gx", "gy")
    place = lambda sec, i, j: (sec * n_gx + i % n_gx) * n_gy + j
    blocks = [(i, j) for i in range(n_gx) for j in range(n_gy)]

    def ring(section, step):
        return [(place(section, i, j), place(section, i + step, j)) for i, j in blocks] + [
            (place(1 - section, i, j), place(1 - section, i, 1 - j)) for i, j in blocks
        ]

    both = [(0, 1), (1, 0)]
    S, V, H = pltpu.SMEM, pltpu.VMEM, pltpu.HBM
    f32 = lambda *shape: jax.ShapeDtypeStruct(shape, F32)
    hbm = lambda w: pltpu.with_memory_space_constraint(w, H)
    columns = size_x * size_y
    ends = lambda planes: f32(6 * planes, depth)
    padded = f32(3, size_x + 2, size_y + 2 * PAD, depth)
    classes = fiber_class.transpose(0, 2, 1)
    lists = interface_rows.reshape(2, 1, size_y)
    places = row_map.reshape(-1)

    field = lambda n: pltpu.VMEM((n, size_x, size_y, depth), F32)
    flat = lambda count: pltpu.VMEM((classes.shape[1], count), jnp.int32)
    angles = fiber_angles.T
    plain, edge_ten, own_list, table = call(
        tension_kernel,
        "tension",
        (
            f32(columns, depth),
            f32(2, size_y, depth),
            jax.ShapeDtypeStruct((1, columns), jnp.int32),
            f32(3 * fiber_angles.shape[0] * classes.shape[1], 3 * depth),
        ),
        (hbm(own), hbm(places), hbm(row_map.reshape(1, columns)), hbm(angles)),
        (H,) * 4,
        [
            field(3),
            field(1),
            field(2),
            pltpu.VMEM(angles.shape, F32),
            pltpu.SMEM((columns,), jnp.int32),
            pltpu.SemaphoreType.DMA((3 + 3 * 4,)),
        ],
    )
    edge_ten = lax.ppermute(edge_ten, "sec", both)
    pad, share = call(share_kernel, "share", (padded, ends(size_x)), (own, plain), (V, V))
    side = lax.ppermute(share, "gy", both)
    result = f32(1, 4, size_x, size_y, depth)
    (gathered,) = call(gather_kernel, "gather", (f32(columns, depth),), (plain, own_list, share), (V,) * 3)
    edge_fib, table = call(
        edge_kernel,
        "edge",
        (f32(2 * size_y, 3 * depth), f32(*table.shape)),
        (table, classes, angles, gathered, lists),
        (V,) * 5,
        [flat(2 * size_y)],
        aliases={0: 1},
    )
    tension = lax.ppermute(gathered, "sec", both)
    assert depth == CELLS * classes.shape[1]
    message = f32(VOLT_ROWS, depth)
    high, low, pad = call(
        message_electric,
        "message_electric",
        (message, message, padded),
        (pad, own, side, edge_fib),
        (V,) * 4,
        aliases={0: 2},
    )
    volt_low = lax.ppermute(high, axes, ring(0, 1))
    volt_high = lax.ppermute(low, axes, ring(0, -1))
    message = f32(MESSAGE_ROWS, depth)
    high, low, pad = call(
        message_mechanic,
        "message_mechanic",
        (message, message, padded),
        (pad, own, side, edge_fib, edge_ten, lists),
        (V,) * 6,
        aliases={0: 2},
    )
    got_low = lax.ppermute(high, axes, ring(1, 1))
    got_high = lax.ppermute(low, axes, ring(1, -1))
    moved, share, keep, result, fib = call(
        inner_electric,
        "inner_electric",
        (padded, ends(size_x + 2), f32(4, size_x, size_y, depth), result, f32(3, columns, depth)),
        (pad, own, plain, classes, table),
        (V,) * 5,
        [flat(columns), pltpu.SemaphoreType.DMA((size_x,))],
        out_spaces=(V, V, V, H, V),
    )
    moved, share, keep, result = call(
        inner_mechanic,
        "inner_mechanic",
        (padded, ends(size_x + 2), f32(4, size_x, size_y, depth), f32(1, 4, size_x, size_y, depth)),
        (pad, own, fib, tension, moved, share, keep, result),
        (V,) * 7 + (H,),
        [pltpu.SemaphoreType.DMA((1,))],
        out_spaces=(V, V, V, H),
        aliases={4: 0, 5: 1, 6: 2, 7: 3},
    )
    side = lax.ppermute(share, "gy", both)
    wide = pltpu.VMEM((3, 2) + padded.shape[2:], F32)
    moved, share = call(
        outer_electric,
        "outer_electric",
        (padded, ends(4)),
        (pad, own, fib, volt_low, volt_high, moved),
        (V,) * 6,
        [wide],
        aliases={5: 0},
    )
    for which, got in enumerate((got_low, got_high)):
        moved, share = call(
            functools.partial(outer_mechanic, which),
            ("outer_low", "outer_high")[which],
            (padded, ends(4)),
            (pad, own, lists, got, moved, share),
            (V,) * 6,
            [wide],
            aliases={4: 0, 5: 1},
        )
    end_side = lax.ppermute(share, "gy", both)
    fields = pltpu.VMEM((3, size_x, size_y, depth), F32)
    held_back = 11
    result, moved, held, final = call(
        middle_kernel,
        "middle",
        (f32(1, 4, size_x, size_y, depth), padded, f32(6, size_y, depth), f32(3, held_back, size_y, depth)),
        (fib, own, lists, got_low, got_high, moved, side, keep, result),
        (V,) * 8 + (H,),
        [fields, pltpu.SemaphoreType.DMA((2,))],
        out_spaces=(H, V, V, V),
        aliases={5: 1, 8: 0},
    )
    return call(
        last_kernel,
        "last",
        (f32(1, 4, size_x, size_y, depth), padded),
        (fib, moved, end_side, keep, held, final, result),
        (V,) * 6 + (H,),
        [fields, pltpu.SemaphoreType.DMA((3,))],
        out_spaces=(H, V),
        aliases={1: 1, 6: 0},
    )[0]


def solution(mesh):
    in_specs = (
        P("sec", None, "gx", "gy", None),
        P(),
        P("gx", "gy", None),
        P("gx", "gy", None),
        P(None, "gx", "gy", None),
    )
    out_specs = P("sec", None, "gx", "gy", None)
    return jax.shard_map(local, mesh=mesh, in_specs=in_specs, out_specs=out_specs, check_vma=False)
```
